256 devices in a mesh: owner: 64 (over x, z_hi, y, core), qgrp: 4 (over z_lo).
Axes of the slice: x: 4, y: 4, z: 8 (z_hi: 2, z_lo: 4; z = z_hi * 4 + z_lo), core: 2. Of those that a mesh axis runs over, the one named last changes fastest.
Arguments:
- queries: float32 [3, 65536], P(None, ('owner', 'qgrp')), may hold values from -1.03 to 1.03, as said below
- winding_in: float32 [65536], P(('owner', 'qgrp')), may hold values from -2 to 2
- triangles: float32 [9, 1048576], P(None, ('owner', 'qgrp')), may hold values from -1.1 to 1.1, as said below
- dipoles: float32 [6, 8192], P(None, ('owner', 'qgrp')), may hold values from -1.2 to 1.2
- plan: int32 [4], replicated, may hold values from 0 to 63, as said below
- near_blocks: int32 [512, 16, 4], P(('owner', 'qgrp')), may hold values from 0 to 31, as said below
- near_count: int32 [512, 16], P(('owner', 'qgrp')), may hold values from 0 to 4, as said below
Outputs:
- winding_out: float32 [65536], P(('owner', 'qgrp'))
The draws below stay inside these ranges and needn't reach their ends.
Inputs may be any that keep to these rules, and one draw needn't show every extreme that they name: `queries`: every point lies 0.004 or more away from the plane z = 0 in z. `triangles`: every corner lies within 0.001 of the plane z = 0 in z. `plan`: distinct owner indices. `near_blocks`: the entries of one list are distinct block numbers. Only the leading near_count entries of a list are live; the first tile has all 4 live for some window panel.
All inputs are finite; a program needn't handle non-finite values.
Results may differ from the reference program's by a relative error of at most 0.0003.
Values sent between devices are 32-bit elements; how exact they have to be, the bound alone decides.
A program may use at most 64 MiB of HBM per device.

```python
import math
import jax
import jax.numpy as jnp
from jax import lax

TILE = 128
BLK = 128
BLOCKS = 32
NEAR = 4
TURNS = 4
PAN_TURN = 4
PANELS_WIN = 16
QUERIES = 65536
TILES = 512
TRI_ALL = 1048576
DIP_ALL = 8192
N_OWNER = 64


two_pi = 2.0 * math.pi


col_width = 2.0 / 12.0


def window_layout(key):
    layout_key = jax.random.fold_in(key, 101)
    subkeys = jax.random.split(layout_key, 7)
    panels_all = N_OWNER * PAN_TURN
    anchor_col = jax.random.randint(subkeys[0], (panels_all,), 0, 9).astype(jnp.int32)
    anchor_row = jax.random.randint(subkeys[1], (panels_all,), 0, BLOCKS // 2 + 1).astype(jnp.int32)
    others = jax.random.permutation(subkeys[2], N_OWNER - 1)[:TURNS - 1].astype(jnp.int32)
    listed = jnp.concatenate([others, jnp.full((1,), N_OWNER - 1, jnp.int32)])
    placing = jax.random.permutation(subkeys[6], TURNS).astype(jnp.int32)
    plan = listed[placing].astype(jnp.int32)
    window = jnp.arange(PANELS_WIN, dtype=jnp.int32)
    window_panel = plan[window // PAN_TURN] * PAN_TURN + window % PAN_TURN
    home_panel = jax.random.randint(subkeys[3], (TILES,), 0, PANELS_WIN).astype(jnp.int32)
    home_block = jax.random.randint(subkeys[4], (TILES,), 0, BLOCKS).astype(jnp.int32)
    tile_number = jnp.arange(TILES, dtype=jnp.int32)
    drawn_level = jax.random.randint(subkeys[5], (TILES,), 0, 4).astype(jnp.int32)
    tile_level = jnp.where(tile_number == 0, 0, drawn_level).astype(jnp.int32)
    home_global = window_panel[home_panel]
    tile_col = anchor_col[home_global] + home_block % 4
    tile_row = anchor_row[home_global] + home_block // 4
    return (anchor_col, anchor_row, plan, window_panel, tile_col, tile_row, tile_level)


def block_cells(anchor_col, anchor_row):
    block_index = jnp.arange(BLOCKS, dtype=jnp.int32)
    cell_col = anchor_col[:, None] + block_index[None, :] % 4
    cell_row = anchor_row[:, None] + block_index[None, :] // 4
    return (cell_col, cell_row)


def draw_queries(key, part):
    layout = window_layout(key)
    key = jax.random.fold_in(key, 12)
    subkeys = jax.random.split(key, 3)
    row_height = 8.0 / (3.0 * BLOCKS)
    tile_of = jnp.arange(QUERIES, dtype=jnp.int32) // TILE
    col_here = layout[4][tile_of].astype(jnp.float32)
    row_here = layout[5][tile_of].astype(jnp.float32)
    level_here = layout[6][tile_of].astype(jnp.float32)
    spread = jax.random.uniform(subkeys[0], (2, QUERIES), jnp.float32, -0.5, 0.5)
    point_x = -1.0 + col_width * (col_here + 0.5 + spread[0])
    point_y = -1.0 + row_height * (row_here + 0.5 + spread[1])
    lift = jax.random.uniform(subkeys[1], (QUERIES,), jnp.float32, 0.0, 1.0)
    side_sign = (jax.random.randint(subkeys[2], (QUERIES,), 0, 2) * 2 - 1).astype(jnp.float32)
    height = side_sign * 0.004 * jnp.exp2(2.0 * level_here) * (1.0 + 3.0 * lift)
    return jnp.stack([point_x, point_y, height], axis=0)


def draw_triangles(key, part):
    layout = window_layout(key)
    key = jax.random.fold_in(key, 11)
    subkeys = jax.random.split(key, 5)
    panels_all = N_OWNER * PAN_TURN
    row_height = 8.0 / (3.0 * BLOCKS)
    radius = math.sqrt(1.5 * col_width * row_height / (1.299 * BLK))
    cell_col, cell_row = block_cells(layout[0], layout[1])
    centre_col = jnp.broadcast_to(cell_col[:, :, None], (panels_all, BLOCKS, BLK)).reshape(-1).astype(jnp.float32)
    centre_row = jnp.broadcast_to(cell_row[:, :, None], (panels_all, BLOCKS, BLK)).reshape(-1).astype(jnp.float32)
    spread = jax.random.uniform(subkeys[0], (2, TRI_ALL), jnp.float32, -0.5, 0.5)
    centre_x = -1.0 + col_width * (centre_col + 0.5 + spread[0])
    centre_y = -1.0 + row_height * (centre_row + 0.5 + spread[1])
    turn_start = jax.random.uniform(subkeys[1], (TRI_ALL,), jnp.float32, 0.0, two_pi)
    jitter = jax.random.uniform(subkeys[2], (3, TRI_ALL), jnp.float32, -0.4, 0.4)
    stretch = jax.random.uniform(subkeys[3], (3, TRI_ALL), jnp.float32, 0.0, 1.0)
    lengths = radius * (0.6 + 0.7 * stretch)
    heights = jax.random.uniform(subkeys[4], (3, TRI_ALL), jnp.float32, -0.001, 0.001)
    corner_rows = []
    for corner in range(3):
        angle = turn_start + two_pi * corner / 3.0 + jitter[corner]
        corner_rows.append(centre_x + lengths[corner] * jnp.cos(angle))
        corner_rows.append(centre_y + lengths[corner] * jnp.sin(angle))
        corner_rows.append(heights[corner])
    return jnp.stack(corner_rows, axis=0)


def draw_dipoles(key, part):
    layout = window_layout(key)
    key = jax.random.fold_in(key, 13)
    subkeys = jax.random.split(key, 3)
    row_height = 8.0 / (3.0 * BLOCKS)
    cell_col, cell_row = block_cells(layout[0], layout[1])
    spread = jax.random.uniform(subkeys[0], (2, DIP_ALL), jnp.float32, -0.25, 0.25)
    centre_x = -1.0 + col_width * (cell_col.reshape(-1).astype(jnp.float32) + 0.5 + spread[0])
    centre_y = -1.0 + row_height * (cell_row.reshape(-1).astype(jnp.float32) + 0.5 + spread[1])
    centre_z = jax.random.uniform(subkeys[1], (DIP_ALL,), jnp.float32, -0.001, 0.001)
    normals = 0.3 * jnp.clip(jax.random.normal(subkeys[2], (3, DIP_ALL), jnp.float32), -4.0, 4.0)
    centres = jnp.stack([centre_x, centre_y, centre_z], axis=0)
    return jnp.concatenate([centres, normals], axis=0)


def draw_plan(key, part):
    layout = window_layout(key)
    return layout[2]


def tile_offsets(layout):
    window_panel = layout[3]
    shift_col = layout[4][:, None] - layout[0][window_panel][None, :]
    shift_row = layout[5][:, None] - layout[1][window_panel][None, :]
    return (shift_col, shift_row)


def draw_near_blocks(key, part):
    layout = window_layout(key)
    shift_col, shift_row = tile_offsets(layout)
    nearest = jnp.clip(shift_row, 0, BLOCKS // 4 - 1) * 4 + jnp.clip(shift_col, 0, 3)
    return jnp.stack([nearest, nearest ^ 1, nearest ^ 4, nearest ^ 5], axis=-1).astype(jnp.int32)


def draw_near_count(key, part):
    layout = window_layout(key)
    shift_col, shift_row = tile_offsets(layout)
    inside = (shift_col >= 0) & (shift_col < 4) & (shift_row >= 0) & (shift_row < BLOCKS // 4)
    return jnp.where(inside, NEAR - layout[6][:, None], 0).astype(jnp.int32)


def levels(stream_key, shape, cuts, smallest, top_value):
    level = 1.0
    for dim, shards_of in cuts:
        draws = jax.random.uniform(jax.random.fold_in(jax.random.fold_in(stream_key, 6), dim), (shards_of,), jnp.float32, smallest / len(cuts), top_value / len(cuts))
        level = level * jnp.repeat(jnp.exp(draws), shape[dim] // shards_of).reshape((-1,) + (1,) * (len(shape) - 1 - dim))
    return level


def noise(key, extent, width, most, pieces=(), kind=jnp.bfloat16):
    drawn = jax.random.normal(key, extent, jnp.float32) * width
    if len(pieces) > 0:
        drawn = levels(key, extent, pieces, -0.22, 0.18) * drawn
    return jnp.clip(drawn, min=-most, max=most).astype(kind)


def setup_inputs(seed: int = 0) -> dict:
    arg_keys = jax.random.split(jax.random.key(seed), 8)
    queries = draw_queries(jax.random.fold_in(arg_keys[7], 71), 0)
    winding_in = noise(arg_keys[1], (QUERIES,), 0.3, 2.0, ((0, 256),), jnp.float32)
    triangles = draw_triangles(jax.random.fold_in(arg_keys[7], 71), 0)
    dipoles = draw_dipoles(jax.random.fold_in(arg_keys[7], 71), 0)
    plan = draw_plan(jax.random.fold_in(arg_keys[7], 71), 0)
    near_blocks = draw_near_blocks(jax.random.fold_in(arg_keys[7], 71), 0)
    near_count = draw_near_count(jax.random.fold_in(arg_keys[7], 71), 0)
    return dict(queries=queries, winding_in=winding_in, triangles=triangles, dipoles=dipoles, plan=plan, near_blocks=near_blocks, near_count=near_count)


four_pi = 4.0 * 3.141592653589793
soften = 0.1

def inner_product(left, right):
    return left[0] * right[0] + left[1] * right[1] + left[2] * right[2]

def cross_product(left, right):
    return (left[1] * right[2] - left[2] * right[1], left[2] * right[0] - left[0] * right[2], left[0] * right[1] - left[1] * right[0])

def solid_terms(points, corners):
    relative = [corners[component][None, :] - points[component % 3][:, None] for component in range(9)]
    to_first = relative[0:3]
    to_second = relative[3:6]
    to_third = relative[6:9]
    length_first = jnp.sqrt(inner_product(to_first, to_first))
    length_second = jnp.sqrt(inner_product(to_second, to_second))
    length_third = jnp.sqrt(inner_product(to_third, to_third))
    volume = inner_product(to_first, cross_product(to_second, to_third))
    denominator = length_first * length_second * length_third + inner_product(to_first, to_second) * length_third + inner_product(to_second, to_third) * length_first + inner_product(to_third, to_first) * length_second
    return 2.0 * jnp.arctan2(volume, denominator) / four_pi

def dipole_terms(points, clusters):
    offset = [clusters[component][None, :] - points[component][:, None] for component in range(3)]
    normal = [clusters[3 + component][None, :] for component in range(3)]
    radius_square = inner_product(offset, offset) + soften
    return inner_product(normal, offset) / (four_pi * radius_square * jnp.sqrt(radius_square))

def reference(queries, winding_in, triangles, dipoles, plan, near_blocks, near_count):
    owned_triangles = triangles.reshape(9, N_OWNER, PAN_TURN, BLOCKS, BLK)
    owned_dipoles = dipoles.reshape(6, N_OWNER, PAN_TURN, BLOCKS)
    chosen = owned_triangles[:, plan].reshape(9, PANELS_WIN, BLOCKS, BLK)
    chosen_dipoles = owned_dipoles[:, plan].reshape(6, PANELS_WIN, BLOCKS)
    flat_dipoles = chosen_dipoles.reshape(6, PANELS_WIN * BLOCKS)
    panel_rows = jnp.arange(PANELS_WIN, dtype=jnp.int32)[:, None]
    slot_order = jnp.arange(NEAR, dtype=jnp.int32)
    tiles = queries.reshape(3, TILES, TILE).transpose(1, 0, 2)

    def tile_winding(packed):
        tile_points, blocks, counts = packed
        far_field = lax.optimization_barrier(jnp.sum(dipole_terms(tile_points, flat_dipoles), axis=1))
        picked = chosen[:, panel_rows, blocks]
        picked_dipoles = chosen_dipoles[:, panel_rows, blocks]
        exact_terms = solid_terms(tile_points, picked.reshape(9, -1)).reshape(TILE, PANELS_WIN, NEAR, BLK).sum(axis=3)
        dipole_part = dipole_terms(tile_points, picked_dipoles.reshape(6, -1)).reshape(TILE, PANELS_WIN, NEAR)
        live_slots = slot_order[None, :] < counts[:, None]
        near_field = lax.optimization_barrier(jnp.sum(jnp.where(live_slots[None], exact_terms - dipole_part, 0.0), axis=(1, 2)))
        return far_field + near_field
    contribution = lax.map(tile_winding, (tiles, near_blocks, near_count))
    return winding_in + contribution.reshape(-1)
```

```python
import functools

import jax
import jax.numpy as jnp
from jax import lax
from jax.experimental import pallas as pl
from jax.experimental.pallas import tpu as pltpu
from jax.sharding import PartitionSpec as P

TILE = 128
BLK = 128
BLOCKS = 32
NEAR = 4
TURNS = 4
PAN_TURN = 4
PANELS = TURNS * PAN_TURN
OWNERS = 64
HALF = 5

MESH = pl.DeviceIdType.MESH

pi = 3.141592653589793
four_pi = 4.0 * pi
soften = 0.1

ATAN = (
    1.0,
    -0.3333309292793274,
    0.19993053376674652,
    -0.14207133650779724,
    0.10654675215482712,
    -0.07533672451972961,
    0.04303932562470436,
    -0.016282981261610985,
    0.0029035459738224745,
)


def gather_kernel(
    plan_ref, queries_ref, triangles_ref, dipoles_ref, lists_ref,
    panel_ref, points_ref, live_ref,
    stage, arrived, chosen, final, message, messages,
    send_one, recv_one, send_two, recv_two, send_msg, recv_msg,
):
    me = lax.axis_index("owner")
    lane = lax.axis_index("qgrp")
    group = me // TURNS
    turn = me % TURNS
    member = turn * PAN_TURN + lane

    barrier = pltpu.get_barrier_semaphore()

    def greet_owner(step, carry):
        other = (me + step) % OWNERS
        pl.semaphore_signal(barrier, inc=1, device_id=(other, lane), device_id_type=MESH)
        return carry

    def greet_member(step, carry):
        other = (lane + 1 + step // TURNS) % PAN_TURN
        pl.semaphore_signal(
            barrier, inc=1, device_id=(group * TURNS + step % TURNS, other), device_id_type=MESH
        )
        return carry

    lax.fori_loop(1, OWNERS, greet_owner, 0)
    lax.fori_loop(0, TURNS * (PAN_TURN - 1), greet_member, 0)

    for block in range(BLOCKS):
        cols = pl.ds(block * BLK, BLK)
        stage[2 * block] = triangles_ref[0:HALF, cols]
        stage[2 * block + 1, 0 : HALF - 1] = triangles_ref[HALF:9, cols]
        stage[2 * block + 1, HALF - 1 : HALF] = jnp.zeros((1, BLK), jnp.float32)
    for component in range(6):
        stage[2 * component + 1, HALF - 1 : HALF, 0:BLOCKS] = dipoles_ref[component : component + 1, :]
    message[0:3] = queries_ref[:, 0:TILE]
    message[3:6] = queries_ref[:, TILE : 2 * TILE]
    message[6:8] = lists_ref[...]

    pl.semaphore_wait(barrier, OWNERS - 1 + TURNS * (PAN_TURN - 1))

    def first_copy(other):
        return pltpu.make_async_remote_copy(
            src_ref=stage.at[other], dst_ref=arrived.at[me], send_sem=send_one, recv_sem=recv_one,
            device_id=(other, lane), device_id_type=MESH,
        )

    def send_first(step, carry):
        first_copy((me + step) % OWNERS).start()
        return carry

    lax.fori_loop(1, OWNERS, send_first, 0)

    def message_copy(to_turn, to_lane):
        return pltpu.make_async_remote_copy(
            src_ref=message, dst_ref=messages.at[member], send_sem=send_msg, recv_sem=recv_msg,
            device_id=(group * TURNS + to_turn, to_lane), device_id_type=MESH,
        )

    def send_message(step, carry):
        to = (member + step) % PANELS
        message_copy(to // PAN_TURN, to % PAN_TURN).start()
        return carry

    lax.fori_loop(1, PANELS, send_message, 0)
    messages[member] = message[...]
    arrived[me] = stage[me]

    def wait_bytes(ref, count, sem):
        part = ref.at[pl.ds(0, count)]
        pltpu.make_async_copy(part, part, sem).wait()

    wait_bytes(arrived, OWNERS - 1, recv_one)
    for window_turn in range(TURNS):
        chosen[window_turn] = arrived[plan_ref[window_turn]]

    def second_copy(other):
        return pltpu.make_async_remote_copy(
            src_ref=chosen.at[other % TURNS], dst_ref=final.at[me], send_sem=send_two, recv_sem=recv_two,
            device_id=(other, lane), device_id_type=MESH,
        )

    def send_second(step, carry):
        second_copy((me + step) % OWNERS).start()
        return carry

    lax.fori_loop(1, OWNERS, send_second, 0)
    final[me] = chosen[turn]

    wait_bytes(messages, PANELS - 1, recv_msg)
    points_ref[...] = messages[...]
    live_ref[...] = messages[:, 6:8, :].astype(jnp.int32)
    wait_bytes(final, OWNERS - 1, recv_two)
    for block in range(BLOCKS):
        panel_ref[block, 0:HALF] = final[2 * block]
        panel_ref[block, HALF : 2 * HALF] = final[2 * block + 1]
    wait_bytes(stage, OWNERS - 1, send_one)
    wait_bytes(messages, PANELS - 1, send_msg)
    wait_bytes(final, OWNERS - 1, send_two)


def near_kernel(live_ref, panel_ref, points_ref, out_ref, columns, spread, centres, real, imag, turns):
    column = (lax.axis_index("owner") % TURNS) * PAN_TURN + lax.axis_index("qgrp")

    rows = jnp.concatenate(
        [panel_ref[c, 2 * HALF - 1 : 2 * HALF, :] for c in range(6)]
        + [jnp.zeros((2, BLK), jnp.float32)], axis=0
    )
    flipped = rows.T
    for component in range(6):
        value = jnp.broadcast_to(flipped[0:BLOCKS, component : component + 1], (BLOCKS, TILE))
        if component >= 3:
            value = value * (1.0 / four_pi)
        centres[component] = value
    ones = jnp.ones((8, BLK), jnp.float32)
    block_order = lax.broadcasted_iota(jnp.int32, (BLOCKS, TILE), 0)

    def exact_block(block, first):
        corner = [
            jnp.broadcast_to(panel_ref[block, c : c + 1, :], (8, BLK)) for c in range(9)
        ]
        ax, ay, az, bx, by, bz, cx, cy, cz = corner
        ux, uy, uz = bx - ax, by - ay, bz - az
        vx, vy, vz = cx - ax, cy - ay, cz - az
        wx, wy, wz = cx - bx, cy - by, cz - bz
        ux2, uy2, uz2 = ux + ux, uy + uy, uz + uz
        nx = uy2 * vz - uz2 * vy
        ny = uz2 * vx - ux2 * vz
        nz = ux2 * vy - uy2 * vx
        side_ab = ux * ux + uy * uy + uz * uz
        side_bc = wx * wx + wy * wy + wz * wz
        side_ca = vx * vx + vy * vy + vz * vz
        for part in range(TILE // 8):
            at = pl.ds(part * 8, 8)
            qx, qy, qz = spread[0, at], spread[1, at], spread[2, at]

            def from_point(x, y, z):
                x, y, z = x - qx, y - qy, z - qz
                square = x * x + y * y + z * z
                return x, y, z, square * lax.rsqrt(square)

            px, py, pz, la = from_point(ax, ay, az)
            lb = from_point(bx, by, bz)[3]
            lc = from_point(cx, cy, cz)[3]
            y = px * nx + py * ny + pz * nz
            x = (la + lb) * (lb + lc) * (lc + la) - (side_ab * lc + side_bc * la + side_ca * lb)
            if first:
                real[at], imag[at] = x, y
                turns[at] = jnp.zeros((8, BLK), jnp.float32)
            else:
                u, v = real[at], imag[at]
                below = y < 0.0
                r, i = u * x - v * y, u * y + v * x
                same = jnp.logical_not(jnp.logical_xor(v < 0.0, below))
                wrapped = jnp.logical_and(same, jnp.logical_xor(i < 0.0, below))
                turns[at] += jnp.where(wrapped, jnp.where(below, -1.0, 1.0), 0.0)
                real[at], imag[at] = r, i

    def angle(x, y):
        ax, ay = jnp.abs(x), jnp.abs(y)
        t = jnp.minimum(ax, ay) / jnp.maximum(ax, ay)
        square = t * t
        value = jnp.full_like(t, ATAN[-1])
        for coefficient in ATAN[-2::-1]:
            value = value * square + coefficient
        value = value * t
        value = jnp.where(ay > ax, 0.5 * pi - value, value)
        value = jnp.where(x < 0.0, pi - value, value)
        return jnp.where(y < 0.0, -value, value)

    def one_member(member, carry):
        block_of_points = points_ref[member]
        columns[...] = block_of_points.T
        for half in range(2):
            count = live_ref[member, half, PANELS * NEAR + column]
            picks = [live_ref[member, half, column * NEAR + s] for s in range(NEAR)]

            offset = [
                centres[c] - jnp.broadcast_to(block_of_points[3 * half + c : 3 * half + c + 1, :], (BLOCKS, TILE))
                for c in range(3)
            ]
            square = offset[0] * offset[0] + offset[1] * offset[1] + offset[2] * offset[2] + soften
            inverse = lax.rsqrt(square)
            dipole = (centres[3] * offset[0] + centres[4] * offset[1] + centres[5] * offset[2]) * (
                inverse * inverse * inverse
            )
            for s in range(NEAR):
                pick = jnp.where(s < count, picks[s], -1)
                dipole = jnp.where(block_order == pick, 0.0, dipole)
            far = jnp.sum(dipole, axis=0, keepdims=True)
            out_ref[member, half : half + 1, :] = far

            @pl.when(count > 0)
            def _():
                for c in range(3):
                    spread[c] = jnp.broadcast_to(
                        columns[:, 3 * half + c : 3 * half + c + 1], (TILE, BLK)
                    )
                exact_block(picks[0], True)

                def more(slot, carry):
                    exact_block(live_ref[member, half, column * NEAR + slot], False)
                    return carry

                lax.fori_loop(1, count, more, 0)
                total = angle(real[...], imag[...]) * (0.5 / pi) + turns[...]
                summed = lax.dot_general(
                    ones, total, (((1,), (1,)), ((), ())),
                    precision=lax.Precision.HIGHEST, preferred_element_type=jnp.float32,
                )
                out_ref[member, half : half + 1, :] += summed[0:1]

        return carry

    lax.fori_loop(0, PANELS, one_member, 0)


def reduce_kernel(partial_ref, winding_ref, out_ref, arrived, send_sem, recv_sem):
    me = lax.axis_index("owner")
    lane = lax.axis_index("qgrp")
    group = me // TURNS
    member = (me % TURNS) * PAN_TURN + lane
    barrier = pltpu.get_barrier_semaphore()

    def device(step):
        to = (member + step) % PANELS
        return to, (group * TURNS + to // PAN_TURN, to % PAN_TURN)

    def greet(step, carry):
        pl.semaphore_signal(barrier, inc=1, device_id=device(step)[1], device_id_type=MESH)
        return carry

    lax.fori_loop(1, PANELS, greet, 0)
    pl.semaphore_wait(barrier, PANELS - 1)

    def send(step, carry):
        to, where = device(step)
        pltpu.make_async_remote_copy(
            src_ref=partial_ref.at[to], dst_ref=arrived.at[member], send_sem=send_sem, recv_sem=recv_sem,
            device_id=where, device_id_type=MESH,
        ).start()
        return carry

    lax.fori_loop(1, PANELS, send, 0)
    arrived[member] = partial_ref[member]
    part = arrived.at[pl.ds(0, PANELS - 1)]
    pltpu.make_async_copy(part, part, recv_sem).wait()
    out_ref[...] = winding_ref[...] + jnp.sum(arrived[...], axis=0)
    pltpu.make_async_copy(part, part, send_sem).wait()


def on_device(queries, winding_in, triangles, dipoles, plan, near_blocks, near_count):
    lists = jnp.concatenate(
        [near_blocks.reshape(2, PANELS * NEAR), near_count, jnp.zeros((2, 128 - PANELS * (NEAR + 1)), jnp.int32)],
        axis=1,
    ).astype(jnp.float32)
    vmem = pl.BlockSpec(memory_space=pltpu.VMEM)
    smem = pl.BlockSpec(memory_space=pltpu.SMEM)
    f32 = jnp.float32
    panel, points, live = pl.pallas_call(
        gather_kernel,
        out_shape=(
            jax.ShapeDtypeStruct((BLOCKS, 2 * HALF, BLK), f32),
            jax.ShapeDtypeStruct((PANELS, 8, TILE), f32),
            jax.ShapeDtypeStruct((PANELS, 2, 128), jnp.int32),
        ),
        in_specs=[smem, vmem, vmem, vmem, vmem],
        out_specs=(vmem, vmem, vmem),
        scratch_shapes=[
            pltpu.VMEM((OWNERS, HALF, BLK), f32),
            pltpu.VMEM((OWNERS, HALF, BLK), f32),
            pltpu.VMEM((TURNS, HALF, BLK), f32),
            pltpu.VMEM((OWNERS, HALF, BLK), f32),
            pltpu.VMEM((8, TILE), f32),
            pltpu.VMEM((PANELS, 8, TILE), f32),
        ]
        + [pltpu.SemaphoreType.DMA] * 6,
        compiler_params=pltpu.CompilerParams(collective_id=0, has_side_effects=True),
        name="gather",
    )(plan, queries, triangles, dipoles, lists)
    partial = pl.pallas_call(
        near_kernel,
        out_shape=jax.ShapeDtypeStruct((PANELS, 2, TILE), f32),
        in_specs=[smem, vmem, vmem],
        out_specs=vmem,
        scratch_shapes=[
            pltpu.VMEM((TILE, 8), f32),
            pltpu.VMEM((3, TILE, BLK), f32),
            pltpu.VMEM((6, BLOCKS, TILE), f32),
            pltpu.VMEM((TILE, BLK), f32),
            pltpu.VMEM((TILE, BLK), f32),
            pltpu.VMEM((TILE, BLK), f32),
        ],
        name="near",
    )(live, panel, points)
    total = pl.pallas_call(
        reduce_kernel,
        out_shape=jax.ShapeDtypeStruct((2, TILE), f32),
        in_specs=[vmem, vmem],
        out_specs=vmem,
        scratch_shapes=[pltpu.VMEM((PANELS, 2, TILE), f32)] + [pltpu.SemaphoreType.DMA] * 2,
        compiler_params=pltpu.CompilerParams(collective_id=1, has_side_effects=True),
        name="reduce",
    )(partial, winding_in.reshape(2, TILE))
    return total.reshape(-1)


def solution(mesh):
    return jax.shard_map(
        on_device,
        mesh=mesh,
        in_specs=(
            P(None, ("owner", "qgrp")),
            P(("owner", "qgrp")),
            P(None, ("owner", "qgrp")),
            P(None, ("owner", "qgrp")),
            P(),
            P(("owner", "qgrp"), None, None),
            P(("owner", "qgrp"), None),
        ),
        out_specs=P(("owner", "qgrp")),
        check_vma=False,
    )
```

```python
import functools

import jax
import jax.numpy as jnp
from jax import lax
from jax.experimental import pallas as pl
from jax.experimental.pallas import tpu as pltpu
from jax.sharding import PartitionSpec as P

TILE = 128
BLK = 128
BLOCKS = 32
NEAR = 4
TURNS = 4
PAN_TURN = 4
PANELS = TURNS * PAN_TURN
OWNERS = 64
ROWS = 10
PARTS = 8
MEMBERS_STEP = 2

MESH = pl.DeviceIdType.MESH

pi = 3.141592653589793
four_pi = 4.0 * pi
soften = 0.1

ATAN = (
    1.0,
    -0.3333309292793274,
    0.19993053376674652,
    -0.14207133650779724,
    0.10654675215482712,
    -0.07533672451972961,
    0.04303932562470436,
    -0.016282981261610985,
    0.0029035459738224745,
)


def block_of(place):
    kind, part = place % 4, place // 4
    return kind % 2 + (part % 2) * 2 + (kind // 2) * 4 + (part // 2) * 8


def owner_of(place, half):
    return (place // 8) * 16 + half * 8 + ((place // 4) % 2) * 4 + place % 4


def gather_kernel(
    plan_ref, queries_ref, triangles_ref, dipoles_ref, blocks_ref, count_ref,
    panel_ref, points_ref, live_ref,
    queries, triangles, dipoles, blocks, count,
    stage, arrived, chosen, final, message, messages,
    load_sems, send_one, recv_one, send_two, recv_two, recv_far, send_msg, recv_msg, known, go,
):
    me = lax.axis_index("owner")
    lane = lax.axis_index("qgrp")
    half = (me // 8) % 2
    place = ((me // 16) * 2 + (me // 4) % 2) * 4 + me % 4
    kind = me % 4
    part = place // 4
    member = kind * PAN_TURN + lane
    first = half == 0
    barrier = pltpu.get_barrier_semaphore()

    loads = [
        pltpu.make_async_copy(source, target, load_sems.at[index])
        for index, (source, target) in enumerate(
            [
                (triangles_ref, triangles), (dipoles_ref, dipoles), (queries_ref, queries),
                (blocks_ref, blocks), (count_ref, count),
            ]
        )
    ]
    for load in loads:
        load.start()

    @pl.when(first)
    def _():
        def greet(step, carry):
            pl.semaphore_signal(
                barrier, inc=1, device_id=((me + step) % OWNERS, lane), device_id_type=MESH
            )
            return carry

        lax.fori_loop(1, OWNERS, greet, 0)

        def greet_member(step, carry):
            pl.semaphore_signal(
                barrier, inc=1,
                device_id=((me // 4) * 4 + step % 4, (lane + 1 + step // 4) % PAN_TURN), device_id_type=MESH,
            )
            return carry

        lax.fori_loop(0, 4 * (PAN_TURN - 1), greet_member, 0)

    loads[0].wait()
    loads[1].wait()
    flipped = jnp.concatenate(
        [jnp.concatenate([dipoles[...], jnp.zeros((2, BLOCKS), jnp.float32)], axis=0),
         jnp.zeros((8, BLK - BLOCKS), jnp.float32)], axis=1
    ).T
    for slot in range(BLOCKS):
        block = block_of(slot)
        stage[slot, 0:9] = triangles[:, block * BLK : (block + 1) * BLK]
        stage[slot, 9:10, 0:8] = flipped[block : block + 1, :]

    def first_copy(to):
        return pltpu.make_async_remote_copy(
            src_ref=stage.at[to], dst_ref=arrived.at[me], send_sem=send_one, recv_sem=recv_one,
            device_id=(owner_of(to, 0), lane), device_id_type=MESH,
        )

    def send_first(step, carry):
        first_copy((place + step) % BLOCKS).start()
        return carry

    def make_message():
        for load in loads[2:]:
            load.wait()
        message[0:3] = queries[:, 0:TILE]
        message[3:6] = queries[:, TILE : 2 * TILE]
        shape = (PANELS, BLK)
        panel = lax.broadcasted_iota(jnp.int32, shape, 0)
        column = lax.broadcasted_iota(jnp.int32, shape, 1)
        for tile in range(2):
            wide = jnp.concatenate(
                [count[tile : tile + 1, :], jnp.zeros((1, BLK - PANELS), jnp.int32)], axis=1
            ).astype(jnp.float32)
            live = jnp.sum(
                jnp.where(panel == column, jnp.broadcast_to(wide, shape), 0.0), axis=1, keepdims=True
            )
            listed = jnp.full(shape, -1.0, jnp.float32)
            for slot in range(NEAR):
                entry = blocks[tile][:, slot : slot + 1].astype(jnp.float32)
                entry = jnp.where(live > slot, entry, -1.0)
                listed = jnp.where(column % NEAR == slot, jnp.broadcast_to(entry, shape), listed)
            listed = jnp.where(column // NEAR == panel, listed + 1.0, 0.0)
            message[6 + tile : 7 + tile] = jnp.sum(listed, axis=0, keepdims=True) - 1.0

    def send_message(step, carry):
        to = (member + step) % PANELS
        pltpu.make_async_remote_copy(
            src_ref=message, dst_ref=messages.at[member], send_sem=send_msg, recv_sem=recv_msg,
            device_id=((me // 4) * 4 + to // PAN_TURN, to % PAN_TURN), device_id_type=MESH,
        ).start()
        return carry

    def send_second(step, carry):
        to = ((part + step) % PARTS) * 4 + kind
        pltpu.make_async_remote_copy(
            src_ref=chosen, dst_ref=final.at[part], send_sem=send_two, recv_sem=recv_two,
            device_id=(owner_of(to, half), lane), device_id_type=MESH,
        ).start()
        return carry

    def wait_bytes(part, sem):
        pltpu.make_async_copy(part, part, sem).wait()

    @pl.when(first)
    def _():
        pl.semaphore_wait(barrier, BLOCKS - 1 + 4 * (PAN_TURN - 1))
        lax.fori_loop(1, BLOCKS, send_first, 0)
        make_message()
        lax.fori_loop(1, PANELS, send_message, 0)
        arrived[me] = stage[place]
        wait_bytes(arrived.at[pl.ds(0, OWNERS - 1)], recv_one)
        for turn in range(TURNS):
            chosen[turn] = arrived[plan_ref[turn]]
        lax.fori_loop(1, PARTS, send_second, 0)
        pltpu.make_async_remote_copy(
            src_ref=chosen, dst_ref=chosen, send_sem=send_two, recv_sem=recv_far,
            device_id=(me + 8, lane), device_id_type=MESH,
        ).start()
        for step in range(1, PAN_TURN):
            pl.semaphore_signal(
                known, inc=1, device_id=(me, (lane + step) % PAN_TURN), device_id_type=MESH
            )
        pl.semaphore_wait(known, PAN_TURN - 1)
        pl.semaphore_signal(go, inc=1, device_id=(me + 8, lane), device_id_type=MESH)

    @pl.when(jnp.logical_not(first))
    def _():
        pl.semaphore_wait(barrier, BLOCKS)
        lax.fori_loop(0, BLOCKS, send_first, 0)
        make_message()
        wait_bytes(chosen, recv_far)
        lax.fori_loop(1, PARTS, send_second, 0)
        pl.semaphore_wait(go, 1)
        lax.fori_loop(1, PANELS, send_message, 0)

    final[part] = chosen[...]
    messages[member] = message[...]
    wait_bytes(messages.at[pl.ds(0, PANELS - 1)], recv_msg)
    points_ref[...] = messages[...]

    shape = (PANELS, BLK)
    column = lax.broadcasted_iota(jnp.int32, shape, 1)
    before = (
        lax.broadcasted_iota(jnp.int32, (BLK, BLK), 0) < lax.broadcasted_iota(jnp.int32, (BLK, BLK), 1)
    ).astype(jnp.float32)
    for tile in range(2):
        listed = messages[:, 6 + tile, :].astype(jnp.int32)
        held = (listed % 2) + ((listed // 4) % 2) * 2 == kind
        held = jnp.logical_and(held, (column // NEAR) % PAN_TURN == lane)
        held = jnp.logical_and(held, jnp.logical_and(listed >= 0, column < PANELS * NEAR))
        value = ((listed // 2) % 2 + (listed // 8) * 2) * 4 + column // PANELS
        value = value.astype(jnp.float32)
        flags = jnp.where(held, 1.0, 0.0)
        rank = lax.dot_general(flags, before, (((1,), (0,)), ((), ())), preferred_element_type=jnp.float32)
        rank = jnp.where(held, rank, -1.0)
        packed = jnp.where(column == PANELS, jnp.sum(flags, axis=1, keepdims=True), 0.0)
        for index in range(PANELS):
            one = jnp.sum(jnp.where(jnp.abs(rank - index) < 0.5, value, 0.0), axis=1, keepdims=True)
            packed = jnp.where(column == index, one, packed)
        live_ref[:, tile, :] = packed.astype(jnp.int32)

    wait_bytes(final.at[pl.ds(0, PARTS - 1)], recv_two)
    for slot in range(BLOCKS):
        panel_ref[slot] = final[slot // 4, slot % 4]

    @pl.when(first)
    def _():
        wait_bytes(stage.at[pl.ds(0, BLOCKS - 1)], send_one)
        wait_bytes(final, send_two)

    @pl.when(jnp.logical_not(first))
    def _():
        wait_bytes(stage, send_one)
        wait_bytes(final.at[pl.ds(0, PARTS - 1)], send_two)

    wait_bytes(messages.at[pl.ds(0, PANELS - 1)], send_msg)


def near_kernel(
    live_ref, panel_ref, points_ref, out_ref, spread, centres, flipped, real, imag, turns, tiles
):
    rows = jnp.concatenate([panel_ref[slot, 9:10, :] for slot in range(BLOCKS)], axis=0)
    for component in range(6):
        value = jnp.broadcast_to(rows[:, component : component + 1], (BLOCKS, TILE))
        if component >= 3:
            value = value * (1.0 / four_pi)
        centres[component] = value

    def dipole(centre, points):
        offset = [centre[c] - jnp.broadcast_to(points[c : c + 1, :], centre[c].shape) for c in range(3)]
        square = offset[0] * offset[0] + offset[1] * offset[1] + offset[2] * offset[2] + soften
        inverse = lax.rsqrt(square)
        return (centre[3] * offset[0] + centre[4] * offset[1] + centre[5] * offset[2]) * (
            inverse * inverse * inverse
        )

    def far_field(step, carry):
        for index in range(MEMBERS_STEP):
            member = step * MEMBERS_STEP + index
            points = points_ref[member]
            flipped[member] = points.T
            for half in range(2):
                field = dipole([centres[c] for c in range(6)], points[3 * half : 3 * half + 3])
                out_ref[member, half : half + 1, :] = jnp.sum(field, axis=0, keepdims=True)
        return carry

    lax.fori_loop(0, PANELS // MEMBERS_STEP, far_field, 0)

    def exact_block(block, tile, member, half, starts):
        corner = [
            jnp.broadcast_to(panel_ref[block, c : c + 1, :], (8, BLK)) for c in range(9)
        ]
        ax, ay, az, bx, by, bz, cx, cy, cz = corner
        ux, uy, uz = bx - ax, by - ay, bz - az
        vx, vy, vz = cx - ax, cy - ay, cz - az
        wx, wy, wz = cx - bx, cy - by, cz - bz
        ux2, uy2, uz2 = ux + ux, uy + uy, uz + uz
        nx = uy2 * vz - uz2 * vy
        ny = uz2 * vx - ux2 * vz
        nz = ux2 * vy - uy2 * vx
        side_ab = ux * ux + uy * uy + uz * uz
        side_bc = wx * wx + wy * wy + wz * wz
        side_ca = vx * vx + vy * vy + vz * vz
        for part in range(TILE // 8):
            at = pl.ds(part * 8, 8)
            if not starts:
                qx, qy, qz = spread[0, at], spread[1, at], spread[2, at]
            else:
                points = flipped[member, at, :]
                qx, qy, qz = [
                    jnp.broadcast_to(points[:, 3 * half + c : 3 * half + c + 1], (8, BLK)) for c in range(3)
                ]
                spread[0, at], spread[1, at], spread[2, at] = qx, qy, qz

            def from_point(x, y, z):
                x, y, z = x - qx, y - qy, z - qz
                square = x * x + y * y + z * z
                return x, y, z, square * lax.rsqrt(square)

            px, py, pz, la = from_point(ax, ay, az)
            lb = from_point(bx, by, bz)[3]
            lc = from_point(cx, cy, cz)[3]
            y = px * nx + py * ny + pz * nz
            x = (la + lb) * (lb + lc) * (lc + la) - (side_ab * lc + side_bc * la + side_ca * lb)
            if starts:
                real[tile, at], imag[tile, at] = x, y
                turns[tile, at] = jnp.zeros((8, BLK), jnp.float32)
            else:
                u, v = real[tile, at], imag[tile, at]
                below = y < 0.0
                r, i = u * x - v * y, u * y + v * x
                same = jnp.logical_not(jnp.logical_xor(v < 0.0, below))
                wrapped = jnp.logical_and(same, jnp.logical_xor(i < 0.0, below))
                turns[tile, at] += jnp.where(wrapped, jnp.where(below, -1.0, 1.0), 0.0)
                real[tile, at], imag[tile, at] = r, i
        row = pl.ds(block, 1)
        field = dipole([centres[c, row, :] for c in range(6)], points_ref[member, 3 * half : 3 * half + 3, :])
        out_ref[member, half : half + 1, :] -= field

    def one_member(member, found):
        for half in range(2):
            count = live_ref[member, half, PANELS]

            @pl.when(count > 0)
            def _():
                tiles[found] = member * 2 + half
                exact_block(live_ref[member, half, 0], found, member, half, True)

                def more(slot, carry):
                    @pl.when(slot % 4 == 0)
                    def _():
                        u, v = real[found], imag[found]
                        factor = 1.0 / (jnp.abs(u) + jnp.abs(v))
                        real[found], imag[found] = u * factor, v * factor

                    exact_block(live_ref[member, half, slot], found, member, half, False)
                    return carry

                lax.fori_loop(1, count, more, 0)

            found = found + jnp.where(count > 0, 1, 0)
        return found

    found = lax.fori_loop(0, PANELS, one_member, jnp.int32(0))

    def angle(x, y):
        ax, ay = jnp.abs(x), jnp.abs(y)
        t = jnp.minimum(ax, ay) / jnp.maximum(ax, ay)
        square = t * t
        value = jnp.full_like(t, ATAN[-1])
        for coefficient in ATAN[-2::-1]:
            value = value * square + coefficient
        value = value * t
        value = jnp.where(ay > ax, 0.5 * pi - value, value)
        value = jnp.where(x < 0.0, pi - value, value)
        return jnp.where(y < 0.0, -value, value)

    def add_angles(tile, carry):
        total = angle(real[tile], imag[tile]) * (0.5 / pi) + turns[tile]
        where = tiles[tile]
        row = pl.ds(where % 2, 1)
        out_ref[where // 2, row, :] += jnp.sum(total.T, axis=0, keepdims=True)
        return carry

    lax.fori_loop(0, found, add_angles, 0)


def near_call(live, panel, points):
    vmem = pl.BlockSpec(memory_space=pltpu.VMEM)
    smem = pl.BlockSpec(memory_space=pltpu.SMEM)
    return pl.pallas_call(
        near_kernel,
        out_shape=jax.ShapeDtypeStruct((PANELS, 2, TILE), jnp.float32),
        in_specs=[smem, vmem, vmem],
        out_specs=vmem,
        scratch_shapes=[
            pltpu.VMEM((3, TILE, BLK), jnp.float32),
            pltpu.VMEM((6, BLOCKS, TILE), jnp.float32),
            pltpu.VMEM((PANELS, TILE, 8), jnp.float32),
            pltpu.VMEM((2 * PANELS, TILE, BLK), jnp.float32),
            pltpu.VMEM((2 * PANELS, TILE, BLK), jnp.float32),
            pltpu.VMEM((2 * PANELS, TILE, BLK), jnp.float32),
            pltpu.SMEM((2 * PANELS,), jnp.int32),
        ],
        compiler_params=pltpu.CompilerParams(vmem_limit_bytes=32 * 1024 * 1024),
        name="near",
    )(live, panel, points)


def reduce_kernel(partial_ref, winding_ref, out_ref, arrived, send_sem, recv_sem):
    me = lax.axis_index("owner")
    lane = lax.axis_index("qgrp")
    group = me // TURNS
    member = (me % TURNS) * PAN_TURN + lane
    barrier = pltpu.get_barrier_semaphore()

    def device(step):
        to = (member + step) % PANELS
        return to, (group * TURNS + to // PAN_TURN, to % PAN_TURN)

    def greet(step, carry):
        pl.semaphore_signal(barrier, inc=1, device_id=device(step)[1], device_id_type=MESH)
        return carry

    lax.fori_loop(1, PANELS, greet, 0)
    pl.semaphore_wait(barrier, PANELS - 1)

    def send(step, carry):
        to, where = device(step)
        pltpu.make_async_remote_copy(
            src_ref=partial_ref.at[to], dst_ref=arrived.at[member], send_sem=send_sem, recv_sem=recv_sem,
            device_id=where, device_id_type=MESH,
        ).start()
        return carry

    lax.fori_loop(1, PANELS, send, 0)
    arrived[member] = partial_ref[member]
    part = arrived.at[pl.ds(0, PANELS - 1)]
    pltpu.make_async_copy(part, part, recv_sem).wait()
    out_ref[...] = winding_ref[...] + jnp.sum(arrived[...], axis=0)
    pltpu.make_async_copy(part, part, send_sem).wait()


def on_device(queries, winding_in, triangles, dipoles, plan, near_blocks, near_count):
    vmem = pl.BlockSpec(memory_space=pltpu.VMEM)
    smem = pl.BlockSpec(memory_space=pltpu.SMEM)
    hbm = pl.BlockSpec(memory_space=pl.ANY)
    f32 = jnp.float32
    panel, points, live = pl.pallas_call(
        gather_kernel,
        out_shape=(
            jax.ShapeDtypeStruct((BLOCKS, ROWS, BLK), f32),
            jax.ShapeDtypeStruct((PANELS, 8, TILE), f32),
            jax.ShapeDtypeStruct((PANELS, 2, 128), jnp.int32),
        ),
        in_specs=[smem, hbm, hbm, hbm, hbm, hbm],
        out_specs=(vmem, vmem, vmem),
        scratch_shapes=[
            pltpu.VMEM((3, 2 * TILE), f32),
            pltpu.VMEM((9, BLOCKS * BLK), f32),
            pltpu.VMEM((6, BLOCKS), f32),
            pltpu.VMEM((2, PANELS, NEAR), jnp.int32),
            pltpu.VMEM((2, PANELS), jnp.int32),
            pltpu.VMEM((BLOCKS, ROWS, BLK), f32),
            pltpu.VMEM((OWNERS, ROWS, BLK), f32),
            pltpu.VMEM((TURNS, ROWS, BLK), f32),
            pltpu.VMEM((PARTS, TURNS, ROWS, BLK), f32),
            pltpu.VMEM((8, TILE), f32),
            pltpu.VMEM((PANELS, 8, TILE), f32),
            pltpu.SemaphoreType.DMA((5,)),
        ]
        + [pltpu.SemaphoreType.DMA] * 7
        + [pltpu.SemaphoreType.REGULAR] * 2,
        compiler_params=pltpu.CompilerParams(collective_id=0, has_side_effects=True),
        name="gather",
    )(plan, queries, triangles, dipoles, near_blocks, near_count)
    partial = near_call(live, panel, points)
    total = pl.pallas_call(
        reduce_kernel,
        out_shape=jax.ShapeDtypeStruct((2, TILE), f32),
        in_specs=[vmem, vmem],
        out_specs=vmem,
        scratch_shapes=[pltpu.VMEM((PANELS, 2, TILE), f32)] + [pltpu.SemaphoreType.DMA] * 2,
        compiler_params=pltpu.CompilerParams(collective_id=1, has_side_effects=True),
        name="reduce",
    )(partial, winding_in.reshape(2, TILE))
    return total.reshape(-1)


def solution(mesh):
    return jax.shard_map(
        on_device,
        mesh=mesh,
        in_specs=(
            P(None, ("owner", "qgrp")),
            P(("owner", "qgrp")),
            P(None, ("owner", "qgrp")),
            P(None, ("owner", "qgrp")),
            P(),
            P(("owner", "qgrp"), None, None),
            P(("owner", "qgrp"), None),
        ),
        out_specs=P(("owner", "qgrp")),
        check_vma=False,
    )
```

```python
import functools

import jax
import jax.numpy as jnp
from jax import lax
from jax.experimental import pallas as pl
from jax.experimental.pallas import tpu as pltpu
from jax.sharding import PartitionSpec as P

TILE = 128
BLK = 128
BLOCKS = 32
NEAR = 4
TURNS = 4
PAN_TURN = 4
PANELS = TURNS * PAN_TURN
OWNERS = 64
ROWS = 10
PARTS = 8
MEMBERS_STEP = 2

MESH = pl.DeviceIdType.MESH

pi = 3.141592653589793
four_pi = 4.0 * pi
soften = 0.1

ATAN = (
    1.0,
    -0.3333309292793274,
    0.19993053376674652,
    -0.14207133650779724,
    0.10654675215482712,
    -0.07533672451972961,
    0.04303932562470436,
    -0.016282981261610985,
    0.0029035459738224745,
)


def block_of(place):
    kind, part = place % 4, place // 4
    return kind % 2 + (part % 2) * 2 + (kind // 2) * 4 + (part // 2) * 8


def owner_of(place, half):
    return (place // 8) * 16 + half * 8 + ((place // 4) % 2) * 4 + place % 4


def gather_kernel(
    plan_ref, queries_ref, triangles_ref, dipoles_ref, blocks_ref, count_ref,
    panel_ref, poles_ref, points_ref, live_ref,
    queries, dipoles, blocks, count, own,
    stage, arrived, chosen, final, message, messages, poles, live,
    load_sems, own_sem, out_sems, send_one, recv_one, send_two, recv_two, recv_far, send_msg, recv_msg, known, go,
):
    me = lax.axis_index("owner")
    lane = lax.axis_index("qgrp")
    half = (me // 8) % 2
    place = ((me // 16) * 2 + (me // 4) % 2) * 4 + me % 4
    kind = me % 4
    part = place // 4
    member = kind * PAN_TURN + lane
    first = half == 0
    barrier = pltpu.get_barrier_semaphore()

    loads = [
        pltpu.make_async_copy(source, target, load_sems.at[index])
        for index, (source, target) in enumerate(
            [
                (dipoles_ref, dipoles), (queries_ref, queries), (blocks_ref, blocks), (count_ref, count),
            ]
        )
    ]
    for load in loads:
        load.start()

    @pl.when(first)
    def _():
        def greet(step, carry):
            pl.semaphore_signal(
                barrier, inc=1, device_id=((me + step) % OWNERS, lane), device_id_type=MESH
            )
            return carry

        lax.fori_loop(1, OWNERS, greet, 0)

        def greet_member(step, carry):
            pl.semaphore_signal(
                barrier, inc=1,
                device_id=((me // 4) * 4 + step % 4, (lane + 1 + step // 4) % PAN_TURN), device_id_type=MESH,
            )
            return carry

        lax.fori_loop(0, 4 * (PAN_TURN - 1), greet_member, 0)

    def block_ref(place):
        return triangles_ref.at[:, pl.ds(pl.multiple_of(block_of(place) * BLK, BLK), BLK)]

    own_block = pltpu.make_async_copy(block_ref(place), own, own_sem)
    own_block.start()

    def make_stage():
        loads[0].wait()
        flipped = jnp.concatenate(
            [jnp.concatenate([dipoles[...], jnp.zeros((2, BLOCKS), jnp.float32)], axis=0),
             jnp.zeros((8, BLK - BLOCKS), jnp.float32)], axis=1
        ).T
        for slot in range(BLOCKS):
            block = block_of(slot)
            stage[slot, :, 0:8] = flipped[block : block + 1, :]

    def send_first(step, carry):
        to = (place + step) % BLOCKS
        pltpu.make_async_remote_copy(
            src_ref=block_ref(to), dst_ref=arrived.at[me, pl.ds(0, 9)], send_sem=send_one, recv_sem=recv_one,
            device_id=(owner_of(to, 0), lane), device_id_type=MESH,
        ).start()
        return carry

    def send_dipole(step, carry):
        to = (place + step) % BLOCKS
        pltpu.make_async_remote_copy(
            src_ref=stage.at[to], dst_ref=arrived.at[me, pl.ds(9, 1)], send_sem=send_one, recv_sem=recv_one,
            device_id=(owner_of(to, 0), lane), device_id_type=MESH,
        ).start()
        return carry

    def make_message():
        for load in loads[1:]:
            load.wait()
        message[0:3] = queries[:, 0:TILE]
        message[3:6] = queries[:, TILE : 2 * TILE]
        for tile in range(2):
            counted = count[tile : tile + 1, :]
            rows = [jnp.where(counted > slot, blocks[tile, slot : slot + 1, :], -1) for slot in range(NEAR)]
            rows.append(jnp.full((1, BLK - PANELS * NEAR), -1, jnp.int32))
            message[6 + tile : 7 + tile] = jnp.concatenate(rows, axis=1).astype(jnp.float32)

    def send_message(step, carry):
        to = (member + step) % PANELS
        pltpu.make_async_remote_copy(
            src_ref=message, dst_ref=messages.at[member], send_sem=send_msg, recv_sem=recv_msg,
            device_id=((me // 4) * 4 + to // PAN_TURN, to % PAN_TURN), device_id_type=MESH,
        ).start()
        return carry

    def send_second(step, carry):
        to = ((part + step) % PARTS) * 4 + kind
        pltpu.make_async_remote_copy(
            src_ref=chosen, dst_ref=final.at[part], send_sem=send_two, recv_sem=recv_two,
            device_id=(owner_of(to, half), lane), device_id_type=MESH,
        ).start()
        return carry

    def wait_bytes(part, sem):
        pltpu.make_async_copy(part, part, sem).wait()

    @pl.when(first)
    def _():
        pl.semaphore_wait(barrier, BLOCKS - 1 + 4 * (PAN_TURN - 1))
        lax.fori_loop(1, BLOCKS, send_first, 0)
        make_stage()
        lax.fori_loop(1, BLOCKS, send_dipole, 0)
        make_message()
        lax.fori_loop(1, PANELS, send_message, 0)
        own_block.wait()
        arrived[me, 0:9] = own[...]
        arrived[me, 9:10] = stage[place]
        wait_bytes(arrived.at[pl.ds(0, OWNERS - 1)], recv_one)
        for turn in range(TURNS):
            chosen[turn] = arrived[plan_ref[turn]]
        lax.fori_loop(1, PARTS, send_second, 0)
        pltpu.make_async_remote_copy(
            src_ref=chosen, dst_ref=chosen, send_sem=send_two, recv_sem=recv_far,
            device_id=(me + 8, lane), device_id_type=MESH,
        ).start()
        for step in range(1, PAN_TURN):
            pl.semaphore_signal(
                known, inc=1, device_id=(me, (lane + step) % PAN_TURN), device_id_type=MESH
            )
        pl.semaphore_wait(known, PAN_TURN - 1)
        pl.semaphore_signal(go, inc=1, device_id=(me + 8, lane), device_id_type=MESH)

    @pl.when(jnp.logical_not(first))
    def _():
        pl.semaphore_wait(barrier, BLOCKS)
        lax.fori_loop(0, BLOCKS, send_first, 0)
        make_stage()
        lax.fori_loop(0, BLOCKS, send_dipole, 0)
        own_block.wait()
        make_message()
        wait_bytes(chosen, recv_far)
        lax.fori_loop(1, PARTS, send_second, 0)
        pl.semaphore_wait(go, 1)
        lax.fori_loop(1, PANELS, send_message, 0)

    final[part] = chosen[...]
    messages[member] = message[...]
    wait_bytes(messages.at[pl.ds(0, PANELS - 1)], recv_msg)
    outs = [
        pltpu.make_async_copy(source, target, out_sems.at[index])
        for index, (source, target) in enumerate(
            [(messages, points_ref), (live, live_ref), (final, panel_ref), (poles, poles_ref)]
        )
    ]
    outs[0].start()

    shape = (PANELS, BLK)
    column = lax.broadcasted_iota(jnp.int32, shape, 1)
    before = (
        lax.broadcasted_iota(jnp.int32, (BLK, BLK), 0) < lax.broadcasted_iota(jnp.int32, (BLK, BLK), 1)
    ).astype(jnp.float32)
    for tile in range(2):
        listed = messages[:, 6 + tile, :].astype(jnp.int32)
        held = (listed % 2) + ((listed // 4) % 2) * 2 == kind
        held = jnp.logical_and(held, column % PAN_TURN == lane)
        held = jnp.logical_and(held, jnp.logical_and(listed >= 0, column < PANELS * NEAR))
        value = ((listed // 2) % 2 + (listed // 8) * 2) * 4 + (column % PANELS) // PAN_TURN
        value = value.astype(jnp.float32)
        flags = jnp.where(held, 1.0, 0.0)
        rank = lax.dot_general(flags, before, (((1,), (0,)), ((), ())), preferred_element_type=jnp.float32)
        rank = jnp.where(held, rank, -1.0)
        packed = jnp.where(column == PANELS, jnp.sum(flags, axis=1, keepdims=True), 0.0)
        for index in range(PANELS):
            one = jnp.sum(jnp.where(jnp.abs(rank - index) < 0.5, value, 0.0), axis=1, keepdims=True)
            packed = jnp.where(column == index, one, packed)
        live[:, tile, :] = packed.astype(jnp.int32)
    outs[1].start()

    wait_bytes(final.at[pl.ds(0, PARTS - 1)], recv_two)
    outs[2].start()
    for slot in range(BLOCKS):
        poles[slot : slot + 1] = final[slot // 4, slot % 4, 9:10, :]
    outs[3].start()

    @pl.when(first)
    def _():
        wait_bytes(arrived.at[pl.ds(0, BLOCKS - 1)], send_one)
        wait_bytes(final, send_two)

    @pl.when(jnp.logical_not(first))
    def _():
        wait_bytes(arrived.at[pl.ds(0, BLOCKS)], send_one)
        wait_bytes(final.at[pl.ds(0, PARTS - 1)], send_two)

    wait_bytes(messages.at[pl.ds(0, PANELS - 1)], send_msg)
    for out in outs:
        out.wait()


def dipole_field(centre, points):
    offset = [centre[c] - jnp.broadcast_to(points[c : c + 1, :], centre[c].shape) for c in range(3)]
    square = offset[0] * offset[0] + offset[1] * offset[1] + offset[2] * offset[2] + soften
    inverse = lax.rsqrt(square)
    return (centre[3] * offset[0] + centre[4] * offset[1] + centre[5] * offset[2]) * (
        inverse * inverse * inverse
    )


def spread_poles(rows, centres):
    for component in range(6):
        value = jnp.broadcast_to(rows[:, component : component + 1], (BLOCKS, TILE))
        if component >= 3:
            value = value * (1.0 / four_pi)
        centres[component] = value


def near_kernel(
    live_hbm, panel_hbm, poles_hbm, points_hbm, out_ref,
    live_ref, panel_ref, poles_ref, points_ref, spread, centres, flipped, real, imag, turns, tiles, sums, sems
):
    loads = [
        pltpu.make_async_copy(source, target, sems.at[index])
        for index, (source, target) in enumerate(
            [(live_hbm, live_ref), (panel_hbm, panel_ref), (poles_hbm, poles_ref), (points_hbm, points_ref)]
        )
    ]
    for load in loads:
        load.start()
    out_ref[...] = jnp.zeros_like(out_ref)
    sums[...] = jnp.zeros_like(sums)
    loads[2].wait()
    spread_poles(poles_ref[...], centres)
    loads[3].wait()
    for member in range(PANELS):
        flipped[member] = points_ref[member].T
    loads[0].wait()
    loads[1].wait()

    def exact_block(block, tile, member, half, starts):
        corner = [
            jnp.broadcast_to(panel_ref[block // 4, block % 4, c : c + 1, :], (8, BLK)) for c in range(9)
        ]
        ax, ay, az, bx, by, bz, cx, cy, cz = corner
        ux, uy, uz = bx - ax, by - ay, bz - az
        vx, vy, vz = cx - ax, cy - ay, cz - az
        wx, wy, wz = cx - bx, cy - by, cz - bz
        ux2, uy2, uz2 = ux + ux, uy + uy, uz + uz
        nx = uy2 * vz - uz2 * vy
        ny = uz2 * vx - ux2 * vz
        nz = ux2 * vy - uy2 * vx
        side_ab = ux * ux + uy * uy + uz * uz
        side_bc = wx * wx + wy * wy + wz * wz
        side_ca = vx * vx + vy * vy + vz * vz
        for part in range(TILE // 8):
            at = pl.ds(part * 8, 8)
            if not starts:
                qx, qy, qz = spread[0, at], spread[1, at], spread[2, at]
            else:
                points = flipped[member, at, :]
                qx, qy, qz = [
                    jnp.broadcast_to(points[:, 3 * half + c : 3 * half + c + 1], (8, BLK)) for c in range(3)
                ]
                spread[0, at], spread[1, at], spread[2, at] = qx, qy, qz

            def from_point(x, y, z):
                x, y, z = x - qx, y - qy, z - qz
                square = x * x + y * y + z * z
                return x, y, z, square * lax.rsqrt(square)

            px, py, pz, la = from_point(ax, ay, az)
            lb = from_point(bx, by, bz)[3]
            lc = from_point(cx, cy, cz)[3]
            y = px * nx + py * ny + pz * nz
            x = (la + lb) * (lb + lc) * (lc + la) - (side_ab * lc + side_bc * la + side_ca * lb)
            if starts:
                real[tile, at], imag[tile, at] = x, y
                turns[tile, at] = jnp.zeros((8, BLK), jnp.float32)
            else:
                u, v = real[tile, at], imag[tile, at]
                below = y < 0.0
                r, i = u * x - v * y, u * y + v * x
                same = jnp.logical_not(jnp.logical_xor(v < 0.0, below))
                wrapped = jnp.logical_and(same, jnp.logical_xor(i < 0.0, below))
                turns[tile, at] += jnp.where(wrapped, jnp.where(below, -1.0, 1.0), 0.0)
                real[tile, at], imag[tile, at] = r, i
        row = pl.ds(block, 1)
        field = dipole_field([centres[c, row, :] for c in range(6)], points_ref[member, 3 * half : 3 * half + 3, :])
        out_ref[member, half : half + 1, :] -= field

    def one_member(member, found):
        for half in range(2):
            count = live_ref[member, half, PANELS]

            @pl.when(count > 0)
            def _():
                tiles[found] = member * 2 + half
                exact_block(live_ref[member, half, 0], found, member, half, True)

                def more(slot, carry):
                    @pl.when(slot % 4 == 0)
                    def _():
                        u, v = real[found], imag[found]
                        factor = 1.0 / (jnp.abs(u) + jnp.abs(v))
                        real[found], imag[found] = u * factor, v * factor

                    exact_block(live_ref[member, half, slot], found, member, half, False)
                    return carry

                lax.fori_loop(1, count, more, 0)

            found = found + jnp.where(count > 0, 1, 0)
        return found

    found = lax.fori_loop(0, PANELS, one_member, jnp.int32(0))

    def angle(x, y):
        ax, ay = jnp.abs(x), jnp.abs(y)
        t = jnp.minimum(ax, ay) / jnp.maximum(ax, ay)
        square = t * t
        value = jnp.full_like(t, ATAN[-1])
        for coefficient in ATAN[-2::-1]:
            value = value * square + coefficient
        value = value * t
        value = jnp.where(ay > ax, 0.5 * pi - value, value)
        value = jnp.where(x < 0.0, pi - value, value)
        return jnp.where(y < 0.0, -value, value)

    lanes = lax.broadcasted_iota(jnp.int32, (TILE, BLK), 1)

    def add_angles(tile, carry):
        total = angle(real[tile], imag[tile]) * (0.5 / pi) + turns[tile]
        sums[...] = jnp.where(lanes == tiles[tile], jnp.sum(total, axis=1, keepdims=True), sums[...])
        return carry

    lax.fori_loop(0, found, add_angles, 0)
    rows = sums[...].T
    for member in range(PANELS):
        out_ref[member] += rows[2 * member : 2 * member + 2, :]


def near_call(live, panel, poles, points):
    hbm = pl.BlockSpec(memory_space=pl.ANY)
    f32 = jnp.float32
    return pl.pallas_call(
        near_kernel,
        out_shape=jax.ShapeDtypeStruct((PANELS, 2, TILE), f32),
        in_specs=[hbm] * 4,
        out_specs=pl.BlockSpec(memory_space=pltpu.VMEM),
        scratch_shapes=[
            pltpu.SMEM((PANELS, 2, 128), jnp.int32),
            pltpu.VMEM((PARTS, TURNS, ROWS, BLK), f32),
            pltpu.VMEM((BLOCKS, BLK), f32),
            pltpu.VMEM((PANELS, 8, TILE), f32),
            pltpu.VMEM((3, TILE, BLK), f32),
            pltpu.VMEM((6, BLOCKS, TILE), f32),
            pltpu.VMEM((PANELS, TILE, 8), f32),
            pltpu.VMEM((2 * PANELS, TILE, BLK), f32),
            pltpu.VMEM((2 * PANELS, TILE, BLK), f32),
            pltpu.VMEM((2 * PANELS, TILE, BLK), f32),
            pltpu.SMEM((2 * PANELS,), jnp.int32),
            pltpu.VMEM((TILE, BLK), f32),
            pltpu.SemaphoreType.DMA((4,)),
        ],
        compiler_params=pltpu.CompilerParams(vmem_limit_bytes=60 * 1024 * 1024),
        name="near",
    )(live, panel, poles, points)


def reduce_kernel(
    partial_hbm, poles_hbm, points_hbm, out_ref,
    partial, far, poles, points, centres, arrived, load_sems, send_sem, recv_sem,
):
    me = lax.axis_index("owner")
    lane = lax.axis_index("qgrp")
    group = me // TURNS
    member = (me % TURNS) * PAN_TURN + lane
    barrier = pltpu.get_barrier_semaphore()
    loads = [
        pltpu.make_async_copy(source, target, load_sems.at[index])
        for index, (source, target) in enumerate(
            [(partial_hbm, partial), (poles_hbm, poles), (points_hbm, points)]
        )
    ]
    for load in loads:
        load.start()

    def device(step):
        to = (member + step) % PANELS
        return to, (group * TURNS + to // PAN_TURN, to % PAN_TURN)

    def greet(step, carry):
        pl.semaphore_signal(barrier, inc=1, device_id=device(step)[1], device_id_type=MESH)
        return carry

    lax.fori_loop(1, PANELS, greet, 0)
    for load in loads:
        load.wait()
    spread_poles(poles[...], centres)

    def far_field(step, carry):
        for index in range(MEMBERS_STEP):
            one = step * MEMBERS_STEP + index
            for half in range(2):
                field = dipole_field([centres[c] for c in range(6)], points[one, 3 * half : 3 * half + 3, :])
                far[one, half : half + 1, :] = partial[one, half : half + 1, :] + jnp.sum(
                    field, axis=0, keepdims=True
                )
        return carry

    lax.fori_loop(0, PANELS // MEMBERS_STEP, far_field, 0)
    pl.semaphore_wait(barrier, PANELS - 1)

    def send(step, carry):
        to, where = device(step)
        pltpu.make_async_remote_copy(
            src_ref=far.at[to], dst_ref=arrived.at[member], send_sem=send_sem, recv_sem=recv_sem,
            device_id=where, device_id_type=MESH,
        ).start()
        return carry

    lax.fori_loop(1, PANELS, send, 0)
    arrived[member] = far[member]
    part = arrived.at[pl.ds(0, PANELS - 1)]
    pltpu.make_async_copy(part, part, recv_sem).wait()
    out_ref[...] = jnp.sum(arrived[...], axis=0)
    pltpu.make_async_copy(part, part, send_sem).wait()


def on_device(queries, winding_in, triangles, dipoles, plan, near_blocks, near_count):
    vmem = pl.BlockSpec(memory_space=pltpu.VMEM)
    smem = pl.BlockSpec(memory_space=pltpu.SMEM)
    hbm = pl.BlockSpec(memory_space=pl.ANY)
    f32 = jnp.float32
    panel, poles, points, live = pl.pallas_call(
        gather_kernel,
        out_shape=(
            jax.ShapeDtypeStruct((PARTS, TURNS, ROWS, BLK), f32),
            jax.ShapeDtypeStruct((BLOCKS, BLK), f32),
            jax.ShapeDtypeStruct((PANELS, 8, TILE), f32),
            jax.ShapeDtypeStruct((PANELS, 2, 128), jnp.int32),
        ),
        in_specs=[smem, hbm, hbm, hbm, hbm, hbm],
        out_specs=(hbm, hbm, hbm, hbm),
        scratch_shapes=[
            pltpu.VMEM((3, 2 * TILE), f32),
            pltpu.VMEM((6, BLOCKS), f32),
            pltpu.VMEM((2, NEAR, PANELS), jnp.int32),
            pltpu.VMEM((2, PANELS), jnp.int32),
            pltpu.VMEM((9, BLK), f32),
            pltpu.VMEM((BLOCKS, 1, BLK), f32),
            pltpu.VMEM((OWNERS, ROWS, BLK), f32),
            pltpu.VMEM((TURNS, ROWS, BLK), f32),
            pltpu.VMEM((PARTS, TURNS, ROWS, BLK), f32),
            pltpu.VMEM((8, TILE), f32),
            pltpu.VMEM((PANELS, 8, TILE), f32),
            pltpu.VMEM((BLOCKS, BLK), f32),
            pltpu.VMEM((PANELS, 2, 128), jnp.int32),
            pltpu.SemaphoreType.DMA((4,)),
            pltpu.SemaphoreType.DMA,
            pltpu.SemaphoreType.DMA((4,)),
        ]
        + [pltpu.SemaphoreType.DMA] * 7
        + [pltpu.SemaphoreType.REGULAR] * 2,
        compiler_params=pltpu.CompilerParams(collective_id=0, has_side_effects=True),
        name="gather",
    )(plan, queries, triangles, dipoles, near_blocks.transpose(0, 2, 1), near_count)
    partial = near_call(live, panel, poles, points)
    total = pl.pallas_call(
        reduce_kernel,
        out_shape=jax.ShapeDtypeStruct((2, TILE), f32),
        in_specs=[hbm] * 3,
        out_specs=vmem,
        scratch_shapes=[
            pltpu.VMEM((PANELS, 2, TILE), f32),
            pltpu.VMEM((PANELS, 2, TILE), f32),
            pltpu.VMEM((BLOCKS, BLK), f32),
            pltpu.VMEM((PANELS, 8, TILE), f32),
            pltpu.VMEM((6, BLOCKS, TILE), f32),
            pltpu.VMEM((PANELS, 2, TILE), f32),
            pltpu.SemaphoreType.DMA((3,)),
            pltpu.SemaphoreType.DMA,
            pltpu.SemaphoreType.DMA,
        ],
        compiler_params=pltpu.CompilerParams(collective_id=1, has_side_effects=True),
        name="reduce",
    )(partial, poles, points)
    return winding_in + total.reshape(-1)


def solution(mesh):
    return jax.shard_map(
        on_device,
        mesh=mesh,
        in_specs=(
            P(None, ("owner", "qgrp")),
            P(("owner", "qgrp")),
            P(None, ("owner", "qgrp")),
            P(None, ("owner", "qgrp")),
            P(),
            P(("owner", "qgrp"), None, None),
            P(("owner", "qgrp"), None),
        ),
        out_specs=P(("owner", "qgrp")),
        check_vma=False,
    )
```

```python
import functools

import jax
import jax.numpy as jnp
from jax import lax
from jax.experimental import pallas as pl
from jax.experimental.pallas import tpu as pltpu
from jax.sharding import PartitionSpec as P

TILE = 128
BLK = 128
BLOCKS = 32
NEAR = 4
TURNS = 4
PAN_TURN = 4
PANELS = TURNS * PAN_TURN
OWNERS = 64
ROWS = 10
PARTS = 8
MEMBERS_STEP = 2

MESH = pl.DeviceIdType.MESH

pi = 3.141592653589793
four_pi = 4.0 * pi
soften = 0.1

ATAN = (
    0.9999994039535522,
    -0.3332701325416565,
    0.19887319207191467,
    -0.13512171804904938,
    0.08435401320457458,
    -0.03744291514158249,
    0.008006880059838295,
)


def block_of(place):
    kind, part = place % 4, place // 4
    return kind % 2 + (part % 2) * 2 + (kind // 2) * 4 + (part // 2) * 8


def owner_of(place, half):
    return (place // 8) * 16 + half * 8 + ((place // 4) % 2) * 4 + place % 4


def stage_place(slot):
    return (slot // 8) * 8 + (slot % 2) * 4 + (slot // 2) % 4


def gather_kernel(
    plan_ref, queries_ref, triangles_ref, dipoles_ref, blocks_ref, count_ref,
    panel_ref, poles_ref, points_ref, live_ref,
    queries, triangles, dipoles, blocks, count,
    stage, arrived, gathered, picked, late, chosen, final, message, messages, poles, live,
    load_sems, out_sems, send_one, recv_one, send_late, recv_late, send_two, recv_two, recv_far, send_msg, recv_msg, known, go,
):
    me = lax.axis_index("owner")
    lane = lax.axis_index("qgrp")
    half = (me // 8) % 2
    place = ((me // 16) * 2 + (me // 4) % 2) * 4 + me % 4
    kind = me % 4
    part = place // 4
    member = kind * PAN_TURN + lane
    mirror = PAN_TURN - 1 - lane
    role = half * lane + (1 - half) * mirror
    first = half == 0
    barrier = pltpu.get_barrier_semaphore()

    loads = [
        pltpu.make_async_copy(source, target, load_sems.at[index])
        for index, (source, target) in enumerate(
            [
                (triangles_ref, triangles), (dipoles_ref, dipoles), (queries_ref, queries),
                (blocks_ref, blocks), (count_ref, count),
            ]
        )
    ]
    for load in loads:
        load.start()

    def greet(owner, to_lane):
        pl.semaphore_signal(barrier, inc=1, device_id=(owner, to_lane), device_id_type=MESH)

    @pl.when(first)
    def _():
        for side in range(2):
            greet(owner_of(place - (part % 2) * 4 + side * 4, 1), mirror)

        def greet_one(step, carry):
            greet(owner_of((place + step) % BLOCKS, 0), mirror)
            return carry

        lax.fori_loop(0, BLOCKS, greet_one, 0)
        for step in range(1, PARTS):
            greet(owner_of(((part + step) % PARTS) * 4 + kind, 0), lane)
        for step in range(1, 4):
            greet((me // 4) * 4 + (me + step) % 4, lane)
        for step in range(4):
            greet((me // 4) * 4 + step, (lane + 2) % PAN_TURN)
            greet((me // 4) * 4 + step, PAN_TURN - 1 - (lane + 2) % PAN_TURN)

    squad = (part // 2) * 4 + kind

    def comrade(step):
        other = (squad + step) % 16
        return other, ((other // 4) * 16 + 8 + (part % 2) * 4 + other % 4, lane)

    @pl.when(jnp.logical_not(first))
    def _():
        def greet_comrade(step, carry):
            greet(*comrade(step)[1])
            return carry

        lax.fori_loop(1, 16, greet_comrade, 0)

    loads[1].wait()
    flipped = jnp.concatenate(
        [jnp.concatenate([dipoles[...], jnp.zeros((2, BLOCKS), jnp.float32)], axis=0),
         jnp.zeros((8, BLK - BLOCKS), jnp.float32)], axis=1
    ).T
    loads[0].wait()
    for slot in range(BLOCKS):
        block = block_of(stage_place(slot))
        stage[slot // 2, slot % 2, 0:9] = triangles[:, block * BLK : (block + 1) * BLK]
        stage[slot // 2, slot % 2, 9:10, 0:8] = flipped[block : block + 1, :]

    def send_first(step, carry):
        to = (place + step) % BLOCKS
        pltpu.make_async_remote_copy(
            src_ref=stage.at[(to // 8) * 4 + to % 4, (to // 4) % 2], dst_ref=arrived.at[place], send_sem=send_one, recv_sem=recv_one,
            device_id=(owner_of(to, 0), mirror), device_id_type=MESH,
        ).start()
        return carry

    def send_comrade(step, carry):
        other, where = comrade(step)
        pltpu.make_async_remote_copy(
            src_ref=stage.at[other], dst_ref=gathered.at[squad], send_sem=send_one, recv_sem=recv_one,
            device_id=where, device_id_type=MESH,
        ).start()
        return carry

    def make_message():
        for load in loads[2:]:
            load.wait()
        message[0:3] = queries[:, 0:TILE]
        message[3:6] = queries[:, TILE : 2 * TILE]
        for tile in range(2):
            counted = count[tile : tile + 1, :]
            rows = [jnp.where(counted > slot, blocks[tile, slot : slot + 1, :], -1) for slot in range(NEAR)]
            rows.append(jnp.full((1, BLK - PANELS * NEAR), -1, jnp.int32))
            message[6 + tile : 7 + tile] = jnp.concatenate(rows, axis=1).astype(jnp.float32)

    def send_message(step, carry):
        to = (member + step) % PANELS
        pltpu.make_async_remote_copy(
            src_ref=message, dst_ref=messages.at[member], send_sem=send_msg, recv_sem=recv_msg,
            device_id=((me // 4) * 4 + to // PAN_TURN, to % PAN_TURN), device_id_type=MESH,
        ).start()
        return carry

    def send_second():
        for step in (5, 4, 3, 6, 2, 7, 1):
            to = ((part + step) % PARTS) * 4 + kind
            pltpu.make_async_remote_copy(
                src_ref=chosen, dst_ref=final.at[part], send_sem=send_two, recv_sem=recv_two,
                device_id=(owner_of(to, half), lane), device_id_type=MESH,
            ).start()

    def wait_bytes(part, sem):
        pltpu.make_async_copy(part, part, sem).wait()

    @pl.when(first)
    def _():
        pl.semaphore_wait(barrier, BLOCKS + PARTS - 1 + 3 + 8)
        lax.fori_loop(0, BLOCKS, send_first, 0)
        make_message()
        lax.fori_loop(1, PANELS, send_message, 0)
        wait_bytes(arrived, recv_one)
        wait_bytes(late, recv_late)
        for turn in range(TURNS):
            owner = plan_ref[turn]
            early = arrived[((owner // 16) * 2 + (owner // 4) % 2) * 4 + owner % 4]
            chosen[turn] = jnp.where((owner // 8) % 2 == 0, early, late[(owner // 4) % 2, turn])
        pltpu.make_async_remote_copy(
            src_ref=chosen, dst_ref=chosen, send_sem=send_two, recv_sem=recv_far,
            device_id=(me + 8, mirror), device_id_type=MESH,
        ).start()
        send_second()
        for step in range(1, PAN_TURN):
            pl.semaphore_signal(
                known, inc=1, device_id=(me, (lane + step) % PAN_TURN), device_id_type=MESH
            )
        pl.semaphore_wait(known, PAN_TURN - 1)
        pl.semaphore_signal(go, inc=1, device_id=(me + 8, mirror), device_id_type=MESH)

    @pl.when(jnp.logical_not(first))
    def _():
        pl.semaphore_wait(barrier, 15 + 2)
        lax.fori_loop(1, 16, send_comrade, 0)
        gathered[squad] = stage[squad]
        wait_bytes(gathered.at[pl.ds(0, 15)], recv_one)
        for turn in range(TURNS):
            owner = plan_ref[turn]
            pair = gathered[(owner // 16) * 4 + owner % 4]
            picked[0, turn] = pair[0]
            picked[1, turn] = pair[1]
        for side in range(2):
            pltpu.make_async_remote_copy(
                src_ref=picked.at[side], dst_ref=late.at[part % 2], send_sem=send_late, recv_sem=recv_late,
                device_id=(owner_of(place - (part % 2) * 4 + side * 4, 0), mirror), device_id_type=MESH,
            ).start()
        make_message()
        wait_bytes(chosen, recv_far)
        send_second()
        pl.semaphore_wait(go, 1)
        lax.fori_loop(1, PANELS, send_message, 0)

    final[part] = chosen[...]
    messages[member] = message[...]
    wait_bytes(messages.at[pl.ds(0, PANELS - 1)], recv_msg)
    outs = [
        pltpu.make_async_copy(source, target, out_sems.at[index])
        for index, (source, target) in enumerate(
            [(messages, points_ref), (live, live_ref), (final, panel_ref), (poles, poles_ref)]
        )
    ]
    outs[0].start()

    shape = (PANELS, BLK)
    column = lax.broadcasted_iota(jnp.int32, shape, 1)
    before = (
        lax.broadcasted_iota(jnp.int32, (BLK, BLK), 0) < lax.broadcasted_iota(jnp.int32, (BLK, BLK), 1)
    ).astype(jnp.float32)
    for tile in range(2):
        listed = messages[:, 6 + tile, :].astype(jnp.int32)
        held = (listed % 2) + ((listed // 4) % 2) * 2 == kind
        held = jnp.logical_and(held, column % PAN_TURN == role)
        held = jnp.logical_and(held, jnp.logical_and(listed >= 0, column < PANELS * NEAR))
        value = ((listed // 2) % 2 + (listed // 8) * 2) * 4 + (column % PANELS) // PAN_TURN
        value = value.astype(jnp.float32)
        flags = jnp.where(held, 1.0, 0.0)
        rank = lax.dot_general(flags, before, (((1,), (0,)), ((), ())), preferred_element_type=jnp.float32)
        rank = jnp.where(held, rank, -1.0)
        packed = jnp.where(column == PANELS, jnp.sum(flags, axis=1, keepdims=True), 0.0)
        for index in range(PANELS):
            one = jnp.sum(jnp.where(jnp.abs(rank - index) < 0.5, value, 0.0), axis=1, keepdims=True)
            packed = jnp.where(column == index, one, packed)
        live[:, tile, :] = packed.astype(jnp.int32)
    outs[1].start()

    wait_bytes(final.at[pl.ds(0, PARTS - 1)], recv_two)
    outs[2].start()
    for slot in range(BLOCKS):
        poles[slot : slot + 1] = final[slot // 4, slot % 4, 9:10, :]
    outs[3].start()

    @pl.when(first)
    def _():
        wait_bytes(stage, send_one)
        wait_bytes(final, send_two)

    @pl.when(jnp.logical_not(first))
    def _():
        wait_bytes(stage.at[pl.ds(0, 15)], send_one)
        wait_bytes(picked, send_late)
        wait_bytes(final.at[pl.ds(0, PARTS - 1)], send_two)

    wait_bytes(messages.at[pl.ds(0, PANELS - 1)], send_msg)
    for out in outs:
        out.wait()


def dipole_field(centre, points):
    offset = [centre[c] - jnp.broadcast_to(points[c : c + 1, :], centre[c].shape) for c in range(3)]
    square = offset[0] * offset[0] + offset[1] * offset[1] + offset[2] * offset[2] + soften
    inverse = lax.rsqrt(square)
    return (centre[3] * offset[0] + centre[4] * offset[1] + centre[5] * offset[2]) * (
        inverse * inverse * inverse
    )


def spread_poles(rows, centres):
    for component in range(6):
        value = jnp.broadcast_to(rows[:, component : component + 1], (BLOCKS, TILE))
        if component >= 3:
            value = value * (1.0 / four_pi)
        centres[component] = value


def near_kernel(
    live_hbm, panel_hbm, poles_hbm, points_hbm, out_ref,
    live_ref, panel_ref, poles_ref, given, points_ref, flipped, picker, centres,
    spread_0, spread_1, real_0, real_1, imag_0, imag_1, turns_0, turns_1, tiles, sums, minus, sems
):
    spread, real, imag, turns = (spread_0, spread_1), (real_0, real_1), (imag_0, imag_1), (turns_0, turns_1)
    loads = [
        pltpu.make_async_copy(source, target, sems.at[index])
        for index, (source, target) in enumerate(
            [(live_hbm, live_ref), (panel_hbm, panel_ref), (poles_hbm, poles_ref), (points_hbm, given)]
        )
    ]
    for load in loads:
        load.start()
    minus[...] = jnp.zeros_like(minus)
    sums[...] = jnp.zeros_like(sums)
    real_0[...] = jnp.ones_like(real_0)
    imag_0[...] = jnp.zeros_like(imag_0)
    turns_0[...] = jnp.zeros_like(turns_0)
    loads[2].wait()
    spread_poles(poles_ref[...], centres)
    loads[3].wait()
    for member in range(PANELS):
        for half in range(2):
            points_ref[2 * member + half, 0:3] = given[member, 3 * half : 3 * half + 3]
    loads[0].wait()

    tiles[0] = 2 * PANELS
    found = jnp.int32(0)
    for tile in range(2 * PANELS):
        tiles[found + 1] = tile
        found = found + jnp.where(live_ref[tile // 2, tile % 2, PANELS] > 0, 1, 0)
    tiles[found + 1] = 0
    lanes = lax.broadcasted_iota(jnp.int32, (8, BLK), 1)

    for member in range(PANELS):
        rest = given[member]
        parts = []
        for _ in range(3):
            parts.append(rest.astype(jnp.bfloat16).astype(jnp.float32))
            rest = rest - parts[-1]
        parts.append(jnp.zeros_like(rest))
        flipped[member] = jnp.concatenate(parts, axis=0).T.astype(jnp.bfloat16)
    shape = (32, 3 * BLK)
    entry = lax.broadcasted_iota(jnp.int32, shape, 0)
    component = lax.broadcasted_iota(jnp.int32, shape, 1) // BLK
    for half in range(2):
        wanted = jnp.logical_and(entry % 8 == 3 * half + component, entry < 24)
        picker[half] = jnp.where(wanted, 1.0, 0.0).astype(jnp.bfloat16)

    def widen(tile):
        return lax.dot_general(
            flipped[tile // 2], picker[tile % 2], (((1,), (0,)), ((), ())), preferred_element_type=jnp.float32
        )

    def spread_part(place, part, wide):
        at = pl.ds(part * 8, 8)
        for c in range(3):
            spread[place][c, at] = wide[part * 8 : part * 8 + 8, c * BLK : (c + 1) * BLK]

    def angle(x, y):
        ax, ay = jnp.abs(x), jnp.abs(y)
        t = jnp.minimum(ax, ay) * pl.reciprocal(jnp.maximum(ax, ay), approx=True)
        square = t * t
        value = jnp.full_like(t, ATAN[-1] * 0.5 / pi)
        for coefficient in ATAN[-2::-1]:
            value = value * square + coefficient * 0.5 / pi
        value = value * t
        value = jnp.where(ay > ax, 0.25 - value, value)
        value = jnp.where(x < 0.0, 0.5 - value, value)
        return jnp.where(y < 0.0, -value, value)

    def angle_part(place, part, tile):
        at = pl.ds(part * 8, 8)
        total = angle(real[place][at], imag[place][at]) + turns[place][at]
        sums[at] = jnp.where(lanes == tile, jnp.sum(total, axis=1, keepdims=True), sums[at])

    def exact_block(block, tile, place, starts, beside):
        corner = [
            jnp.broadcast_to(panel_ref[block // 4, block % 4, c : c + 1, :], (8, BLK)) for c in range(9)
        ]
        ax, ay, az, bx, by, bz, cx, cy, cz = corner
        ux, uy, uz = bx - ax, by - ay, bz - az
        vx, vy, vz = cx - ax, cy - ay, cz - az
        wx, wy, wz = cx - bx, cy - by, cz - bz
        ux2, uy2, uz2 = ux + ux, uy + uy, uz + uz
        nx = uy2 * vz - uz2 * vy
        ny = uz2 * vx - ux2 * vz
        nz = ux2 * vy - uy2 * vx
        side_ab = ux * ux + uy * uy + uz * uz
        side_bc = wx * wx + wy * wy + wz * wz
        side_ca = vx * vx + vy * vy + vz * vz
        for part in range(TILE // 8):
            at = pl.ds(part * 8, 8)
            beside(part)
            qx, qy, qz = spread[place][0, at], spread[place][1, at], spread[place][2, at]

            def from_point(x, y, z):
                x, y, z = x - qx, y - qy, z - qz
                square = x * x + y * y + z * z
                return x, y, z, square * lax.rsqrt(square)

            px, py, pz, la = from_point(ax, ay, az)
            lb = from_point(bx, by, bz)[3]
            lc = from_point(cx, cy, cz)[3]
            y = px * nx + py * ny + pz * nz
            x = (la + lb) * (lb + lc) * (lc + la) - (side_ab * lc + side_bc * la + side_ca * lb)
            if starts:
                real[place][at], imag[place][at] = x, y
                turns[place][at] = jnp.zeros((8, BLK), jnp.float32)
            else:
                u, v = real[place][at], imag[place][at]
                below = y < 0.0
                r, i = u * x - v * y, u * y + v * x
                same = jnp.logical_not(jnp.logical_xor(v < 0.0, below))
                wrapped = jnp.logical_and(same, jnp.logical_xor(i < 0.0, below))
                turns[place][at] += jnp.where(wrapped, jnp.where(below, -1.0, 1.0), 0.0)
                real[place][at], imag[place][at] = r, i
        row = pl.ds(block, 1)
        field = dipole_field([centres[c, row, :] for c in range(6)], points_ref[tile, 0:3, :])
        minus[pl.ds(tile, 1), :] -= field

    first = widen(tiles[1])
    for part in range(TILE // 8):
        spread_part(1, part, first)
    loads[1].wait()

    def one_tile(index, place):
        tile = tiles[index]
        last, following = tiles[index - 1], tiles[index + 1]
        member, half = tile // 2, tile % 2
        across = widen(following)

        def beside(part):
            angle_part(1 - place, part, last)
            spread_part(1 - place, part, across)

        exact_block(live_ref[member, half, 0], tile, place, True, beside)

        def more(slot, carry):
            @pl.when(slot % 4 == 0)
            def _():
                u, v = real[place][...], imag[place][...]
                factor = 1.0 / (jnp.abs(u) + jnp.abs(v))
                real[place][...], imag[place][...] = u * factor, v * factor

            exact_block(live_ref[member, half, slot], tile, place, False, lambda part: None)
            return carry

        lax.fori_loop(1, live_ref[member, half, PANELS], more, 0)

    def two_tiles(step, carry):
        one_tile(2 * step + 1, 1)

        @pl.when(2 * step + 2 <= found)
        def _():
            one_tile(2 * step + 2, 0)

        return carry

    lax.fori_loop(0, (found + 1) // 2, two_tiles, 0)
    for place in range(2):

        @pl.when(found % 2 == place)
        def _():
            for part in range(TILE // 8):
                angle_part(place, part, tiles[found])

    rows = sums[...].T
    rows = rows[0 : 2 * PANELS, :] + minus[...]
    for member in range(PANELS):
        out_ref[member] = rows[2 * member : 2 * member + 2, :]


def near_call(live, panel, poles, points):
    hbm = pl.BlockSpec(memory_space=pl.ANY)
    f32 = jnp.float32
    return pl.pallas_call(
        near_kernel,
        out_shape=jax.ShapeDtypeStruct((PANELS, 2, TILE), f32),
        in_specs=[hbm] * 4,
        out_specs=pl.BlockSpec(memory_space=pltpu.VMEM),
        scratch_shapes=[
            pltpu.SMEM((PANELS, 2, 128), jnp.int32),
            pltpu.VMEM((PARTS, TURNS, ROWS, BLK), f32),
            pltpu.VMEM((BLOCKS, BLK), f32),
            pltpu.VMEM((PANELS, 8, TILE), f32),
            pltpu.VMEM((2 * PANELS, 8, TILE), f32),
            pltpu.VMEM((PANELS, TILE, 32), jnp.bfloat16),
            pltpu.VMEM((2, 32, 3 * BLK), jnp.bfloat16),
            pltpu.VMEM((6, BLOCKS, TILE), f32),
            pltpu.VMEM((3, TILE, BLK), f32),
            pltpu.VMEM((3, TILE, BLK), f32),
        ]
        + [pltpu.VMEM((TILE, BLK), f32)] * 6
        + [
            pltpu.SMEM((2 * PANELS + 2,), jnp.int32),
            pltpu.VMEM((TILE, BLK), f32),
            pltpu.VMEM((2 * PANELS, TILE), f32),
            pltpu.SemaphoreType.DMA((4,)),
        ],
        compiler_params=pltpu.CompilerParams(vmem_limit_bytes=60 * 1024 * 1024),
        name="near",
    )(live, panel, poles, points)


def reduce_kernel(
    partial_hbm, poles_hbm, points_hbm, out_ref,
    partial, far, poles, points, centres, arrived, load_sems, send_sem, recv_sem,
):
    me = lax.axis_index("owner")
    lane = lax.axis_index("qgrp")
    group = me // TURNS
    member = (me % TURNS) * PAN_TURN + lane
    barrier = pltpu.get_barrier_semaphore()
    loads = [
        pltpu.make_async_copy(source, target, load_sems.at[index])
        for index, (source, target) in enumerate(
            [(partial_hbm, partial), (poles_hbm, poles), (points_hbm, points)]
        )
    ]
    for load in loads:
        load.start()

    def device(step):
        to = (member + step) % PANELS
        return to, (group * TURNS + to // PAN_TURN, to % PAN_TURN)

    def greet(step, carry):
        pl.semaphore_signal(barrier, inc=1, device_id=device(step)[1], device_id_type=MESH)
        return carry

    lax.fori_loop(1, PANELS, greet, 0)
    for load in loads:
        load.wait()
    spread_poles(poles[...], centres)

    def far_field(step, carry):
        for index in range(MEMBERS_STEP):
            one = step * MEMBERS_STEP + index
            for half in range(2):
                field = dipole_field([centres[c] for c in range(6)], points[one, 3 * half : 3 * half + 3, :])
                far[one, half : half + 1, :] = partial[one, half : half + 1, :] + jnp.sum(
                    field, axis=0, keepdims=True
                )
        return carry

    lax.fori_loop(0, PANELS // MEMBERS_STEP, far_field, 0)
    pl.semaphore_wait(barrier, PANELS - 1)

    def send(step, carry):
        to, where = device(step)
        pltpu.make_async_remote_copy(
            src_ref=far.at[to], dst_ref=arrived.at[member], send_sem=send_sem, recv_sem=recv_sem,
            device_id=where, device_id_type=MESH,
        ).start()
        return carry

    lax.fori_loop(1, PANELS, send, 0)
    arrived[member] = far[member]
    part = arrived.at[pl.ds(0, PANELS - 1)]
    pltpu.make_async_copy(part, part, recv_sem).wait()
    out_ref[...] = jnp.sum(arrived[...], axis=0)
    pltpu.make_async_copy(part, part, send_sem).wait()


def on_device(queries, winding_in, triangles, dipoles, plan, near_blocks, near_count):
    vmem = pl.BlockSpec(memory_space=pltpu.VMEM)
    smem = pl.BlockSpec(memory_space=pltpu.SMEM)
    hbm = pl.BlockSpec(memory_space=pl.ANY)
    f32 = jnp.float32
    panel, poles, points, live = pl.pallas_call(
        gather_kernel,
        out_shape=(
            jax.ShapeDtypeStruct((PARTS, TURNS, ROWS, BLK), f32),
            jax.ShapeDtypeStruct((BLOCKS, BLK), f32),
            jax.ShapeDtypeStruct((PANELS, 8, TILE), f32),
            jax.ShapeDtypeStruct((PANELS, 2, 128), jnp.int32),
        ),
        in_specs=[smem, hbm, hbm, hbm, hbm, hbm],
        out_specs=(hbm, hbm, hbm, hbm),
        scratch_shapes=[
            pltpu.VMEM((3, 2 * TILE), f32),
            pltpu.VMEM((9, BLOCKS * BLK), f32),
            pltpu.VMEM((6, BLOCKS), f32),
            pltpu.VMEM((2, NEAR, PANELS), jnp.int32),
            pltpu.VMEM((2, PANELS), jnp.int32),
            pltpu.VMEM((BLOCKS // 2, 2, ROWS, BLK), f32),
            pltpu.VMEM((BLOCKS, ROWS, BLK), f32),
            pltpu.VMEM((BLOCKS // 2, 2, ROWS, BLK), f32),
            pltpu.VMEM((2, TURNS, ROWS, BLK), f32),
            pltpu.VMEM((2, TURNS, ROWS, BLK), f32),
            pltpu.VMEM((TURNS, ROWS, BLK), f32),
            pltpu.VMEM((PARTS, TURNS, ROWS, BLK), f32),
            pltpu.VMEM((8, TILE), f32),
            pltpu.VMEM((PANELS, 8, TILE), f32),
            pltpu.VMEM((BLOCKS, BLK), f32),
            pltpu.VMEM((PANELS, 2, 128), jnp.int32),
            pltpu.SemaphoreType.DMA((5,)),
            pltpu.SemaphoreType.DMA((4,)),
        ]
        + [pltpu.SemaphoreType.DMA] * 9
        + [pltpu.SemaphoreType.REGULAR] * 2,
        compiler_params=pltpu.CompilerParams(collective_id=0, has_side_effects=True),
        name="gather",
    )(plan, queries, triangles, dipoles, near_blocks.transpose(0, 2, 1), near_count)
    partial = near_call(live, panel, poles, points)
    total = pl.pallas_call(
        reduce_kernel,
        out_shape=jax.ShapeDtypeStruct((2, TILE), f32),
        in_specs=[hbm] * 3,
        out_specs=vmem,
        scratch_shapes=[
            pltpu.VMEM((PANELS, 2, TILE), f32),
            pltpu.VMEM((PANELS, 2, TILE), f32),
            pltpu.VMEM((BLOCKS, BLK), f32),
            pltpu.VMEM((PANELS, 8, TILE), f32),
            pltpu.VMEM((6, BLOCKS, TILE), f32),
            pltpu.VMEM((PANELS, 2, TILE), f32),
            pltpu.SemaphoreType.DMA((3,)),
            pltpu.SemaphoreType.DMA,
            pltpu.SemaphoreType.DMA,
        ],
        compiler_params=pltpu.CompilerParams(collective_id=1, has_side_effects=True),
        name="reduce",
    )(partial, poles, points)
    return winding_in + total.reshape(-1)


def solution(mesh):
    return jax.shard_map(
        on_device,
        mesh=mesh,
        in_specs=(
            P(None, ("owner", "qgrp")),
            P(("owner", "qgrp")),
            P(None, ("owner", "qgrp")),
            P(None, ("owner", "qgrp")),
            P(),
            P(("owner", "qgrp"), None, None),
            P(("owner", "qgrp"), None),
        ),
        out_specs=P(("owner", "qgrp")),
        check_vma=False,
    )
```

```python
import functools

import jax
import jax.numpy as jnp
from jax import lax
from jax.experimental import pallas as pl
from jax.experimental.pallas import tpu as pltpu
from jax.sharding import PartitionSpec as P

TILE = 128
BLK = 128
BLOCKS = 32
NEAR = 4
TURNS = 4
PAN_TURN = 4
PANELS = TURNS * PAN_TURN
OWNERS = 64
ROWS = 10
PARTS = 8
MEMBERS_STEP = 2

MESH = pl.DeviceIdType.MESH

pi = 3.141592653589793
four_pi = 4.0 * pi
soften = 0.1

ATAN = (
    0.9999994039535522,
    -0.3332701325416565,
    0.19887319207191467,
    -0.13512171804904938,
    0.08435401320457458,
    -0.03744291514158249,
    0.008006880059838295,
)


def quotient(number, by):
    return number // by if isinstance(number, int) else lax.div(number, jnp.int32(by))


def remainder(number, by):
    return number % by if isinstance(number, int) else lax.rem(number, jnp.int32(by))


def block_of(place):
    kind, part = place % 4, place // 4
    return kind % 2 + (part % 2) * 2 + (kind // 2) * 4 + (part // 2) * 8


def stage_place(slot):
    return (slot // 8) * 8 + (slot % 2) * 4 + (slot // 2) % 4


def far_lanes(lane):
    side = quotient(lane, 2)
    return 3 * (1 - side), 2 - side, side * (5 - lane) + (1 - side) * (1 - lane)


def gather_kernel(
    plan_ref, queries_ref, triangles_ref, dipoles_ref, blocks_ref, count_ref,
    panel_ref, points_ref, live_ref,
    queries, triangles, dipoles, blocks, count,
    stage, gathered, picked, offered, chosen, message, messages, live,
    load_sems, out_sems, send_one, recv_one, send_pick, recv_pick, send_two, recv_two, recv_far, send_msg, recv_msg,
):
    me = lax.axis_index("owner")
    lane = lax.axis_index("qgrp")
    kind = remainder(me, 4)
    side = remainder(quotient(me, 4), 2)
    half = remainder(quotient(me, 8), 2)
    across = quotient(me, 16)
    part = across * 2 + side
    member = kind * PAN_TURN + lane
    squad = across * 4 + kind
    group = me - kind
    mirror = PAN_TURN - 1 - lane
    role = half * lane + (1 - half) * mirror
    first = half == 0
    barrier = pltpu.get_barrier_semaphore()

    loads = [
        pltpu.make_async_copy(source, target, load_sems.at[index])
        for index, (source, target) in enumerate(
            [
                (triangles_ref, triangles), (dipoles_ref, dipoles), (queries_ref, queries),
                (blocks_ref, blocks), (count_ref, count),
            ]
        )
    ]
    for load in loads:
        load.start()

    def greet(owner, to_lane):
        pl.semaphore_signal(barrier, inc=1, device_id=(owner, to_lane), device_id_type=MESH)

    squads = [(dx, dk) for dx in (2, 1, 3, 0) for dk in (2, 3, 1, 0) if (dx, dk) != (0, 0)]
    lanes = far_lanes(lane)

    def comrade(dx, dk):
        to_across, to_kind = remainder(across + dx, 4), remainder(kind + dk, 4)
        return to_across * 4 + to_kind, (to_across * 16 + half * 8 + side * 4 + to_kind, lane)

    @pl.when(first)
    def _():
        for to_side in range(2):
            greet(across * 16 + 8 + to_side * 4 + kind, mirror)
            greet(across * 16 + to_side * 4 + kind, mirror)

    for dx in (2, 1, 3, 0):
        greet(remainder(across + dx, 4) * 16 + half * 8 + (1 - side) * 4 + kind, lane)
    for to_lane in lanes:
        for to_kind in range(4):
            greet(group + to_kind, to_lane)
    for dx, dk in squads:
        greet(*comrade(dx, dk)[1])

    loads[1].wait()
    flipped = jnp.concatenate(
        [jnp.concatenate([dipoles[...], jnp.zeros((2, BLOCKS), jnp.float32)], axis=0),
         jnp.zeros((8, BLK - BLOCKS), jnp.float32)], axis=1
    ).T
    loads[0].wait()
    for slot in range(BLOCKS):
        block = block_of(stage_place(slot))
        stage[slot // 2, slot % 2, 0:9] = triangles[:, block * BLK : (block + 1) * BLK]
        stage[slot // 2, slot % 2, 9:10, 0:8] = flipped[block : block + 1, :]
    for load in loads[2:]:
        load.wait()
    message[0:3] = queries[:, 0:TILE]
    message[3:6] = queries[:, TILE : 2 * TILE]
    for tile in range(2):
        counted = count[tile : tile + 1, :]
        rows = [jnp.where(counted > slot, blocks[tile, slot : slot + 1, :], -1) for slot in range(NEAR)]
        rows.append(jnp.full((1, BLK - PANELS * NEAR), -1, jnp.int32))
        message[6 + tile : 7 + tile] = jnp.concatenate(rows, axis=1).astype(jnp.float32)

    def wait_bytes(part, sem):
        pltpu.make_async_copy(part, part, sem).wait()

    pl.semaphore_wait(barrier, 15 + 4 * (PAN_TURN - 1) + 4 + 2)

    for dx, dk in squads:
        other, where = comrade(dx, dk)
        pltpu.make_async_remote_copy(
            src_ref=stage.at[other], dst_ref=gathered.at[squad], send_sem=send_one, recv_sem=recv_one,
            device_id=where, device_id_type=MESH,
        ).start()

    def send_message(owner, to_lane):
        pltpu.make_async_remote_copy(
            src_ref=message, dst_ref=messages.at[member], send_sem=send_msg, recv_sem=recv_msg,
            device_id=(owner, to_lane), device_id_type=MESH,
        ).start()

    for to_lane in lanes:
        for to_kind in range(4):
            send_message(group + to_kind, to_lane)
    for dk in range(1, 4):
        send_message(group + remainder(kind + dk, 4), lane)
    gathered[squad] = stage[squad]
    messages[member] = message[...]
    wait_bytes(gathered.at[pl.ds(0, 15)], recv_one)
    for turn in range(TURNS):
        owner = plan_ref[turn]
        pair = gathered[quotient(owner, 16) * 4 + remainder(owner, 4)]
        picked[0, turn] = pair[0]
        picked[1, turn] = pair[1]
    for to_side in range(2):
        pltpu.make_async_remote_copy(
            src_ref=picked.at[to_side], dst_ref=offered.at[half * 2 + side], send_sem=send_pick, recv_sem=recv_pick,
            device_id=(across * 16 + to_side * 4 + kind, mirror), device_id_type=MESH,
        ).start()

    @pl.when(first)
    def _():
        wait_bytes(offered, recv_pick)
        for turn in range(TURNS):
            owner = plan_ref[turn]
            squad_of = remainder(quotient(owner, 8), 2) * 2 + remainder(quotient(owner, 4), 2)
            chosen[turn] = offered[squad_of, turn]
        pltpu.make_async_remote_copy(
            src_ref=chosen, dst_ref=chosen, send_sem=send_two, recv_sem=recv_far,
            device_id=(me + 8, mirror), device_id_type=MESH,
        ).start()

    @pl.when(jnp.logical_not(first))
    def _():
        wait_bytes(chosen, recv_far)

    for dx, flip in ((2, 1), (2, 0), (1, 1), (3, 1), (0, 1), (1, 0), (3, 0)):
        to_side = side + flip * (1 - 2 * side)
        pltpu.make_async_remote_copy(
            src_ref=chosen, dst_ref=panel_ref.at[part], send_sem=send_two, recv_sem=recv_two,
            device_id=(remainder(across + dx, 4) * 16 + half * 8 + to_side * 4 + kind, lane), device_id_type=MESH,
        ).start()
    outs = [
        pltpu.make_async_copy(source, target, out_sems.at[index])
        for index, (source, target) in enumerate(
            [(chosen, panel_ref.at[part]), (messages, points_ref), (live, live_ref)]
        )
    ]
    outs[0].start()
    wait_bytes(messages.at[pl.ds(0, PANELS - 1)], recv_msg)
    outs[1].start()

    shape = (PANELS, BLK)
    column = lax.broadcasted_iota(jnp.int32, shape, 1)
    before = (
        lax.broadcasted_iota(jnp.int32, (BLK, BLK), 0) < lax.broadcasted_iota(jnp.int32, (BLK, BLK), 1)
    ).astype(jnp.float32)
    for tile in range(2):
        listed = messages[:, 6 + tile, :].astype(jnp.int32)
        held = (listed % 2) + ((listed // 4) % 2) * 2 == kind
        held = jnp.logical_and(held, column % PAN_TURN == role)
        held = jnp.logical_and(held, jnp.logical_and(listed >= 0, column < PANELS * NEAR))
        value = ((listed // 2) % 2 + (listed // 8) * 2) * 4 + (column % PANELS) // PAN_TURN
        value = value.astype(jnp.float32)
        flags = jnp.where(held, 1.0, 0.0)
        rank = lax.dot_general(flags, before, (((1,), (0,)), ((), ())), preferred_element_type=jnp.float32)
        rank = jnp.where(held, rank, -1.0)
        packed = jnp.where(column == PANELS, jnp.sum(flags, axis=1, keepdims=True), 0.0)
        for index in range(PANELS):
            one = jnp.sum(jnp.where(jnp.abs(rank - index) < 0.5, value, 0.0), axis=1, keepdims=True)
            packed = jnp.where(column == index, one, packed)
        live[:, tile, :] = packed.astype(jnp.int32)
    outs[2].start()

    wait_bytes(stage.at[pl.ds(0, 15)], send_one)
    wait_bytes(picked, send_pick)
    wait_bytes(messages.at[pl.ds(0, PANELS - 1)], send_msg)

    @pl.when(first)
    def _():
        wait_bytes(panel_ref, send_two)

    @pl.when(jnp.logical_not(first))
    def _():
        wait_bytes(panel_ref.at[pl.ds(0, PARTS - 1)], send_two)

    for out in outs:
        out.wait()
    wait_bytes(panel_ref.at[pl.ds(0, PARTS - 1)], recv_two)


def dipole_field(centre, points):
    offset = [centre[c] - jnp.broadcast_to(points[c : c + 1, :], centre[c].shape) for c in range(3)]
    square = offset[0] * offset[0] + offset[1] * offset[1] + offset[2] * offset[2] + soften
    inverse = lax.rsqrt(square)
    return (centre[3] * offset[0] + centre[4] * offset[1] + centre[5] * offset[2]) * (
        inverse * inverse * inverse
    )


def spread_poles(poles, centres):
    rows = jnp.concatenate([poles[slot // 4, slot % 4] for slot in range(BLOCKS)], axis=0)
    for component in range(6):
        value = jnp.broadcast_to(rows[:, component : component + 1], (BLOCKS, TILE))
        if component >= 3:
            value = value * (1.0 / four_pi)
        centres[component] = value


def near_kernel(
    live_hbm, panel_hbm, points_hbm, out_ref,
    live_ref, panel_ref, poles_ref, given, points_ref, flipped, picker, centres,
    spread_0, spread_1, real_0, real_1, imag_0, imag_1, turns_0, turns_1, tiles, sums, minus, sems
):
    spread, real, imag, turns = (spread_0, spread_1), (real_0, real_1), (imag_0, imag_1), (turns_0, turns_1)
    loads = [
        pltpu.make_async_copy(source, target, sems.at[index])
        for index, (source, target) in enumerate(
            [(live_hbm, live_ref), (panel_hbm, panel_ref), (panel_hbm.at[:, :, pl.ds(9, 1), :], poles_ref), (points_hbm, given)]
        )
    ]
    for load in loads:
        load.start()
    minus[...] = jnp.zeros_like(minus)
    sums[...] = jnp.zeros_like(sums)
    real_0[...] = jnp.ones_like(real_0)
    imag_0[...] = jnp.zeros_like(imag_0)
    turns_0[...] = jnp.zeros_like(turns_0)
    loads[2].wait()
    spread_poles(poles_ref, centres)
    loads[3].wait()
    for member in range(PANELS):
        for half in range(2):
            points_ref[2 * member + half, 0:3] = given[member, 3 * half : 3 * half + 3]
    loads[0].wait()

    tiles[0] = 2 * PANELS
    found = jnp.int32(0)
    for tile in range(2 * PANELS):
        tiles[found + 1] = tile
        found = found + jnp.where(live_ref[tile // 2, tile % 2, PANELS] > 0, 1, 0)
    tiles[found + 1] = 0
    lanes = lax.broadcasted_iota(jnp.int32, (8, BLK), 1)

    for member in range(PANELS):
        rest = given[member]
        parts = []
        for _ in range(3):
            parts.append(rest.astype(jnp.bfloat16).astype(jnp.float32))
            rest = rest - parts[-1]
        parts.append(jnp.zeros_like(rest))
        flipped[member] = jnp.concatenate(parts, axis=0).T.astype(jnp.bfloat16)
    shape = (32, 3 * BLK)
    entry = lax.broadcasted_iota(jnp.int32, shape, 0)
    component = lax.broadcasted_iota(jnp.int32, shape, 1) // BLK
    for half in range(2):
        wanted = jnp.logical_and(entry % 8 == 3 * half + component, entry < 24)
        picker[half] = jnp.where(wanted, 1.0, 0.0).astype(jnp.bfloat16)

    def widen(tile):
        return lax.dot_general(
            flipped[tile // 2], picker[tile % 2], (((1,), (0,)), ((), ())), preferred_element_type=jnp.float32
        )

    def spread_part(place, part, wide):
        at = pl.ds(part * 8, 8)
        for c in range(3):
            spread[place][c, at] = wide[part * 8 : part * 8 + 8, c * BLK : (c + 1) * BLK]

    def angle(x, y):
        ax, ay = jnp.abs(x), jnp.abs(y)
        t = jnp.minimum(ax, ay) * pl.reciprocal(jnp.maximum(ax, ay), approx=True)
        square = t * t
        value = jnp.full_like(t, ATAN[-1] * 0.5 / pi)
        for coefficient in ATAN[-2::-1]:
            value = value * square + coefficient * 0.5 / pi
        value = value * t
        value = jnp.where(ay > ax, 0.25 - value, value)
        value = jnp.where(x < 0.0, 0.5 - value, value)
        return jnp.where(y < 0.0, -value, value)

    def angle_part(place, part, tile):
        at = pl.ds(part * 8, 8)
        total = angle(real[place][at], imag[place][at]) + turns[place][at]
        sums[at] = jnp.where(lanes == tile, jnp.sum(total, axis=1, keepdims=True), sums[at])

    def exact_block(block, tile, place, starts, beside):
        corner = [
            jnp.broadcast_to(panel_ref[block // 4, block % 4, c : c + 1, :], (8, BLK)) for c in range(9)
        ]
        ax, ay, az, bx, by, bz, cx, cy, cz = corner
        ux, uy, uz = bx - ax, by - ay, bz - az
        vx, vy, vz = cx - ax, cy - ay, cz - az
        wx, wy, wz = cx - bx, cy - by, cz - bz
        ux2, uy2, uz2 = ux + ux, uy + uy, uz + uz
        nx = uy2 * vz - uz2 * vy
        ny = uz2 * vx - ux2 * vz
        nz = ux2 * vy - uy2 * vx
        side_ab = ux * ux + uy * uy + uz * uz
        side_bc = wx * wx + wy * wy + wz * wz
        side_ca = vx * vx + vy * vy + vz * vz
        for part in range(TILE // 8):
            at = pl.ds(part * 8, 8)
            beside(part)
            qx, qy, qz = spread[place][0, at], spread[place][1, at], spread[place][2, at]

            def from_point(x, y, z):
                x, y, z = x - qx, y - qy, z - qz
                square = x * x + y * y + z * z
                return x, y, z, square * lax.rsqrt(square)

            px, py, pz, la = from_point(ax, ay, az)
            lb = from_point(bx, by, bz)[3]
            lc = from_point(cx, cy, cz)[3]
            y = px * nx + py * ny + pz * nz
            x = (la + lb) * (lb + lc) * (lc + la) - (side_ab * lc + side_bc * la + side_ca * lb)
            if starts:
                real[place][at], imag[place][at] = x, y
                turns[place][at] = jnp.zeros((8, BLK), jnp.float32)
            else:
                u, v = real[place][at], imag[place][at]
                below = y < 0.0
                r, i = u * x - v * y, u * y + v * x
                same = jnp.logical_not(jnp.logical_xor(v < 0.0, below))
                wrapped = jnp.logical_and(same, jnp.logical_xor(i < 0.0, below))
                turns[place][at] += jnp.where(wrapped, jnp.where(below, -1.0, 1.0), 0.0)
                real[place][at], imag[place][at] = r, i
        row = pl.ds(block, 1)
        field = dipole_field([centres[c, row, :] for c in range(6)], points_ref[tile, 0:3, :])
        minus[pl.ds(tile, 1), :] -= field

    first = widen(tiles[1])
    for part in range(TILE // 8):
        spread_part(1, part, first)
    loads[1].wait()

    def one_tile(index, place):
        tile = tiles[index]
        last, following = tiles[index - 1], tiles[index + 1]
        member, half = tile // 2, tile % 2
        across = widen(following)

        def beside(part):
            angle_part(1 - place, part, last)
            spread_part(1 - place, part, across)

        exact_block(live_ref[member, half, 0], tile, place, True, beside)

        def more(slot, carry):
            @pl.when(slot % 4 == 0)
            def _():
                u, v = real[place][...], imag[place][...]
                factor = 1.0 / (jnp.abs(u) + jnp.abs(v))
                real[place][...], imag[place][...] = u * factor, v * factor

            exact_block(live_ref[member, half, slot], tile, place, False, lambda part: None)
            return carry

        lax.fori_loop(1, live_ref[member, half, PANELS], more, 0)

    def two_tiles(step, carry):
        one_tile(2 * step + 1, 1)

        @pl.when(2 * step + 2 <= found)
        def _():
            one_tile(2 * step + 2, 0)

        return carry

    lax.fori_loop(0, (found + 1) // 2, two_tiles, 0)
    for place in range(2):

        @pl.when(found % 2 == place)
        def _():
            for part in range(TILE // 8):
                angle_part(place, part, tiles[found])

    rows = sums[...].T
    rows = rows[0 : 2 * PANELS, :] + minus[...]
    for member in range(PANELS):
        out_ref[member] = rows[2 * member : 2 * member + 2, :]


def near_call(live, panel, points):
    hbm = pl.BlockSpec(memory_space=pl.ANY)
    f32 = jnp.float32
    return pl.pallas_call(
        near_kernel,
        out_shape=jax.ShapeDtypeStruct((PANELS, 2, TILE), f32),
        in_specs=[hbm] * 3,
        out_specs=pl.BlockSpec(memory_space=pltpu.VMEM),
        scratch_shapes=[
            pltpu.SMEM((PANELS, 2, 128), jnp.int32),
            pltpu.VMEM((PARTS, TURNS, ROWS, BLK), f32),
            pltpu.VMEM((PARTS, TURNS, 1, BLK), f32),
            pltpu.VMEM((PANELS, 8, TILE), f32),
            pltpu.VMEM((2 * PANELS, 8, TILE), f32),
            pltpu.VMEM((PANELS, TILE, 32), jnp.bfloat16),
            pltpu.VMEM((2, 32, 3 * BLK), jnp.bfloat16),
            pltpu.VMEM((6, BLOCKS, TILE), f32),
            pltpu.VMEM((3, TILE, BLK), f32),
            pltpu.VMEM((3, TILE, BLK), f32),
        ]
        + [pltpu.VMEM((TILE, BLK), f32)] * 6
        + [
            pltpu.SMEM((2 * PANELS + 2,), jnp.int32),
            pltpu.VMEM((TILE, BLK), f32),
            pltpu.VMEM((2 * PANELS, TILE), f32),
            pltpu.SemaphoreType.DMA((4,)),
        ],
        compiler_params=pltpu.CompilerParams(vmem_limit_bytes=60 * 1024 * 1024),
        name="near",
    )(live, panel, points)


def reduce_kernel(
    partial_hbm, panel_hbm, points_hbm, out_ref,
    partial, far, poles, points, centres, arrived, load_sems, send_sem, recv_sem,
):
    me = lax.axis_index("owner")
    lane = lax.axis_index("qgrp")
    kind = remainder(me, 4)
    group = me - kind
    member = kind * PAN_TURN + lane
    partners = [(to_kind, to_lane) for to_lane in far_lanes(lane) for to_kind in range(4)]
    partners += [(remainder(kind + dk, 4), lane) for dk in range(1, 4)]
    barrier = pltpu.get_barrier_semaphore()
    loads = [
        pltpu.make_async_copy(source, target, load_sems.at[index])
        for index, (source, target) in enumerate(
            [(partial_hbm, partial), (panel_hbm.at[:, :, pl.ds(9, 1), :], poles), (points_hbm, points)]
        )
    ]
    for load in loads:
        load.start()

    for to_kind, to_lane in partners:
        pl.semaphore_signal(barrier, inc=1, device_id=(group + to_kind, to_lane), device_id_type=MESH)
    for load in loads:
        load.wait()
    spread_poles(poles, centres)

    def far_field(step, carry):
        for index in range(MEMBERS_STEP):
            one = step * MEMBERS_STEP + index
            for half in range(2):
                field = dipole_field([centres[c] for c in range(6)], points[one, 3 * half : 3 * half + 3, :])
                far[one, half : half + 1, :] = partial[one, half : half + 1, :] + jnp.sum(
                    field, axis=0, keepdims=True
                )
        return carry

    lax.fori_loop(0, PANELS // MEMBERS_STEP, far_field, 0)
    pl.semaphore_wait(barrier, PANELS - 1)

    for to_kind, to_lane in partners:
        pltpu.make_async_remote_copy(
            src_ref=far.at[to_kind * PAN_TURN + to_lane], dst_ref=arrived.at[member],
            send_sem=send_sem, recv_sem=recv_sem, device_id=(group + to_kind, to_lane), device_id_type=MESH,
        ).start()
    arrived[member] = far[member]
    part = arrived.at[pl.ds(0, PANELS - 1)]
    pltpu.make_async_copy(part, part, recv_sem).wait()
    out_ref[...] = jnp.sum(arrived[...], axis=0)
    pltpu.make_async_copy(part, part, send_sem).wait()


def on_device(queries, winding_in, triangles, dipoles, plan, near_blocks, near_count):
    vmem = pl.BlockSpec(memory_space=pltpu.VMEM)
    smem = pl.BlockSpec(memory_space=pltpu.SMEM)
    hbm = pl.BlockSpec(memory_space=pl.ANY)
    f32 = jnp.float32
    panel, points, live = pl.pallas_call(
        gather_kernel,
        out_shape=(
            jax.ShapeDtypeStruct((PARTS, TURNS, ROWS, BLK), f32),
            jax.ShapeDtypeStruct((PANELS, 8, TILE), f32),
            jax.ShapeDtypeStruct((PANELS, 2, 128), jnp.int32),
        ),
        in_specs=[smem, hbm, hbm, hbm, hbm, hbm],
        out_specs=(hbm, hbm, hbm),
        scratch_shapes=[
            pltpu.VMEM((3, 2 * TILE), f32),
            pltpu.VMEM((9, BLOCKS * BLK), f32),
            pltpu.VMEM((6, BLOCKS), f32),
            pltpu.VMEM((2, NEAR, PANELS), jnp.int32),
            pltpu.VMEM((2, PANELS), jnp.int32),
            pltpu.VMEM((16, 2, ROWS, BLK), f32),
            pltpu.VMEM((16, 2, ROWS, BLK), f32),
            pltpu.VMEM((2, TURNS, ROWS, BLK), f32),
            pltpu.VMEM((4, TURNS, ROWS, BLK), f32),
            pltpu.VMEM((TURNS, ROWS, BLK), f32),
            pltpu.VMEM((8, TILE), f32),
            pltpu.VMEM((PANELS, 8, TILE), f32),
            pltpu.VMEM((PANELS, 2, 128), jnp.int32),
            pltpu.SemaphoreType.DMA((5,)),
            pltpu.SemaphoreType.DMA((3,)),
        ]
        + [pltpu.SemaphoreType.DMA] * 9,
        compiler_params=pltpu.CompilerParams(collective_id=0, has_side_effects=True),
        name="gather",
    )(plan, queries, triangles, dipoles, near_blocks.transpose(0, 2, 1), near_count)
    partial = near_call(live, panel, points)
    total = pl.pallas_call(
        reduce_kernel,
        out_shape=jax.ShapeDtypeStruct((2, TILE), f32),
        in_specs=[hbm] * 3,
        out_specs=vmem,
        scratch_shapes=[
            pltpu.VMEM((PANELS, 2, TILE), f32),
            pltpu.VMEM((PANELS, 2, TILE), f32),
            pltpu.VMEM((PARTS, TURNS, 1, BLK), f32),
            pltpu.VMEM((PANELS, 8, TILE), f32),
            pltpu.VMEM((6, BLOCKS, TILE), f32),
            pltpu.VMEM((PANELS, 2, TILE), f32),
            pltpu.SemaphoreType.DMA((3,)),
            pltpu.SemaphoreType.DMA,
            pltpu.SemaphoreType.DMA,
        ],
        compiler_params=pltpu.CompilerParams(collective_id=1, has_side_effects=True),
        name="reduce",
    )(partial, panel, points)
    return winding_in + total.reshape(-1)


def solution(mesh):
    return jax.shard_map(
        on_device,
        mesh=mesh,
        in_specs=(
            P(None, ("owner", "qgrp")),
            P(("owner", "qgrp")),
            P(None, ("owner", "qgrp")),
            P(None, ("owner", "qgrp")),
            P(),
            P(("owner", "qgrp"), None, None),
            P(("owner", "qgrp"), None),
        ),
        out_specs=P(("owner", "qgrp")),
        check_vma=False,
    )
```

```python
import functools

import jax
import jax.numpy as jnp
from jax import lax
from jax.experimental import pallas as pl
from jax.experimental.pallas import tpu as pltpu
from jax.sharding import PartitionSpec as P

TILE = 128
BLK = 128
BLOCKS = 32
NEAR = 4
TURNS = 4
PAN_TURN = 4
PANELS = TURNS * PAN_TURN
OWNERS = 64
ROWS = 10
PARTS = 8
MEMBERS_STEP = 2
VMEM_LIMIT = 16 * 1024 * 1024

MESH = pl.DeviceIdType.MESH

pi = 3.141592653589793
four_pi = 4.0 * pi
soften = 0.1

ATAN = (
    0.9999994039535522,
    -0.3332701325416565,
    0.19887319207191467,
    -0.13512171804904938,
    0.08435401320457458,
    -0.03744291514158249,
    0.008006880059838295,
)


def quotient(number, by):
    return number // by if isinstance(number, int) else lax.div(number, jnp.int32(by))


def remainder(number, by):
    return number % by if isinstance(number, int) else lax.rem(number, jnp.int32(by))


def block_of(place):
    kind, part = place % 4, place // 4
    return kind % 2 + (part % 2) * 2 + (kind // 2) * 4 + (part // 2) * 8


def stage_place(slot):
    return (slot // 8) * 8 + (slot % 2) * 4 + (slot // 2) % 4


def far_lanes(lane):
    side = quotient(lane, 2)
    return 3 * (1 - side), 2 - side, side * (5 - lane) + (1 - side) * (1 - lane)


def gather_kernel(
    plan_ref, queries_ref, triangles_ref, dipoles_ref, blocks_ref, count_ref,
    panel_ref, points_ref, live_ref,
    queries, triangles, dipoles, blocks, count, turn_owner,
    stage, gathered, picked, offered, chosen, message, messages, live,
    load_sems, out_sems, send_one, recv_one, send_pick, recv_pick, send_two, recv_two, recv_far, send_msg, recv_msg,
):
    me = lax.axis_index("owner")
    lane = lax.axis_index("qgrp")
    kind = remainder(me, 4)
    side = remainder(quotient(me, 4), 2)
    half = remainder(quotient(me, 8), 2)
    across = quotient(me, 16)
    part = across * 2 + side
    member = kind * PAN_TURN + lane
    squad = across * 4 + kind
    group = me - kind
    mirror = PAN_TURN - 1 - lane
    role = half * lane + (1 - half) * mirror
    first = half == 0
    barrier = pltpu.get_barrier_semaphore()

    loads = [
        pltpu.make_async_copy(source, target, load_sems.at[index])
        for index, (source, target) in enumerate(
            [
                (triangles_ref, triangles), (dipoles_ref, dipoles), (queries_ref, queries),
                (blocks_ref, blocks), (count_ref, count), (plan_ref, turn_owner),
            ]
        )
    ]
    for load in loads:
        load.start()

    def greet(owner, to_lane):
        pl.semaphore_signal(barrier, inc=1, device_id=(owner, to_lane), device_id_type=MESH)

    squads = [(dx, dk) for dx in (2, 1, 3, 0) for dk in (2, 3, 1, 0) if (dx, dk) != (0, 0)]
    lanes = far_lanes(lane)

    def comrade(dx, dk):
        to_across, to_kind = remainder(across + dx, 4), remainder(kind + dk, 4)
        return to_across * 4 + to_kind, (to_across * 16 + half * 8 + side * 4 + to_kind, lane)

    @pl.when(first)
    def _():
        for to_side in range(2):
            greet(across * 16 + 8 + to_side * 4 + kind, mirror)
            greet(across * 16 + to_side * 4 + kind, mirror)

    for dx in (2, 1, 3, 0):
        greet(remainder(across + dx, 4) * 16 + half * 8 + (1 - side) * 4 + kind, lane)
    for to_lane in lanes:
        for to_kind in range(4):
            greet(group + to_kind, to_lane)
    for dx, dk in squads:
        greet(*comrade(dx, dk)[1])

    loads[1].wait()
    flipped = jnp.concatenate(
        [jnp.concatenate([dipoles[...], jnp.zeros((2, BLOCKS), jnp.float32)], axis=0),
         jnp.zeros((8, BLK - BLOCKS), jnp.float32)], axis=1
    ).T
    loads[0].wait()
    for slot in range(BLOCKS):
        block = block_of(stage_place(slot))
        stage[slot // 2, slot % 2, 0:9] = triangles[:, block * BLK : (block + 1) * BLK]
        stage[slot // 2, slot % 2, 9:10, 0:8] = flipped[block : block + 1, :]
    for load in loads[2:]:
        load.wait()
    message[0:3] = queries[:, 0:TILE]
    message[3:6] = queries[:, TILE : 2 * TILE]
    for tile in range(2):
        counted = count[tile : tile + 1, :]
        rows = [jnp.where(counted > slot, blocks[tile, slot : slot + 1, :], -1) for slot in range(NEAR)]
        rows.append(jnp.full((1, BLK - PANELS * NEAR), -1, jnp.int32))
        message[6 + tile : 7 + tile] = jnp.concatenate(rows, axis=1).astype(jnp.float32)

    def wait_bytes(part, sem):
        pltpu.make_async_copy(part, part, sem).wait()

    pl.semaphore_wait(barrier, 15 + 4 * (PAN_TURN - 1) + 4 + 2)

    for dx, dk in squads:
        other, where = comrade(dx, dk)
        pltpu.make_async_remote_copy(
            src_ref=stage.at[other], dst_ref=gathered.at[squad], send_sem=send_one, recv_sem=recv_one,
            device_id=where, device_id_type=MESH,
        ).start()

    def send_message(owner, to_lane):
        pltpu.make_async_remote_copy(
            src_ref=message, dst_ref=messages.at[member], send_sem=send_msg, recv_sem=recv_msg,
            device_id=(owner, to_lane), device_id_type=MESH,
        ).start()

    for to_lane in lanes:
        for to_kind in range(4):
            send_message(group + to_kind, to_lane)
    for dk in range(1, 4):
        send_message(group + remainder(kind + dk, 4), lane)
    gathered[squad] = stage[squad]
    messages[member] = message[...]
    wait_bytes(gathered.at[pl.ds(0, 15)], recv_one)
    for turn in range(TURNS):
        owner = turn_owner[turn]
        pair = gathered[quotient(owner, 16) * 4 + remainder(owner, 4)]
        picked[0, turn] = pair[0]
        picked[1, turn] = pair[1]
    for to_side in range(2):
        pltpu.make_async_remote_copy(
            src_ref=picked.at[to_side], dst_ref=offered.at[half * 2 + side], send_sem=send_pick, recv_sem=recv_pick,
            device_id=(across * 16 + to_side * 4 + kind, mirror), device_id_type=MESH,
        ).start()

    @pl.when(first)
    def _():
        wait_bytes(offered, recv_pick)
        for turn in range(TURNS):
            owner = turn_owner[turn]
            squad_of = remainder(quotient(owner, 8), 2) * 2 + remainder(quotient(owner, 4), 2)
            chosen[turn] = offered[squad_of, turn]
        pltpu.make_async_remote_copy(
            src_ref=chosen, dst_ref=chosen, send_sem=send_two, recv_sem=recv_far,
            device_id=(me + 8, mirror), device_id_type=MESH,
        ).start()

    @pl.when(jnp.logical_not(first))
    def _():
        wait_bytes(chosen, recv_far)

    for dx, flip in ((2, 1), (2, 0), (1, 1), (3, 1), (0, 1), (1, 0), (3, 0)):
        to_side = side + flip * (1 - 2 * side)
        pltpu.make_async_remote_copy(
            src_ref=chosen, dst_ref=panel_ref.at[part], send_sem=send_two, recv_sem=recv_two,
            device_id=(remainder(across + dx, 4) * 16 + half * 8 + to_side * 4 + kind, lane), device_id_type=MESH,
        ).start()
    outs = [
        pltpu.make_async_copy(source, target, out_sems.at[index])
        for index, (source, target) in enumerate(
            [(chosen, panel_ref.at[part]), (messages, points_ref), (live, live_ref)]
        )
    ]
    outs[0].start()
    wait_bytes(messages.at[pl.ds(0, PANELS - 1)], recv_msg)
    outs[1].start()

    shape = (PANELS, BLK)
    column = lax.broadcasted_iota(jnp.int32, shape, 1)
    before = (
        lax.broadcasted_iota(jnp.int32, (BLK, BLK), 0) < lax.broadcasted_iota(jnp.int32, (BLK, BLK), 1)
    ).astype(jnp.float32)
    for tile in range(2):
        listed = messages[:, 6 + tile, :].astype(jnp.int32)
        held = (listed % 2) + ((listed // 4) % 2) * 2 == kind
        held = jnp.logical_and(held, column % PAN_TURN == role)
        held = jnp.logical_and(held, jnp.logical_and(listed >= 0, column < PANELS * NEAR))
        value = ((listed // 2) % 2 + (listed // 8) * 2) * 4 + (column % PANELS) // PAN_TURN
        value = value.astype(jnp.float32)
        flags = jnp.where(held, 1.0, 0.0)
        rank = lax.dot_general(flags, before, (((1,), (0,)), ((), ())), preferred_element_type=jnp.float32)
        rank = jnp.where(held, rank, -1.0)
        packed = jnp.where(column == PANELS, jnp.sum(flags, axis=1, keepdims=True), 0.0)
        for index in range(PANELS):
            one = jnp.sum(jnp.where(jnp.abs(rank - index) < 0.5, value, 0.0), axis=1, keepdims=True)
            packed = jnp.where(column == index, one, packed)
        live[:, tile, :] = packed.astype(jnp.int32)
    outs[2].start()

    wait_bytes(stage.at[pl.ds(0, 15)], send_one)
    wait_bytes(picked, send_pick)
    wait_bytes(messages.at[pl.ds(0, PANELS - 1)], send_msg)

    @pl.when(first)
    def _():
        wait_bytes(panel_ref, send_two)

    @pl.when(jnp.logical_not(first))
    def _():
        wait_bytes(panel_ref.at[pl.ds(0, PARTS - 1)], send_two)

    for out in outs:
        out.wait()
    wait_bytes(panel_ref.at[pl.ds(0, PARTS - 1)], recv_two)


def dipole_field(centre, points):
    offset = [centre[c] - jnp.broadcast_to(points[c : c + 1, :], centre[c].shape) for c in range(3)]
    square = offset[0] * offset[0] + offset[1] * offset[1] + offset[2] * offset[2] + soften
    inverse = lax.rsqrt(square)
    return (centre[3] * offset[0] + centre[4] * offset[1] + centre[5] * offset[2]) * (
        inverse * inverse * inverse
    )


def spread_poles(panel, centres):
    rows = jnp.concatenate([panel[slot // 4, slot % 4, 9:10, :] for slot in range(BLOCKS)], axis=0)
    for component in range(6):
        value = jnp.broadcast_to(rows[:, component : component + 1], (BLOCKS, TILE))
        if component >= 3:
            value = value * (1.0 / four_pi)
        centres[component] = value


def near_kernel(
    live_hbm, panel_ref, given, out_ref,
    live_ref, points_ref, flipped, picker, centres,
    spread_0, spread_1, real_0, real_1, imag_0, imag_1, turns_0, turns_1, tiles, sums, minus, sem
):
    spread, real, imag, turns = (spread_0, spread_1), (real_0, real_1), (imag_0, imag_1), (turns_0, turns_1)
    load = pltpu.make_async_copy(live_hbm, live_ref, sem)
    load.start()
    minus[...] = jnp.zeros_like(minus)
    sums[...] = jnp.zeros_like(sums)
    real_0[...] = jnp.ones_like(real_0)
    imag_0[...] = jnp.zeros_like(imag_0)
    turns_0[...] = jnp.zeros_like(turns_0)
    spread_poles(panel_ref, centres)
    for member in range(PANELS):
        for half in range(2):
            points_ref[2 * member + half, 0:3] = given[member, 3 * half : 3 * half + 3]
    load.wait()
    tiles[0] = 2 * PANELS
    found = jnp.int32(0)
    for tile in range(2 * PANELS):
        tiles[found + 1] = tile
        found = found + jnp.where(live_ref[tile // 2, tile % 2, PANELS] > 0, 1, 0)
    tiles[found + 1] = 0
    lanes = lax.broadcasted_iota(jnp.int32, (8, BLK), 1)

    for member in range(PANELS):
        rest = given[member]
        parts = []
        for _ in range(3):
            parts.append(rest.astype(jnp.bfloat16).astype(jnp.float32))
            rest = rest - parts[-1]
        parts.append(jnp.zeros_like(rest))
        flipped[member] = jnp.concatenate(parts, axis=0).T.astype(jnp.bfloat16)
    shape = (32, 3 * BLK)
    entry = lax.broadcasted_iota(jnp.int32, shape, 0)
    component = lax.broadcasted_iota(jnp.int32, shape, 1) // BLK
    for half in range(2):
        wanted = jnp.logical_and(entry % 8 == 3 * half + component, entry < 24)
        picker[half] = jnp.where(wanted, 1.0, 0.0).astype(jnp.bfloat16)

    def widen(tile):
        return lax.dot_general(
            flipped[tile // 2], picker[tile % 2], (((1,), (0,)), ((), ())), preferred_element_type=jnp.float32
        )

    def spread_part(place, part, wide):
        at = pl.ds(part * 8, 8)
        for c in range(3):
            spread[place][c, at] = wide[part * 8 : part * 8 + 8, c * BLK : (c + 1) * BLK]

    def angle(x, y):
        ax, ay = jnp.abs(x), jnp.abs(y)
        t = jnp.minimum(ax, ay) * pl.reciprocal(jnp.maximum(ax, ay), approx=True)
        square = t * t
        value = jnp.full_like(t, ATAN[-1] * 0.5 / pi)
        for coefficient in ATAN[-2::-1]:
            value = value * square + coefficient * 0.5 / pi
        value = value * t
        value = jnp.where(ay > ax, 0.25 - value, value)
        value = jnp.where(x < 0.0, 0.5 - value, value)
        return jnp.where(y < 0.0, -value, value)

    def angle_part(place, part, tile):
        at = pl.ds(part * 8, 8)
        total = angle(real[place][at], imag[place][at]) + turns[place][at]
        sums[at] = jnp.where(lanes == tile, jnp.sum(total, axis=1, keepdims=True), sums[at])

    def exact_block(block, tile, place, starts, beside):
        corner = [
            jnp.broadcast_to(panel_ref[block // 4, block % 4, c : c + 1, :], (8, BLK)) for c in range(9)
        ]
        ax, ay, az, bx, by, bz, cx, cy, cz = corner
        ux, uy, uz = bx - ax, by - ay, bz - az
        vx, vy, vz = cx - ax, cy - ay, cz - az
        wx, wy, wz = cx - bx, cy - by, cz - bz
        ux2, uy2, uz2 = ux + ux, uy + uy, uz + uz
        nx = uy2 * vz - uz2 * vy
        ny = uz2 * vx - ux2 * vz
        nz = ux2 * vy - uy2 * vx
        side_ab = ux * ux + uy * uy + uz * uz
        side_bc = wx * wx + wy * wy + wz * wz
        side_ca = vx * vx + vy * vy + vz * vz
        for part in range(TILE // 8):
            at = pl.ds(part * 8, 8)
            beside(part)
            qx, qy, qz = spread[place][0, at], spread[place][1, at], spread[place][2, at]

            def from_point(x, y, z):
                x, y, z = x - qx, y - qy, z - qz
                square = x * x + y * y + z * z
                return x, y, z, square * lax.rsqrt(square)

            px, py, pz, la = from_point(ax, ay, az)
            lb = from_point(bx, by, bz)[3]
            lc = from_point(cx, cy, cz)[3]
            y = px * nx + py * ny + pz * nz
            x = (la + lb) * (lb + lc) * (lc + la) - (side_ab * lc + side_bc * la + side_ca * lb)
            if starts:
                real[place][at], imag[place][at] = x, y
                turns[place][at] = jnp.zeros((8, BLK), jnp.float32)
            else:
                u, v = real[place][at], imag[place][at]
                below = y < 0.0
                r, i = u * x - v * y, u * y + v * x
                same = jnp.logical_not(jnp.logical_xor(v < 0.0, below))
                wrapped = jnp.logical_and(same, jnp.logical_xor(i < 0.0, below))
                turns[place][at] += jnp.where(wrapped, jnp.where(below, -1.0, 1.0), 0.0)
                real[place][at], imag[place][at] = r, i
        row = pl.ds(block, 1)
        field = dipole_field([centres[c, row, :] for c in range(6)], points_ref[tile, 0:3, :])
        minus[pl.ds(tile, 1), :] -= field

    first = widen(tiles[1])
    for part in range(TILE // 8):
        spread_part(1, part, first)

    def one_tile(index, place):
        tile = tiles[index]
        last, following = tiles[index - 1], tiles[index + 1]
        member, half = tile // 2, tile % 2
        across = widen(following)

        def beside(part):
            angle_part(1 - place, part, last)
            spread_part(1 - place, part, across)

        exact_block(live_ref[member, half, 0], tile, place, True, beside)

        def more(slot, carry):
            @pl.when(slot % 4 == 0)
            def _():
                u, v = real[place][...], imag[place][...]
                factor = 1.0 / (jnp.abs(u) + jnp.abs(v))
                real[place][...], imag[place][...] = u * factor, v * factor

            exact_block(live_ref[member, half, slot], tile, place, False, lambda part: None)
            return carry

        lax.fori_loop(1, live_ref[member, half, PANELS], more, 0)

    def two_tiles(step, carry):
        one_tile(2 * step + 1, 1)

        @pl.when(2 * step + 2 <= found)
        def _():
            one_tile(2 * step + 2, 0)

        return carry

    lax.fori_loop(0, (found + 1) // 2, two_tiles, 0)
    for place in range(2):

        @pl.when(found % 2 == place)
        def _():
            for part in range(TILE // 8):
                angle_part(place, part, tiles[found])

    rows = sums[...].T
    rows = rows[0 : 2 * PANELS, :] + minus[...]
    for member in range(PANELS):
        out_ref[member] = rows[2 * member : 2 * member + 2, :]


def near_call(live, panel, points):
    hbm = pl.BlockSpec(memory_space=pl.ANY)
    vmem = pl.BlockSpec(memory_space=pltpu.VMEM)
    f32 = jnp.float32
    return pl.pallas_call(
        near_kernel,
        out_shape=jax.ShapeDtypeStruct((PANELS, 2, TILE), f32),
        in_specs=[hbm, vmem, vmem],
        out_specs=vmem,
        scratch_shapes=[
            pltpu.SMEM((PANELS, 2, 128), jnp.int32),
            pltpu.VMEM((2 * PANELS, 8, TILE), f32),
            pltpu.VMEM((PANELS, TILE, 32), jnp.bfloat16),
            pltpu.VMEM((2, 32, 3 * BLK), jnp.bfloat16),
            pltpu.VMEM((6, BLOCKS, TILE), f32),
            pltpu.VMEM((3, TILE, BLK), f32),
            pltpu.VMEM((3, TILE, BLK), f32),
        ]
        + [pltpu.VMEM((TILE, BLK), f32)] * 6
        + [
            pltpu.SMEM((2 * PANELS + 2,), jnp.int32),
            pltpu.VMEM((TILE, BLK), f32),
            pltpu.VMEM((2 * PANELS, TILE), f32),
            pltpu.SemaphoreType.DMA,
        ],
        compiler_params=pltpu.CompilerParams(vmem_limit_bytes=VMEM_LIMIT),
        name="near",
    )(live, panel, points)


def reduce_kernel(
    partial, panel, points, out_ref, far, centres, arrived, send_sem, recv_sem,
):
    me = lax.axis_index("owner")
    lane = lax.axis_index("qgrp")
    kind = remainder(me, 4)
    group = me - kind
    member = kind * PAN_TURN + lane
    partners = [(to_kind, to_lane) for to_lane in far_lanes(lane) for to_kind in range(4)]
    partners += [(remainder(kind + dk, 4), lane) for dk in range(1, 4)]
    barrier = pltpu.get_barrier_semaphore()
    for to_kind, to_lane in partners:
        pl.semaphore_signal(barrier, inc=1, device_id=(group + to_kind, to_lane), device_id_type=MESH)
    spread_poles(panel, centres)

    def far_field(step, carry):
        for index in range(MEMBERS_STEP):
            one = step * MEMBERS_STEP + index
            for half in range(2):
                field = dipole_field([centres[c] for c in range(6)], points[one, 3 * half : 3 * half + 3, :])
                far[one, half : half + 1, :] = partial[one, half : half + 1, :] + jnp.sum(
                    field, axis=0, keepdims=True
                )
        return carry

    lax.fori_loop(0, PANELS // MEMBERS_STEP, far_field, 0)
    pl.semaphore_wait(barrier, PANELS - 1)

    for to_kind, to_lane in partners:
        pltpu.make_async_remote_copy(
            src_ref=far.at[to_kind * PAN_TURN + to_lane], dst_ref=arrived.at[member],
            send_sem=send_sem, recv_sem=recv_sem, device_id=(group + to_kind, to_lane), device_id_type=MESH,
        ).start()
    arrived[member] = far[member]
    part = arrived.at[pl.ds(0, PANELS - 1)]
    pltpu.make_async_copy(part, part, recv_sem).wait()
    out_ref[...] = jnp.sum(arrived[...], axis=0)
    pltpu.make_async_copy(part, part, send_sem).wait()


def on_device(queries, winding_in, triangles, dipoles, plan, near_blocks, near_count):
    vmem = pl.BlockSpec(memory_space=pltpu.VMEM)
    hbm = pl.BlockSpec(memory_space=pl.ANY)
    f32 = jnp.float32
    panel, points, live = pl.pallas_call(
        gather_kernel,
        out_shape=(
            jax.ShapeDtypeStruct((PARTS, TURNS, ROWS, BLK), f32),
            jax.ShapeDtypeStruct((PANELS, 8, TILE), f32),
            jax.ShapeDtypeStruct((PANELS, 2, 128), jnp.int32),
        ),
        in_specs=[hbm] * 6,
        out_specs=(hbm, hbm, hbm),
        scratch_shapes=[
            pltpu.VMEM((3, 2 * TILE), f32),
            pltpu.VMEM((9, BLOCKS * BLK), f32),
            pltpu.VMEM((6, BLOCKS), f32),
            pltpu.VMEM((2, NEAR, PANELS), jnp.int32),
            pltpu.VMEM((2, PANELS), jnp.int32),
            pltpu.SMEM((TURNS,), jnp.int32),
            pltpu.VMEM((16, 2, ROWS, BLK), f32),
            pltpu.VMEM((16, 2, ROWS, BLK), f32),
            pltpu.VMEM((2, TURNS, ROWS, BLK), f32),
            pltpu.VMEM((4, TURNS, ROWS, BLK), f32),
            pltpu.VMEM((TURNS, ROWS, BLK), f32),
            pltpu.VMEM((8, TILE), f32),
            pltpu.VMEM((PANELS, 8, TILE), f32),
            pltpu.VMEM((PANELS, 2, 128), jnp.int32),
            pltpu.SemaphoreType.DMA((6,)),
            pltpu.SemaphoreType.DMA((3,)),
        ]
        + [pltpu.SemaphoreType.DMA] * 9,
        compiler_params=pltpu.CompilerParams(collective_id=0, has_side_effects=True, vmem_limit_bytes=VMEM_LIMIT),
        name="gather",
    )(
        *[
            pltpu.with_memory_space_constraint(array, pltpu.HBM)
            for array in (plan, queries, triangles, dipoles, near_blocks.transpose(0, 2, 1), near_count)
        ],
    )
    partial = near_call(live, panel, points)
    total = pl.pallas_call(
        reduce_kernel,
        out_shape=jax.ShapeDtypeStruct((2, TILE), f32),
        in_specs=[vmem] * 3,
        out_specs=vmem,
        scratch_shapes=[
            pltpu.VMEM((PANELS, 2, TILE), f32),
            pltpu.VMEM((6, BLOCKS, TILE), f32),
            pltpu.VMEM((PANELS, 2, TILE), f32),
            pltpu.SemaphoreType.DMA,
            pltpu.SemaphoreType.DMA,
        ],
        compiler_params=pltpu.CompilerParams(collective_id=1, has_side_effects=True, vmem_limit_bytes=VMEM_LIMIT),
        name="reduce",
    )(partial, panel, points)
    return winding_in + total.reshape(-1)


def solution(mesh):
    return jax.shard_map(
        on_device,
        mesh=mesh,
        in_specs=(
            P(None, ("owner", "qgrp")),
            P(("owner", "qgrp")),
            P(None, ("owner", "qgrp")),
            P(None, ("owner", "qgrp")),
            P(),
            P(("owner", "qgrp"), None, None),
            P(("owner", "qgrp"), None),
        ),
        out_specs=P(("owner", "qgrp")),
        check_vma=False,
    )
```

```python
import functools

import jax
import jax.numpy as jnp
from jax import lax
from jax.experimental import pallas as pl
from jax.experimental.pallas import tpu as pltpu
from jax.sharding import PartitionSpec as P

TILE = 128
BLK = 128
BLOCKS = 32
NEAR = 4
TURNS = 4
PAN_TURN = 4
PANELS = TURNS * PAN_TURN
OWNERS = 64
ROWS = 10
MEMBERS = 8
PARTS = 16
HELD = PARTS * TURNS
MEMBERS_STEP = 2
VMEM_LIMIT = 16 * 1024 * 1024

MESH = pl.DeviceIdType.MESH

pi = 3.141592653589793
four_pi = 4.0 * pi
soften = 0.1

ATAN = (
    0.9999994039535522,
    -0.3332701325416565,
    0.19887319207191467,
    -0.13512171804904938,
    0.08435401320457458,
    -0.03744291514158249,
    0.008006880059838295,
)


def quotient(number, by):
    return number // by if isinstance(number, int) else lax.div(number, jnp.int32(by))


def remainder(number, by):
    return number % by if isinstance(number, int) else lax.rem(number, jnp.int32(by))


def block_of(place):
    kind, part = place % 4, place // 4
    return kind % 2 + (part % 2) * 2 + (kind // 2) * 4 + (part // 2) * 8


def stage_place(slot):
    return (slot // 8) * 8 + (slot % 2) * 4 + (slot // 2) % 4


def far_lanes(lane):
    side = quotient(lane, 2)
    return 3 * (1 - side), 2 - side, side * (5 - lane) + (1 - side) * (1 - lane)


def gather_kernel(
    plan_ref, queries_ref, triangles_ref, dipoles_ref, blocks_ref, count_ref,
    panel_ref, points_ref, live_ref, flipped_ref,
    queries, triangles, dipoles, blocks, count, turn_owner,
    stage, gathered, picked, offered, chosen, message, messages, live,
    load_sems, out_sems, send_one, recv_one, send_pick, recv_pick, send_two, recv_two, recv_far, send_msg, recv_msg,
):
    me = lax.axis_index("owner")
    lane = lax.axis_index("qgrp")
    kind = remainder(me, 4)
    side = remainder(quotient(me, 4), 2)
    half = remainder(quotient(me, 8), 2)
    across = quotient(me, 16)
    core = remainder(me, 2)
    level = remainder(quotient(me, 2), 4)
    part = across * 4 + level
    member = core * PAN_TURN + lane
    squad = across * 4 + kind
    group = me - core
    mirror = PAN_TURN - 1 - lane
    role = half * lane + (1 - half) * mirror
    first = half == 0
    barrier = pltpu.get_barrier_semaphore()

    loads = [
        pltpu.make_async_copy(source, target, load_sems.at[index])
        for index, (source, target) in enumerate(
            [
                (triangles_ref, triangles), (dipoles_ref, dipoles), (queries_ref, queries),
                (blocks_ref, blocks), (count_ref, count), (plan_ref, turn_owner),
            ]
        )
    ]
    def greet(owner, to_lane):
        pl.semaphore_signal(barrier, inc=1, device_id=(owner, to_lane), device_id_type=MESH)

    squads = [(dx, dk) for dx in (2, 1, 3, 0) for dk in (2, 3, 1, 0) if (dx, dk) != (0, 0)]
    lanes = far_lanes(lane)

    def comrade(dx, dk):
        to_across, to_kind = remainder(across + dx, 4), remainder(kind + dk, 4)
        return to_across * 4 + to_kind, (to_across * 16 + half * 8 + side * 4 + to_kind, lane)

    @pl.when(first)
    def _():
        for to_side in range(2):
            greet(across * 16 + 8 + to_side * 4 + kind, mirror)
            greet(across * 16 + to_side * 4 + kind, mirror)

    for dx in (2, 1, 3, 0):
        for low in range(2):
            greet(remainder(across + dx, 4) * 16 + half * 8 + (1 - side) * 4 + low * 2 + core, lane)
    for to_lane in lanes:
        for to_core in range(2):
            greet(group + to_core, to_lane)
    for dx, dk in squads:
        greet(*comrade(dx, dk)[1])

    for load in loads:
        load.start()

    loads[1].wait()
    flipped = jnp.concatenate(
        [jnp.concatenate([dipoles[...], jnp.zeros((2, BLOCKS), jnp.float32)], axis=0),
         jnp.zeros((8, BLK - BLOCKS), jnp.float32)], axis=1
    ).T
    loads[0].wait()
    for slot in range(BLOCKS):
        block = block_of(stage_place(slot))
        stage[slot // 2, slot % 2, 0:9] = triangles[:, block * BLK : (block + 1) * BLK]
        stage[slot // 2, slot % 2, 9:10, 0:8] = flipped[block : block + 1, :]
    for load in loads[2:]:
        load.wait()
    message[0:3] = queries[:, 0:TILE]
    message[3:6] = queries[:, TILE : 2 * TILE]
    for tile in range(2):
        counted = count[tile : tile + 1, :]
        rows = [jnp.where(counted > slot, blocks[tile, slot : slot + 1, :], -1) for slot in range(NEAR)]
        rows.append(jnp.full((1, BLK - PANELS * NEAR), -1, jnp.int32))
        message[6 + tile : 7 + tile] = jnp.concatenate(rows, axis=1).astype(jnp.float32)

    def wait_bytes(part, sem):
        pltpu.make_async_copy(part, part, sem).wait()

    pl.semaphore_wait(barrier, 15 + 2 * (PAN_TURN - 1) + 8 + 2)

    for dx, dk in squads:
        other, where = comrade(dx, dk)
        pltpu.make_async_remote_copy(
            src_ref=stage.at[other], dst_ref=gathered.at[squad], send_sem=send_one, recv_sem=recv_one,
            device_id=where, device_id_type=MESH,
        ).start()

    def send_message(owner, to_lane):
        pltpu.make_async_remote_copy(
            src_ref=message, dst_ref=messages.at[member], send_sem=send_msg, recv_sem=recv_msg,
            device_id=(owner, to_lane), device_id_type=MESH,
        ).start()

    for to_lane in lanes:
        for to_core in range(2):
            send_message(group + to_core, to_lane)
    send_message(group + 1 - core, lane)
    gathered[squad] = stage[squad]
    messages[member] = message[...]
    wait_bytes(gathered.at[pl.ds(0, 15)], recv_one)
    for turn in range(TURNS):
        owner = turn_owner[turn]
        pair = gathered[quotient(owner, 16) * 4 + remainder(owner, 4)]
        picked[0, turn] = pair[0]
        picked[1, turn] = pair[1]
    for to_side in range(2):
        pltpu.make_async_remote_copy(
            src_ref=picked.at[to_side], dst_ref=offered.at[half * 2 + side], send_sem=send_pick, recv_sem=recv_pick,
            device_id=(across * 16 + to_side * 4 + kind, mirror), device_id_type=MESH,
        ).start()

    @pl.when(first)
    def _():
        wait_bytes(offered, recv_pick)
        for turn in range(TURNS):
            owner = turn_owner[turn]
            squad_of = remainder(quotient(owner, 8), 2) * 2 + remainder(quotient(owner, 4), 2)
            chosen[turn] = offered[squad_of, turn]
        pltpu.make_async_remote_copy(
            src_ref=chosen, dst_ref=chosen, send_sem=send_two, recv_sem=recv_far,
            device_id=(me + 8, mirror), device_id_type=MESH,
        ).start()

    @pl.when(jnp.logical_not(first))
    def _():
        wait_bytes(chosen, recv_far)

    for dx, dy in [(dx, dy) for dx in (2, 1, 3, 0) for dy in (2, 1, 3, 0) if (dx, dy) != (0, 0)]:
        to_level = remainder(level + dy, 4)
        pltpu.make_async_remote_copy(
            src_ref=chosen, dst_ref=panel_ref.at[part], send_sem=send_two, recv_sem=recv_two,
            device_id=(remainder(across + dx, 4) * 16 + half * 8 + to_level * 2 + core, lane), device_id_type=MESH,
        ).start()
    outs = [
        pltpu.make_async_copy(source, target, out_sems.at[index])
        for index, (source, target) in enumerate(
            [(chosen, panel_ref.at[part]), (messages, points_ref), (live, live_ref)]
        )
    ]
    outs[0].start()
    wait_bytes(messages.at[pl.ds(0, MEMBERS - 1)], recv_msg)
    outs[1].start()

    shape = (MEMBERS, BLK)
    column = lax.broadcasted_iota(jnp.int32, shape, 1)
    before = (
        lax.broadcasted_iota(jnp.int32, (BLK, BLK), 0) < lax.broadcasted_iota(jnp.int32, (BLK, BLK), 1)
    ).astype(jnp.float32)
    for tile in range(2):
        listed = messages[:, 6 + tile, :].astype(jnp.int32)
        held = listed % 2 == core
        held = jnp.logical_and(held, column % PAN_TURN == role)
        held = jnp.logical_and(held, jnp.logical_and(listed >= 0, column < PANELS * NEAR))
        where = (listed // 8) * 4 + ((listed // 2) % 2) * 2 + (listed // 4) % 2
        value = where * TURNS + (column % PANELS) // PAN_TURN
        value = value.astype(jnp.float32)
        flags = jnp.where(held, 1.0, 0.0)
        rank = lax.dot_general(flags, before, (((1,), (0,)), ((), ())), preferred_element_type=jnp.float32)
        rank = jnp.where(held, rank, -1.0)
        packed = jnp.where(column == PANELS, jnp.sum(flags, axis=1, keepdims=True), 0.0)
        for index in range(PANELS):
            one = jnp.sum(jnp.where(jnp.abs(rank - index) < 0.5, value, 0.0), axis=1, keepdims=True)
            packed = jnp.where(column == index, one, packed)
        live[:, tile, :] = packed[:, 0:32].astype(jnp.int32)
    outs[2].start()

    def flip(to, carry):
        rest = messages[to]
        parts = []
        for _ in range(3):
            parts.append(rest.astype(jnp.bfloat16).astype(jnp.float32))
            rest = rest - parts[-1]
        parts.append(jnp.zeros_like(rest))
        flipped_ref[to] = jnp.concatenate(parts, axis=0).T.astype(jnp.bfloat16)
        return carry

    lax.fori_loop(0, MEMBERS, flip, 0)

    wait_bytes(stage.at[pl.ds(0, 15)], send_one)
    wait_bytes(picked, send_pick)
    wait_bytes(messages.at[pl.ds(0, MEMBERS - 1)], send_msg)

    @pl.when(first)
    def _():
        wait_bytes(panel_ref, send_two)

    @pl.when(jnp.logical_not(first))
    def _():
        wait_bytes(panel_ref.at[pl.ds(0, PARTS - 1)], send_two)

    for out in outs:
        out.wait()
    wait_bytes(panel_ref.at[pl.ds(0, PARTS - 1)], recv_two)


def dipole_field(centre, points):
    offset = [centre[c] - jnp.broadcast_to(points[c : c + 1, :], centre[c].shape) for c in range(3)]
    square = offset[0] * offset[0] + offset[1] * offset[1] + offset[2] * offset[2] + soften
    inverse = lax.rsqrt(square)
    return (centre[3] * offset[0] + centre[4] * offset[1] + centre[5] * offset[2]) * (
        inverse * inverse * inverse
    )


def spread_poles(panel, centres):
    rows = jnp.concatenate([panel[slot // 4, slot % 4, 9:10, :] for slot in range(HELD)], axis=0)
    for component in range(6):
        value = jnp.broadcast_to(rows[:, component : component + 1], (HELD, TILE))
        if component >= 3:
            value = value * (1.0 / four_pi)
        centres[component] = value


def near_kernel(
    live_hbm, panel_ref, given, flipped, out_ref,
    live_ref, points_ref, picker, centres,
    spread_0, spread_1, real_0, real_1, imag_0, imag_1, turns_0, turns_1, tiles, sums, minus, sem
):
    spread, real, imag, turns = (spread_0, spread_1), (real_0, real_1), (imag_0, imag_1), (turns_0, turns_1)
    load = pltpu.make_async_copy(live_hbm, live_ref, sem)
    load.start()
    minus[...] = jnp.zeros_like(minus)
    sums[...] = jnp.zeros_like(sums)
    real_0[...] = jnp.ones_like(real_0)
    imag_0[...] = jnp.zeros_like(imag_0)
    turns_0[...] = jnp.zeros_like(turns_0)
    spread_poles(panel_ref, centres)
    for member in range(MEMBERS):
        for half in range(2):
            points_ref[2 * member + half, 0:3] = given[member, 3 * half : 3 * half + 3]
    load.wait()
    tiles[0] = 2 * MEMBERS
    found = jnp.int32(0)
    for tile in range(2 * MEMBERS):
        tiles[found + 1] = tile
        found = found + jnp.where(live_ref[tile // 2, tile % 2, PANELS] > 0, 1, 0)
    tiles[found + 1] = 0
    lanes = lax.broadcasted_iota(jnp.int32, (8, BLK), 1)

    shape = (32, 3 * BLK)
    entry = lax.broadcasted_iota(jnp.int32, shape, 0)
    component = lax.broadcasted_iota(jnp.int32, shape, 1) // BLK
    for half in range(2):
        wanted = jnp.logical_and(entry % 8 == 3 * half + component, entry < 24)
        picker[half] = jnp.where(wanted, 1.0, 0.0).astype(jnp.bfloat16)

    def widen(tile):
        return lax.dot_general(
            flipped[tile // 2], picker[tile % 2], (((1,), (0,)), ((), ())), preferred_element_type=jnp.float32
        )

    def spread_part(place, part, wide):
        at = pl.ds(part * 8, 8)
        for c in range(3):
            spread[place][c, at] = wide[part * 8 : part * 8 + 8, c * BLK : (c + 1) * BLK]

    def angle(x, y):
        ax, ay = jnp.abs(x), jnp.abs(y)
        t = jnp.minimum(ax, ay) * pl.reciprocal(jnp.maximum(ax, ay), approx=True)
        square = t * t
        value = jnp.full_like(t, ATAN[-1] * 0.5 / pi)
        for coefficient in ATAN[-2::-1]:
            value = value * square + coefficient * 0.5 / pi
        value = value * t
        value = jnp.where(ay > ax, 0.25 - value, value)
        value = jnp.where(x < 0.0, 0.5 - value, value)
        return jnp.where(y < 0.0, -value, value)

    def angle_part(place, part, tile):
        at = pl.ds(part * 8, 8)
        total = angle(real[place][at], imag[place][at]) + turns[place][at]
        sums[at] = jnp.where(lanes == tile, jnp.sum(total, axis=1, keepdims=True), sums[at])

    def exact_block(block, tile, place, starts, beside):
        corner = [
            jnp.broadcast_to(panel_ref[block // 4, block % 4, c : c + 1, :], (8, BLK)) for c in range(9)
        ]
        ax, ay, az, bx, by, bz, cx, cy, cz = corner
        ux, uy, uz = bx - ax, by - ay, bz - az
        vx, vy, vz = cx - ax, cy - ay, cz - az
        wx, wy, wz = cx - bx, cy - by, cz - bz
        ux2, uy2, uz2 = ux + ux, uy + uy, uz + uz
        nx = uy2 * vz - uz2 * vy
        ny = uz2 * vx - ux2 * vz
        nz = ux2 * vy - uy2 * vx
        side_ab = ux * ux + uy * uy + uz * uz
        side_bc = wx * wx + wy * wy + wz * wz
        side_ca = vx * vx + vy * vy + vz * vz
        for part in range(TILE // 8):
            at = pl.ds(part * 8, 8)
            beside(part)
            qx, qy, qz = spread[place][0, at], spread[place][1, at], spread[place][2, at]

            def from_point(x, y, z):
                x, y, z = x - qx, y - qy, z - qz
                square = x * x + y * y + z * z
                return x, y, z, square * lax.rsqrt(square)

            px, py, pz, la = from_point(ax, ay, az)
            lb = from_point(bx, by, bz)[3]
            lc = from_point(cx, cy, cz)[3]
            y = px * nx + py * ny + pz * nz
            x = (la + lb) * (lb + lc) * (lc + la) - (side_ab * lc + side_bc * la + side_ca * lb)
            if starts:
                real[place][at], imag[place][at] = x, y
                turns[place][at] = jnp.zeros((8, BLK), jnp.float32)
            else:
                u, v = real[place][at], imag[place][at]
                below = y < 0.0
                r, i = u * x - v * y, u * y + v * x
                same = jnp.logical_not(jnp.logical_xor(v < 0.0, below))
                wrapped = jnp.logical_and(same, jnp.logical_xor(i < 0.0, below))
                turns[place][at] += jnp.where(wrapped, jnp.where(below, -1.0, 1.0), 0.0)
                real[place][at], imag[place][at] = r, i
        row = pl.ds(block, 1)
        field = dipole_field([centres[c, row, :] for c in range(6)], points_ref[tile, 0:3, :])
        minus[pl.ds(tile, 1), :] -= field

    first = widen(tiles[1])
    for part in range(TILE // 8):
        spread_part(1, part, first)

    def one_tile(index, place):
        tile = tiles[index]
        last, following = tiles[index - 1], tiles[index + 1]
        member, half = tile // 2, tile % 2
        across = widen(following)

        def beside(part):
            angle_part(1 - place, part, last)
            spread_part(1 - place, part, across)

        exact_block(live_ref[member, half, 0], tile, place, True, beside)

        def more(slot, carry):
            @pl.when(slot % 4 == 0)
            def _():
                u, v = real[place][...], imag[place][...]
                factor = 1.0 / (jnp.abs(u) + jnp.abs(v))
                real[place][...], imag[place][...] = u * factor, v * factor

            exact_block(live_ref[member, half, slot], tile, place, False, lambda part: None)
            return carry

        lax.fori_loop(1, live_ref[member, half, PANELS], more, 0)

    def two_tiles(step, carry):
        one_tile(2 * step + 1, 1)

        @pl.when(2 * step + 2 <= found)
        def _():
            one_tile(2 * step + 2, 0)

        return carry

    lax.fori_loop(0, (found + 1) // 2, two_tiles, 0)
    for place in range(2):

        @pl.when(found % 2 == place)
        def _():
            for part in range(TILE // 8):
                angle_part(place, part, tiles[found])

    rows = sums[...].T
    rows = rows[0 : 2 * MEMBERS, :] + minus[...]
    for member in range(MEMBERS):
        out_ref[member] = rows[2 * member : 2 * member + 2, :]


def near_call(live, panel, points, flipped):
    hbm = pl.BlockSpec(memory_space=pl.ANY)
    vmem = pl.BlockSpec(memory_space=pltpu.VMEM)
    f32 = jnp.float32
    return pl.pallas_call(
        near_kernel,
        out_shape=jax.ShapeDtypeStruct((MEMBERS, 2, TILE), f32),
        in_specs=[hbm, vmem, vmem, vmem],
        out_specs=vmem,
        scratch_shapes=[
            pltpu.SMEM((MEMBERS, 2, 32), jnp.int32),
            pltpu.VMEM((2 * MEMBERS, 8, TILE), f32),
            pltpu.VMEM((2, 32, 3 * BLK), jnp.bfloat16),
            pltpu.VMEM((6, HELD, TILE), f32),
            pltpu.VMEM((3, TILE, BLK), f32),
            pltpu.VMEM((3, TILE, BLK), f32),
        ]
        + [pltpu.VMEM((TILE, BLK), f32)] * 6
        + [
            pltpu.SMEM((2 * MEMBERS + 2,), jnp.int32),
            pltpu.VMEM((TILE, BLK), f32),
            pltpu.VMEM((2 * MEMBERS, TILE), f32),
            pltpu.SemaphoreType.DMA,
        ],
        compiler_params=pltpu.CompilerParams(vmem_limit_bytes=VMEM_LIMIT),
        name="near",
    )(live, panel, points, flipped)


def reduce_kernel(
    partial, panel, points, out_ref, far, centres, arrived, send_sem, recv_sem,
):
    me = lax.axis_index("owner")
    lane = lax.axis_index("qgrp")
    core = remainder(me, 2)
    group = me - core
    member = core * PAN_TURN + lane
    partners = [(to_core, to_lane) for to_lane in far_lanes(lane) for to_core in range(2)]
    partners.append((1 - core, lane))
    barrier = pltpu.get_barrier_semaphore()
    for to_core, to_lane in partners:
        pl.semaphore_signal(barrier, inc=1, device_id=(group + to_core, to_lane), device_id_type=MESH)
    spread_poles(panel, centres)

    def far_field(step, carry):
        for index in range(MEMBERS_STEP):
            one = step * MEMBERS_STEP + index
            for half in range(2):
                field = dipole_field([centres[c] for c in range(6)], points[one, 3 * half : 3 * half + 3, :])
                far[one, half : half + 1, :] = partial[one, half : half + 1, :] + jnp.sum(
                    field, axis=0, keepdims=True
                )
        return carry

    lax.fori_loop(0, MEMBERS // MEMBERS_STEP, far_field, 0)
    pl.semaphore_wait(barrier, MEMBERS - 1)

    for to_core, to_lane in partners:
        pltpu.make_async_remote_copy(
            src_ref=far.at[to_core * PAN_TURN + to_lane], dst_ref=arrived.at[member],
            send_sem=send_sem, recv_sem=recv_sem, device_id=(group + to_core, to_lane), device_id_type=MESH,
        ).start()
    arrived[member] = far[member]
    part = arrived.at[pl.ds(0, MEMBERS - 1)]
    pltpu.make_async_copy(part, part, recv_sem).wait()
    out_ref[...] = jnp.sum(arrived[...], axis=0)
    pltpu.make_async_copy(part, part, send_sem).wait()


def on_device(queries, winding_in, triangles, dipoles, plan, near_blocks, near_count):
    vmem = pl.BlockSpec(memory_space=pltpu.VMEM)
    hbm = pl.BlockSpec(memory_space=pl.ANY)
    f32 = jnp.float32
    panel, points, live, flipped = pl.pallas_call(
        gather_kernel,
        out_shape=(
            jax.ShapeDtypeStruct((PARTS, TURNS, ROWS, BLK), f32),
            jax.ShapeDtypeStruct((MEMBERS, 8, TILE), f32),
            jax.ShapeDtypeStruct((MEMBERS, 2, 32), jnp.int32),
            jax.ShapeDtypeStruct((MEMBERS, TILE, 32), jnp.bfloat16),
        ),
        in_specs=[hbm] * 6,
        out_specs=(hbm, hbm, hbm, vmem),
        scratch_shapes=[
            pltpu.VMEM((3, 2 * TILE), f32),
            pltpu.VMEM((9, BLOCKS * BLK), f32),
            pltpu.VMEM((6, BLOCKS), f32),
            pltpu.VMEM((2, NEAR, PANELS), jnp.int32),
            pltpu.VMEM((2, PANELS), jnp.int32),
            pltpu.SMEM((TURNS,), jnp.int32),
            pltpu.VMEM((16, 2, ROWS, BLK), f32),
            pltpu.VMEM((16, 2, ROWS, BLK), f32),
            pltpu.VMEM((2, TURNS, ROWS, BLK), f32),
            pltpu.VMEM((4, TURNS, ROWS, BLK), f32),
            pltpu.VMEM((TURNS, ROWS, BLK), f32),
            pltpu.VMEM((8, TILE), f32),
            pltpu.VMEM((MEMBERS, 8, TILE), f32),
            pltpu.VMEM((MEMBERS, 2, 32), jnp.int32),
            pltpu.SemaphoreType.DMA((6,)),
            pltpu.SemaphoreType.DMA((3,)),
        ]
        + [pltpu.SemaphoreType.DMA] * 9,
        compiler_params=pltpu.CompilerParams(collective_id=0, has_side_effects=True, vmem_limit_bytes=VMEM_LIMIT),
        name="gather",
    )(
        *[
            pltpu.with_memory_space_constraint(array, pltpu.HBM)
            for array in (plan, queries, triangles, dipoles, near_blocks.transpose(0, 2, 1), near_count)
        ],
    )
    partial = near_call(live, panel, points, flipped)
    total = pl.pallas_call(
        reduce_kernel,
        out_shape=jax.ShapeDtypeStruct((2, TILE), f32),
        in_specs=[vmem] * 3,
        out_specs=vmem,
        scratch_shapes=[
            pltpu.VMEM((MEMBERS, 2, TILE), f32),
            pltpu.VMEM((6, HELD, TILE), f32),
            pltpu.VMEM((MEMBERS, 2, TILE), f32),
            pltpu.SemaphoreType.DMA,
            pltpu.SemaphoreType.DMA,
        ],
        compiler_params=pltpu.CompilerParams(collective_id=1, has_side_effects=True, vmem_limit_bytes=VMEM_LIMIT),
        name="reduce",
    )(partial, panel, points)
    return winding_in + total.reshape(-1)


def solution(mesh):
    return jax.shard_map(
        on_device,
        mesh=mesh,
        in_specs=(
            P(None, ("owner", "qgrp")),
            P(("owner", "qgrp")),
            P(None, ("owner", "qgrp")),
            P(None, ("owner", "qgrp")),
            P(),
            P(("owner", "qgrp"), None, None),
            P(("owner", "qgrp"), None),
        ),
        out_specs=P(("owner", "qgrp")),
        check_vma=False,
    )
```

```python
import functools

import jax
import jax.numpy as jnp
from jax import lax
from jax.experimental import pallas as pl
from jax.experimental.pallas import tpu as pltpu
from jax.sharding import PartitionSpec as P

TILE = 128
BLK = 128
BLOCKS = 32
NEAR = 4
TURNS = 4
PAN_TURN = 4
PANELS = TURNS * PAN_TURN
OWNERS = 64
ROWS = 10
MEMBERS = 8
PARTS = 16
HELD = PARTS * TURNS
MEMBERS_STEP = 2
VMEM_LIMIT = 16 * 1024 * 1024

MESH = pl.DeviceIdType.MESH

pi = 3.141592653589793
four_pi = 4.0 * pi
soften = 0.1

ATAN = (
    0.9999994039535522,
    -0.3332701325416565,
    0.19887319207191467,
    -0.13512171804904938,
    0.08435401320457458,
    -0.03744291514158249,
    0.008006880059838295,
)


def quotient(number, by):
    return number // by if isinstance(number, int) else lax.div(number, jnp.int32(by))


def remainder(number, by):
    return number % by if isinstance(number, int) else lax.rem(number, jnp.int32(by))


def block_of(place):
    kind, part = place % 4, place // 4
    return kind % 2 + (part % 2) * 2 + (kind // 2) * 4 + (part // 2) * 8


def stage_place(slot):
    return (slot // 8) * 8 + (slot % 2) * 4 + (slot // 2) % 4


def far_lanes(lane):
    side = quotient(lane, 2)
    return 3 * (1 - side), 2 - side, side * (5 - lane) + (1 - side) * (1 - lane)


def gather_kernel(
    plan_ref, queries_ref, triangles_ref, dipoles_ref, blocks_ref, count_ref,
    panel_ref, points_ref, live_ref, flipped_ref,
    queries, triangles, dipoles, blocks, count, turn_owner,
    stage, gathered, picked, offered, chosen, message, messages, live,
    load_sems, out_sems, send_one, recv_one, send_pick, recv_pick, send_two, recv_two, recv_far, send_msg, recv_msg,
):
    me = lax.axis_index("owner")
    lane = lax.axis_index("qgrp")
    kind = remainder(me, 4)
    side = remainder(quotient(me, 4), 2)
    half = remainder(quotient(me, 8), 2)
    across = quotient(me, 16)
    core = remainder(me, 2)
    level = remainder(quotient(me, 2), 4)
    part = across * 4 + level
    member = core * PAN_TURN + lane
    squad = across * 4 + kind
    group = me - core
    mirror = PAN_TURN - 1 - lane
    role = half * lane + (1 - half) * mirror
    first = half == 0
    barrier = pltpu.get_barrier_semaphore()

    loads = [
        pltpu.make_async_copy(source, target, load_sems.at[index])
        for index, (source, target) in enumerate(
            [
                (triangles_ref, triangles), (dipoles_ref, dipoles), (queries_ref, queries),
                (blocks_ref, blocks), (count_ref, count), (plan_ref, turn_owner),
            ]
        )
    ]
    def greet(owner, to_lane):
        pl.semaphore_signal(barrier, inc=1, device_id=(owner, to_lane), device_id_type=MESH)

    squads = [(dx, dk) for dx in (2, 1, 3, 0) for dk in (2, 3, 1, 0) if (dx, dk) != (0, 0)]
    lanes = far_lanes(lane)

    def comrade(dx, dk):
        to_across, to_kind = remainder(across + dx, 4), remainder(kind + dk, 4)
        return to_across * 4 + to_kind, (to_across * 16 + half * 8 + side * 4 + to_kind, lane)

    @pl.when(first)
    def _():
        for to_side in range(2):
            greet(across * 16 + 8 + to_side * 4 + kind, mirror)
            greet(across * 16 + to_side * 4 + kind, mirror)

    for dx in (2, 1, 3, 0):
        for low in range(2):
            greet(remainder(across + dx, 4) * 16 + half * 8 + (1 - side) * 4 + low * 2 + core, lane)
    for to_lane in lanes:
        for to_core in range(2):
            greet(group + to_core, to_lane)
    for dx, dk in squads:
        greet(*comrade(dx, dk)[1])

    for load in loads:
        load.start()

    loads[1].wait()
    flipped = jnp.concatenate(
        [jnp.concatenate([dipoles[...], jnp.zeros((2, BLOCKS), jnp.float32)], axis=0),
         jnp.zeros((8, BLK - BLOCKS), jnp.float32)], axis=1
    ).T
    loads[0].wait()
    for slot in range(BLOCKS):
        block = block_of(stage_place(slot))
        stage[slot // 2, slot % 2, 0:9] = triangles[:, block * BLK : (block + 1) * BLK]
        stage[slot // 2, slot % 2, 9:10, 0:8] = flipped[block : block + 1, :]
    for load in loads[2:]:
        load.wait()
    message[0:3] = queries[:, 0:TILE]
    message[3:6] = queries[:, TILE : 2 * TILE]
    for tile in range(2):
        counted = count[tile : tile + 1, :]
        rows = [jnp.where(counted > slot, blocks[tile, slot : slot + 1, :], -1) for slot in range(NEAR)]
        rows.append(jnp.full((1, BLK - PANELS * NEAR), -1, jnp.int32))
        message[6 + tile : 7 + tile] = jnp.concatenate(rows, axis=1).astype(jnp.float32)

    def wait_bytes(part, sem):
        pltpu.make_async_copy(part, part, sem).wait()

    pl.semaphore_wait(barrier, 15 + 2 * (PAN_TURN - 1) + 8 + 2)

    for dx, dk in squads:
        other, where = comrade(dx, dk)
        pltpu.make_async_remote_copy(
            src_ref=stage.at[other], dst_ref=gathered.at[squad], send_sem=send_one, recv_sem=recv_one,
            device_id=where, device_id_type=MESH,
        ).start()

    def send_message(owner, to_lane):
        pltpu.make_async_remote_copy(
            src_ref=message, dst_ref=messages.at[member], send_sem=send_msg, recv_sem=recv_msg,
            device_id=(owner, to_lane), device_id_type=MESH,
        ).start()

    for to_lane in lanes:
        for to_core in range(2):
            send_message(group + to_core, to_lane)
    send_message(group + 1 - core, lane)
    gathered[squad] = stage[squad]
    messages[member] = message[...]
    wait_bytes(gathered.at[pl.ds(0, 15)], recv_one)
    for turn in range(TURNS):
        owner = turn_owner[turn]
        pair = gathered[quotient(owner, 16) * 4 + remainder(owner, 4)]
        picked[0, turn] = pair[0]
        picked[1, turn] = pair[1]
    for to_side in range(2):
        pltpu.make_async_remote_copy(
            src_ref=picked.at[to_side], dst_ref=offered.at[half * 2 + side], send_sem=send_pick, recv_sem=recv_pick,
            device_id=(across * 16 + to_side * 4 + kind, mirror), device_id_type=MESH,
        ).start()

    @pl.when(first)
    def _():
        wait_bytes(offered, recv_pick)
        for turn in range(TURNS):
            owner = turn_owner[turn]
            squad_of = remainder(quotient(owner, 8), 2) * 2 + remainder(quotient(owner, 4), 2)
            chosen[turn] = offered[squad_of, turn]
        pltpu.make_async_remote_copy(
            src_ref=chosen, dst_ref=chosen, send_sem=send_two, recv_sem=recv_far,
            device_id=(me + 8, mirror), device_id_type=MESH,
        ).start()

    @pl.when(jnp.logical_not(first))
    def _():
        wait_bytes(chosen, recv_far)

    for dx, dy in [(dx, dy) for dy, dx in [(2, 2), (0, 2), (2, 0), (1, 2), (2, 1), (3, 2), (2, 3), (1, 1), (3, 3), (1, 3), (3, 1), (0, 1), (1, 0), (0, 3), (3, 0)]]:
        to_level = remainder(level + dy, 4)
        pltpu.make_async_remote_copy(
            src_ref=chosen, dst_ref=panel_ref.at[part], send_sem=send_two, recv_sem=recv_two,
            device_id=(remainder(across + dx, 4) * 16 + half * 8 + to_level * 2 + core, lane), device_id_type=MESH,
        ).start()
    outs = [
        pltpu.make_async_copy(source, target, out_sems.at[index])
        for index, (source, target) in enumerate(
            [(chosen, panel_ref.at[part]), (messages, points_ref), (live, live_ref)]
        )
    ]
    outs[0].start()
    wait_bytes(messages.at[pl.ds(0, MEMBERS - 1)], recv_msg)
    outs[1].start()

    shape = (MEMBERS, BLK)
    column = lax.broadcasted_iota(jnp.int32, shape, 1)
    before = (
        lax.broadcasted_iota(jnp.int32, (BLK, BLK), 0) < lax.broadcasted_iota(jnp.int32, (BLK, BLK), 1)
    ).astype(jnp.float32)
    for tile in range(2):
        listed = messages[:, 6 + tile, :].astype(jnp.int32)
        held = listed % 2 == core
        held = jnp.logical_and(held, column % PAN_TURN == role)
        held = jnp.logical_and(held, jnp.logical_and(listed >= 0, column < PANELS * NEAR))
        where = (listed // 8) * 4 + ((listed // 2) % 2) * 2 + (listed // 4) % 2
        value = where * TURNS + (column % PANELS) // PAN_TURN
        value = value.astype(jnp.float32)
        flags = jnp.where(held, 1.0, 0.0)
        rank = lax.dot_general(flags, before, (((1,), (0,)), ((), ())), preferred_element_type=jnp.float32)
        rank = jnp.where(held, rank, -1.0)
        packed = jnp.where(column == PANELS, jnp.sum(flags, axis=1, keepdims=True), 0.0)
        for index in range(PANELS):
            one = jnp.sum(jnp.where(jnp.abs(rank - index) < 0.5, value, 0.0), axis=1, keepdims=True)
            packed = jnp.where(column == index, one, packed)
        live[:, tile, :] = packed[:, 0:32].astype(jnp.int32)
    outs[2].start()

    def flip(to, carry):
        rest = messages[to]
        parts = []
        for _ in range(3):
            parts.append(rest.astype(jnp.bfloat16).astype(jnp.float32))
            rest = rest - parts[-1]
        parts.append(jnp.zeros_like(rest))
        flipped_ref[to] = jnp.concatenate(parts, axis=0).T.astype(jnp.bfloat16)
        return carry

    lax.fori_loop(0, MEMBERS, flip, 0)

    wait_bytes(stage.at[pl.ds(0, 15)], send_one)
    wait_bytes(picked, send_pick)
    wait_bytes(messages.at[pl.ds(0, MEMBERS - 1)], send_msg)

    @pl.when(first)
    def _():
        wait_bytes(panel_ref, send_two)

    @pl.when(jnp.logical_not(first))
    def _():
        wait_bytes(panel_ref.at[pl.ds(0, PARTS - 1)], send_two)

    for out in outs:
        out.wait()
    wait_bytes(panel_ref.at[pl.ds(0, PARTS - 1)], recv_two)


def dipole_field(centre, points):
    offset = [centre[c] - jnp.broadcast_to(points[c : c + 1, :], centre[c].shape) for c in range(3)]
    square = offset[0] * offset[0] + offset[1] * offset[1] + offset[2] * offset[2] + soften
    inverse = lax.rsqrt(square)
    return (centre[3] * offset[0] + centre[4] * offset[1] + centre[5] * offset[2]) * (
        inverse * inverse * inverse
    )


def spread_poles(panel, centres):
    rows = jnp.concatenate([panel[slot // 4, slot % 4, 9:10, :] for slot in range(HELD)], axis=0)
    for component in range(6):
        value = jnp.broadcast_to(rows[:, component : component + 1], (HELD, TILE))
        if component >= 3:
            value = value * (1.0 / four_pi)
        centres[component] = value


def near_kernel(
    live_hbm, panel_ref, given, flipped, out_ref,
    live_ref, points_ref, picker, centres,
    spread_0, spread_1, real_0, real_1, imag_0, imag_1, turns_0, turns_1, tiles, sums, minus, sem
):
    spread, real, imag, turns = (spread_0, spread_1), (real_0, real_1), (imag_0, imag_1), (turns_0, turns_1)
    load = pltpu.make_async_copy(live_hbm, live_ref, sem)
    load.start()
    minus[...] = jnp.zeros_like(minus)
    sums[...] = jnp.zeros_like(sums)
    real_0[...] = jnp.ones_like(real_0)
    imag_0[...] = jnp.zeros_like(imag_0)
    turns_0[...] = jnp.zeros_like(turns_0)
    spread_poles(panel_ref, centres)
    for member in range(MEMBERS):
        for half in range(2):
            points_ref[2 * member + half, 0:3] = given[member, 3 * half : 3 * half + 3]
    load.wait()
    tiles[0] = 2 * MEMBERS
    found = jnp.int32(0)
    for tile in range(2 * MEMBERS):
        tiles[found + 1] = tile
        found = found + jnp.where(live_ref[tile // 2, tile % 2, PANELS] > 0, 1, 0)
    tiles[found + 1] = 0
    lanes = lax.broadcasted_iota(jnp.int32, (8, BLK), 1)

    shape = (32, 3 * BLK)
    entry = lax.broadcasted_iota(jnp.int32, shape, 0)
    component = lax.broadcasted_iota(jnp.int32, shape, 1) // BLK
    for half in range(2):
        wanted = jnp.logical_and(entry % 8 == 3 * half + component, entry < 24)
        picker[half] = jnp.where(wanted, 1.0, 0.0).astype(jnp.bfloat16)

    def widen(tile):
        return lax.dot_general(
            flipped[tile // 2], picker[tile % 2], (((1,), (0,)), ((), ())), preferred_element_type=jnp.float32
        )

    def spread_part(place, part, wide):
        at = pl.ds(part * 8, 8)
        for c in range(3):
            spread[place][c, at] = wide[part * 8 : part * 8 + 8, c * BLK : (c + 1) * BLK]

    def angle(x, y):
        ax, ay = jnp.abs(x), jnp.abs(y)
        t = jnp.minimum(ax, ay) * pl.reciprocal(jnp.maximum(ax, ay), approx=True)
        square = t * t
        value = jnp.full_like(t, ATAN[-1] * 0.5 / pi)
        for coefficient in ATAN[-2::-1]:
            value = value * square + coefficient * 0.5 / pi
        value = value * t
        value = jnp.where(ay > ax, 0.25 - value, value)
        value = jnp.where(x < 0.0, 0.5 - value, value)
        return jnp.where(y < 0.0, -value, value)

    def angle_part(place, part, tile):
        at = pl.ds(part * 8, 8)
        total = angle(real[place][at], imag[place][at]) + turns[place][at]
        sums[at] = jnp.where(lanes == tile, jnp.sum(total, axis=1, keepdims=True), sums[at])

    def exact_block(block, tile, place, starts, beside):
        corner = [
            jnp.broadcast_to(panel_ref[block // 4, block % 4, c : c + 1, :], (8, BLK)) for c in range(9)
        ]
        ax, ay, az, bx, by, bz, cx, cy, cz = corner
        ux, uy, uz = bx - ax, by - ay, bz - az
        vx, vy, vz = cx - ax, cy - ay, cz - az
        wx, wy, wz = cx - bx, cy - by, cz - bz
        ux2, uy2, uz2 = ux + ux, uy + uy, uz + uz
        nx = uy2 * vz - uz2 * vy
        ny = uz2 * vx - ux2 * vz
        nz = ux2 * vy - uy2 * vx
        side_ab = ux * ux + uy * uy + uz * uz
        side_bc = wx * wx + wy * wy + wz * wz
        side_ca = vx * vx + vy * vy + vz * vz
        for part in range(TILE // 8):
            at = pl.ds(part * 8, 8)
            beside(part)
            qx, qy, qz = spread[place][0, at], spread[place][1, at], spread[place][2, at]

            def from_point(x, y, z):
                x, y, z = x - qx, y - qy, z - qz
                square = x * x + y * y + z * z
                return x, y, z, square * lax.rsqrt(square)

            px, py, pz, la = from_point(ax, ay, az)
            lb = from_point(bx, by, bz)[3]
            lc = from_point(cx, cy, cz)[3]
            y = px * nx + py * ny + pz * nz
            x = (la + lb) * (lb + lc) * (lc + la) - (side_ab * lc + side_bc * la + side_ca * lb)
            if starts:
                real[place][at], imag[place][at] = x, y
                turns[place][at] = jnp.zeros((8, BLK), jnp.float32)
            else:
                u, v = real[place][at], imag[place][at]
                below = y < 0.0
                r, i = u * x - v * y, u * y + v * x
                same = jnp.logical_not(jnp.logical_xor(v < 0.0, below))
                wrapped = jnp.logical_and(same, jnp.logical_xor(i < 0.0, below))
                turns[place][at] += jnp.where(wrapped, jnp.where(below, -1.0, 1.0), 0.0)
                real[place][at], imag[place][at] = r, i
        row = pl.ds(block, 1)
        field = dipole_field([centres[c, row, :] for c in range(6)], points_ref[tile, 0:3, :])
        minus[pl.ds(tile, 1), :] -= field

    first = widen(tiles[1])
    for part in range(TILE // 8):
        spread_part(1, part, first)

    def one_tile(index, place):
        tile = tiles[index]
        last, following = tiles[index - 1], tiles[index + 1]
        member, half = tile // 2, tile % 2
        across = widen(following)

        def beside(part):
            angle_part(1 - place, part, last)
            spread_part(1 - place, part, across)

        exact_block(live_ref[member, half, 0], tile, place, True, beside)

        def more(slot, carry):
            @pl.when(slot % 4 == 0)
            def _():
                u, v = real[place][...], imag[place][...]
                factor = 1.0 / (jnp.abs(u) + jnp.abs(v))
                real[place][...], imag[place][...] = u * factor, v * factor

            exact_block(live_ref[member, half, slot], tile, place, False, lambda part: None)
            return carry

        lax.fori_loop(1, live_ref[member, half, PANELS], more, 0)

    def two_tiles(step, carry):
        one_tile(2 * step + 1, 1)

        @pl.when(2 * step + 2 <= found)
        def _():
            one_tile(2 * step + 2, 0)

        return carry

    lax.fori_loop(0, (found + 1) // 2, two_tiles, 0)
    for place in range(2):

        @pl.when(found % 2 == place)
        def _():
            for part in range(TILE // 8):
                angle_part(place, part, tiles[found])

    rows = sums[...].T
    rows = rows[0 : 2 * MEMBERS, :] + minus[...]
    for member in range(MEMBERS):
        out_ref[member] = rows[2 * member : 2 * member + 2, :]


def near_call(live, panel, points, flipped):
    hbm = pl.BlockSpec(memory_space=pl.ANY)
    vmem = pl.BlockSpec(memory_space=pltpu.VMEM)
    f32 = jnp.float32
    return pl.pallas_call(
        near_kernel,
        out_shape=jax.ShapeDtypeStruct((MEMBERS, 2, TILE), f32),
        in_specs=[hbm, vmem, vmem, vmem],
        out_specs=vmem,
        scratch_shapes=[
            pltpu.SMEM((MEMBERS, 2, 32), jnp.int32),
            pltpu.VMEM((2 * MEMBERS, 8, TILE), f32),
            pltpu.VMEM((2, 32, 3 * BLK), jnp.bfloat16),
            pltpu.VMEM((6, HELD, TILE), f32),
            pltpu.VMEM((3, TILE, BLK), f32),
            pltpu.VMEM((3, TILE, BLK), f32),
        ]
        + [pltpu.VMEM((TILE, BLK), f32)] * 6
        + [
            pltpu.SMEM((2 * MEMBERS + 2,), jnp.int32),
            pltpu.VMEM((TILE, BLK), f32),
            pltpu.VMEM((2 * MEMBERS, TILE), f32),
            pltpu.SemaphoreType.DMA,
        ],
        compiler_params=pltpu.CompilerParams(vmem_limit_bytes=VMEM_LIMIT),
        name="near",
    )(live, panel, points, flipped)


def reduce_kernel(
    partial, panel, points, out_ref, far, centres, arrived, send_sem, recv_sem,
):
    me = lax.axis_index("owner")
    lane = lax.axis_index("qgrp")
    core = remainder(me, 2)
    group = me - core
    member = core * PAN_TURN + lane
    partners = [(to_core, to_lane) for to_lane in far_lanes(lane) for to_core in range(2)]
    partners.append((1 - core, lane))
    barrier = pltpu.get_barrier_semaphore()
    for to_core, to_lane in partners:
        pl.semaphore_signal(barrier, inc=1, device_id=(group + to_core, to_lane), device_id_type=MESH)
    spread_poles(panel, centres)

    def far_field(step, carry):
        for index in range(MEMBERS_STEP):
            one = step * MEMBERS_STEP + index
            for half in range(2):
                field = dipole_field([centres[c] for c in range(6)], points[one, 3 * half : 3 * half + 3, :])
                far[one, half : half + 1, :] = partial[one, half : half + 1, :] + jnp.sum(
                    field, axis=0, keepdims=True
                )
        return carry

    lax.fori_loop(0, MEMBERS // MEMBERS_STEP, far_field, 0)
    pl.semaphore_wait(barrier, MEMBERS - 1)

    for to_core, to_lane in partners:
        pltpu.make_async_remote_copy(
            src_ref=far.at[to_core * PAN_TURN + to_lane], dst_ref=arrived.at[member],
            send_sem=send_sem, recv_sem=recv_sem, device_id=(group + to_core, to_lane), device_id_type=MESH,
        ).start()
    arrived[member] = far[member]
    part = arrived.at[pl.ds(0, MEMBERS - 1)]
    pltpu.make_async_copy(part, part, recv_sem).wait()
    out_ref[...] = jnp.sum(arrived[...], axis=0)
    pltpu.make_async_copy(part, part, send_sem).wait()


def on_device(queries, winding_in, triangles, dipoles, plan, near_blocks, near_count):
    vmem = pl.BlockSpec(memory_space=pltpu.VMEM)
    hbm = pl.BlockSpec(memory_space=pl.ANY)
    f32 = jnp.float32
    panel, points, live, flipped = pl.pallas_call(
        gather_kernel,
        out_shape=(
            jax.ShapeDtypeStruct((PARTS, TURNS, ROWS, BLK), f32),
            jax.ShapeDtypeStruct((MEMBERS, 8, TILE), f32),
            jax.ShapeDtypeStruct((MEMBERS, 2, 32), jnp.int32),
            jax.ShapeDtypeStruct((MEMBERS, TILE, 32), jnp.bfloat16),
        ),
        in_specs=[hbm] * 6,
        out_specs=(hbm, hbm, hbm, vmem),
        scratch_shapes=[
            pltpu.VMEM((3, 2 * TILE), f32),
            pltpu.VMEM((9, BLOCKS * BLK), f32),
            pltpu.VMEM((6, BLOCKS), f32),
            pltpu.VMEM((2, NEAR, PANELS), jnp.int32),
            pltpu.VMEM((2, PANELS), jnp.int32),
            pltpu.SMEM((TURNS,), jnp.int32),
            pltpu.VMEM((16, 2, ROWS, BLK), f32),
            pltpu.VMEM((16, 2, ROWS, BLK), f32),
            pltpu.VMEM((2, TURNS, ROWS, BLK), f32),
            pltpu.VMEM((4, TURNS, ROWS, BLK), f32),
            pltpu.VMEM((TURNS, ROWS, BLK), f32),
            pltpu.VMEM((8, TILE), f32),
            pltpu.VMEM((MEMBERS, 8, TILE), f32),
            pltpu.VMEM((MEMBERS, 2, 32), jnp.int32),
            pltpu.SemaphoreType.DMA((6,)),
            pltpu.SemaphoreType.DMA((3,)),
        ]
        + [pltpu.SemaphoreType.DMA] * 9,
        compiler_params=pltpu.CompilerParams(collective_id=0, has_side_effects=True, vmem_limit_bytes=VMEM_LIMIT),
        name="gather",
    )(
        *[
            pltpu.with_memory_space_constraint(array, pltpu.HBM)
            for array in (plan, queries, triangles, dipoles, near_blocks.transpose(0, 2, 1), near_count)
        ],
    )
    partial = near_call(live, panel, points, flipped)
    total = pl.pallas_call(
        reduce_kernel,
        out_shape=jax.ShapeDtypeStruct((2, TILE), f32),
        in_specs=[vmem] * 3,
        out_specs=vmem,
        scratch_shapes=[
            pltpu.VMEM((MEMBERS, 2, TILE), f32),
            pltpu.VMEM((6, HELD, TILE), f32),
            pltpu.VMEM((MEMBERS, 2, TILE), f32),
            pltpu.SemaphoreType.DMA,
            pltpu.SemaphoreType.DMA,
        ],
        compiler_params=pltpu.CompilerParams(collective_id=1, has_side_effects=True, vmem_limit_bytes=VMEM_LIMIT),
        name="reduce",
    )(partial, panel, points)
    return winding_in + total.reshape(-1)


def solution(mesh):
    return jax.shard_map(
        on_device,
        mesh=mesh,
        in_specs=(
            P(None, ("owner", "qgrp")),
            P(("owner", "qgrp")),
            P(None, ("owner", "qgrp")),
            P(None, ("owner", "qgrp")),
            P(),
            P(("owner", "qgrp"), None, None),
            P(("owner", "qgrp"), None),
        ),
        out_specs=P(("owner", "qgrp")),
        check_vma=False,
    )
```

```python
import functools

import jax
import jax.numpy as jnp
from jax import lax
from jax.experimental import pallas as pl
from jax.experimental.pallas import tpu as pltpu
from jax.sharding import PartitionSpec as P

TILE = 128
BLK = 128
BLOCKS = 32
NEAR = 4
TURNS = 4
PAN_TURN = 4
PANELS = TURNS * PAN_TURN
OWNERS = 64
ROWS = 10
MEMBERS = 8
PARTS = 16
HELD = PARTS * TURNS
MEMBERS_STEP = 2
VMEM_LIMIT = 16 * 1024 * 1024

MESH = pl.DeviceIdType.MESH

pi = 3.141592653589793
four_pi = 4.0 * pi
soften = 0.1

ATAN = (
    0.9999994039535522,
    -0.3332701325416565,
    0.19887319207191467,
    -0.13512171804904938,
    0.08435401320457458,
    -0.03744291514158249,
    0.008006880059838295,
)


def quotient(number, by):
    return number // by if isinstance(number, int) else lax.div(number, jnp.int32(by))


def remainder(number, by):
    return number % by if isinstance(number, int) else lax.rem(number, jnp.int32(by))


def block_of(across, level, core):
    return core + (level // 2) * 2 + (level % 2) * 4 + across * 8


def far_lanes(lane):
    side = quotient(lane, 2)
    return 3 * (1 - side), 2 - side, side * (5 - lane) + (1 - side) * (1 - lane)


def gather_kernel(
    plan_ref, queries_ref, triangles_ref, dipoles_ref, blocks_ref, count_ref,
    panel_ref, points_ref, live_ref, flipped_ref,
    queries, triangles, dipoles, blocks, count, turn_owner,
    stage, gathered, picked, offered, chosen, message, messages, live,
    load_sems, out_sems, send_one, recv_one, send_pick, recv_pick, send_two, recv_two, recv_far, send_msg, recv_msg,
):
    me = lax.axis_index("owner")
    lane = lax.axis_index("qgrp")
    half = remainder(quotient(me, 8), 2)
    across = quotient(me, 16)
    core = remainder(me, 2)
    level = remainder(quotient(me, 2), 4)
    part = across * 4 + level
    member = core * PAN_TURN + lane
    squad = across * 2 + core
    group = me - core
    mirror = PAN_TURN - 1 - lane
    role = half * lane + (1 - half) * mirror
    first = half == 0
    barrier = pltpu.get_barrier_semaphore()

    loads = [
        pltpu.make_async_copy(source, target, load_sems.at[index])
        for index, (source, target) in enumerate(
            [
                (triangles_ref, triangles), (dipoles_ref, dipoles), (queries_ref, queries),
                (blocks_ref, blocks), (count_ref, count), (plan_ref, turn_owner),
            ]
        )
    ]
    def greet(owner, to_lane):
        pl.semaphore_signal(barrier, inc=1, device_id=(owner, to_lane), device_id_type=MESH)

    squads = [(dx, dc) for dx in (2, 1, 3, 0) for dc in (1, 0) if (dx, dc) != (0, 0)]
    lanes = far_lanes(lane)

    def comrade(dx, dc):
        to_across, to_core = remainder(across + dx, 4), remainder(core + dc, 2)
        return to_across * 2 + to_core, (to_across * 16 + half * 8 + level * 2 + to_core, lane)

    @pl.when(first)
    def _():
        for to_level in range(4):
            greet(across * 16 + 8 + to_level * 2 + core, mirror)
            greet(across * 16 + to_level * 2 + core, mirror)

    for dx in (2, 1, 3, 0):
        for dy in (2, 1, 3):
            greet(remainder(across + dx, 4) * 16 + half * 8 + remainder(level + dy, 4) * 2 + core, lane)
    for to_lane in lanes:
        for to_core in range(2):
            greet(group + to_core, to_lane)
    for dx, dc in squads:
        greet(*comrade(dx, dc)[1])

    for load in loads:
        load.start()

    loads[1].wait()
    flipped = jnp.concatenate(
        [jnp.concatenate([dipoles[...], jnp.zeros((2, BLOCKS), jnp.float32)], axis=0),
         jnp.zeros((8, BLK - BLOCKS), jnp.float32)], axis=1
    ).T
    loads[0].wait()
    for slot in range(BLOCKS):
        block = block_of(slot // 8, slot % 4, (slot // 4) % 2)
        stage[slot // 4, slot % 4, 0:9] = triangles[:, block * BLK : (block + 1) * BLK]
        stage[slot // 4, slot % 4, 9:10, 0:8] = flipped[block : block + 1, :]
    for load in loads[2:]:
        load.wait()
    message[0:3] = queries[:, 0:TILE]
    message[3:6] = queries[:, TILE : 2 * TILE]
    for tile in range(2):
        counted = count[tile : tile + 1, :]
        rows = [jnp.where(counted > slot, blocks[tile, slot : slot + 1, :], -1) for slot in range(NEAR)]
        rows.append(jnp.full((1, BLK - PANELS * NEAR), -1, jnp.int32))
        message[6 + tile : 7 + tile] = jnp.concatenate(rows, axis=1).astype(jnp.float32)

    def wait_bytes(part, sem):
        pltpu.make_async_copy(part, part, sem).wait()

    pl.semaphore_wait(barrier, 7 + 2 * (PAN_TURN - 1) + 12 + 4)

    for dx, dc in squads:
        other, where = comrade(dx, dc)
        pltpu.make_async_remote_copy(
            src_ref=stage.at[other], dst_ref=gathered.at[squad], send_sem=send_one, recv_sem=recv_one,
            device_id=where, device_id_type=MESH,
        ).start()

    def send_message(owner, to_lane):
        pltpu.make_async_remote_copy(
            src_ref=message, dst_ref=messages.at[member], send_sem=send_msg, recv_sem=recv_msg,
            device_id=(owner, to_lane), device_id_type=MESH,
        ).start()

    for to_lane in lanes:
        for to_core in range(2):
            send_message(group + to_core, to_lane)
    send_message(group + 1 - core, lane)
    gathered[squad] = stage[squad]
    messages[member] = message[...]
    wait_bytes(gathered.at[pl.ds(0, 7)], recv_one)
    for turn in range(TURNS):
        owner = turn_owner[turn]
        pieces = gathered[quotient(owner, 16) * 2 + remainder(owner, 2)]
        for to_level in range(4):
            picked[to_level, turn] = pieces[to_level]
    for dy in (2, 1, 3, 0):
        to_level = remainder(level + dy, 4)
        pltpu.make_async_remote_copy(
            src_ref=picked.at[to_level], dst_ref=offered.at[half * 4 + level], send_sem=send_pick, recv_sem=recv_pick,
            device_id=(across * 16 + to_level * 2 + core, mirror), device_id_type=MESH,
        ).start()

    @pl.when(first)
    def _():
        wait_bytes(offered, recv_pick)
        for turn in range(TURNS):
            owner = turn_owner[turn]
            squad_of = remainder(quotient(owner, 8), 2) * 4 + remainder(quotient(owner, 2), 4)
            chosen[turn] = offered[squad_of, turn]
        pltpu.make_async_remote_copy(
            src_ref=chosen, dst_ref=chosen, send_sem=send_two, recv_sem=recv_far,
            device_id=(me + 8, mirror), device_id_type=MESH,
        ).start()

    @pl.when(jnp.logical_not(first))
    def _():
        wait_bytes(chosen, recv_far)

    for dx, dy in [(dx, dy) for dx in (2, 1, 3, 0) for dy in (2, 1, 3, 0) if (dx, dy) != (0, 0)]:
        to_level = remainder(level + dy, 4)
        pltpu.make_async_remote_copy(
            src_ref=chosen, dst_ref=panel_ref.at[part], send_sem=send_two, recv_sem=recv_two,
            device_id=(remainder(across + dx, 4) * 16 + half * 8 + to_level * 2 + core, lane), device_id_type=MESH,
        ).start()
    outs = [
        pltpu.make_async_copy(source, target, out_sems.at[index])
        for index, (source, target) in enumerate(
            [(chosen, panel_ref.at[part]), (messages, points_ref), (live, live_ref)]
        )
    ]
    outs[0].start()
    wait_bytes(messages.at[pl.ds(0, MEMBERS - 1)], recv_msg)
    outs[1].start()

    shape = (MEMBERS, BLK)
    column = lax.broadcasted_iota(jnp.int32, shape, 1)
    before = (
        lax.broadcasted_iota(jnp.int32, (BLK, BLK), 0) < lax.broadcasted_iota(jnp.int32, (BLK, BLK), 1)
    ).astype(jnp.float32)
    for tile in range(2):
        listed = messages[:, 6 + tile, :].astype(jnp.int32)
        held = listed % 2 == core
        held = jnp.logical_and(held, column % PAN_TURN == role)
        held = jnp.logical_and(held, jnp.logical_and(listed >= 0, column < PANELS * NEAR))
        where = (listed // 8) * 4 + ((listed // 2) % 2) * 2 + (listed // 4) % 2
        value = where * TURNS + (column % PANELS) // PAN_TURN
        value = value.astype(jnp.float32)
        flags = jnp.where(held, 1.0, 0.0)
        rank = lax.dot_general(flags, before, (((1,), (0,)), ((), ())), preferred_element_type=jnp.float32)
        rank = jnp.where(held, rank, -1.0)
        packed = jnp.where(column == PANELS, jnp.sum(flags, axis=1, keepdims=True), 0.0)
        for index in range(PANELS):
            one = jnp.sum(jnp.where(jnp.abs(rank - index) < 0.5, value, 0.0), axis=1, keepdims=True)
            packed = jnp.where(column == index, one, packed)
        live[:, tile, :] = packed[:, 0:32].astype(jnp.int32)
    outs[2].start()

    def flip(to, carry):
        rest = messages[to]
        parts = []
        for _ in range(3):
            parts.append(rest.astype(jnp.bfloat16).astype(jnp.float32))
            rest = rest - parts[-1]
        parts.append(jnp.zeros_like(rest))
        flipped_ref[to] = jnp.concatenate(parts, axis=0).T.astype(jnp.bfloat16)
        return carry

    lax.fori_loop(0, MEMBERS, flip, 0)

    wait_bytes(stage.at[pl.ds(0, 7)], send_one)
    wait_bytes(picked, send_pick)
    wait_bytes(messages.at[pl.ds(0, MEMBERS - 1)], send_msg)

    @pl.when(first)
    def _():
        wait_bytes(panel_ref, send_two)

    @pl.when(jnp.logical_not(first))
    def _():
        wait_bytes(panel_ref.at[pl.ds(0, PARTS - 1)], send_two)

    for out in outs:
        out.wait()
    wait_bytes(panel_ref.at[pl.ds(0, PARTS - 1)], recv_two)


def dipole_field(centre, points):
    offset = [centre[c] - jnp.broadcast_to(points[c : c + 1, :], centre[c].shape) for c in range(3)]
    square = offset[0] * offset[0] + offset[1] * offset[1] + offset[2] * offset[2] + soften
    inverse = lax.rsqrt(square)
    return (centre[3] * offset[0] + centre[4] * offset[1] + centre[5] * offset[2]) * (
        inverse * inverse * inverse
    )


def spread_poles(panel, centres):
    rows = jnp.concatenate([panel[slot // 4, slot % 4, 9:10, :] for slot in range(HELD)], axis=0)
    for component in range(6):
        value = jnp.broadcast_to(rows[:, component : component + 1], (HELD, TILE))
        if component >= 3:
            value = value * (1.0 / four_pi)
        centres[component] = value


def near_kernel(
    live_hbm, panel_ref, given, flipped, out_ref,
    live_ref, points_ref, picker, centres,
    spread_0, spread_1, real_0, real_1, imag_0, imag_1, turns_0, turns_1, tiles, sums, minus, sem
):
    spread, real, imag, turns = (spread_0, spread_1), (real_0, real_1), (imag_0, imag_1), (turns_0, turns_1)
    load = pltpu.make_async_copy(live_hbm, live_ref, sem)
    load.start()
    minus[...] = jnp.zeros_like(minus)
    sums[...] = jnp.zeros_like(sums)
    real_0[...] = jnp.ones_like(real_0)
    imag_0[...] = jnp.zeros_like(imag_0)
    turns_0[...] = jnp.zeros_like(turns_0)
    spread_poles(panel_ref, centres)
    for member in range(MEMBERS):
        for half in range(2):
            points_ref[2 * member + half, 0:3] = given[member, 3 * half : 3 * half + 3]
    load.wait()
    tiles[0] = 2 * MEMBERS
    found = jnp.int32(0)
    for tile in range(2 * MEMBERS):
        tiles[found + 1] = tile
        found = found + jnp.where(live_ref[tile // 2, tile % 2, PANELS] > 0, 1, 0)
    tiles[found + 1] = 0
    lanes = lax.broadcasted_iota(jnp.int32, (8, BLK), 1)

    shape = (32, 3 * BLK)
    entry = lax.broadcasted_iota(jnp.int32, shape, 0)
    component = lax.broadcasted_iota(jnp.int32, shape, 1) // BLK
    for half in range(2):
        wanted = jnp.logical_and(entry % 8 == 3 * half + component, entry < 24)
        picker[half] = jnp.where(wanted, 1.0, 0.0).astype(jnp.bfloat16)

    def widen(tile):
        return lax.dot_general(
            flipped[tile // 2], picker[tile % 2], (((1,), (0,)), ((), ())), preferred_element_type=jnp.float32
        )

    def spread_part(place, part, wide):
        at = pl.ds(part * 8, 8)
        for c in range(3):
            spread[place][c, at] = wide[part * 8 : part * 8 + 8, c * BLK : (c + 1) * BLK]

    def angle(x, y):
        ax, ay = jnp.abs(x), jnp.abs(y)
        t = jnp.minimum(ax, ay) * pl.reciprocal(jnp.maximum(ax, ay), approx=True)
        square = t * t
        value = jnp.full_like(t, ATAN[-1] * 0.5 / pi)
        for coefficient in ATAN[-2::-1]:
            value = value * square + coefficient * 0.5 / pi
        value = value * t
        value = jnp.where(ay > ax, 0.25 - value, value)
        value = jnp.where(x < 0.0, 0.5 - value, value)
        return jnp.where(y < 0.0, -value, value)

    def angle_part(place, part, tile):
        at = pl.ds(part * 8, 8)
        total = angle(real[place][at], imag[place][at]) + turns[place][at]
        sums[at] = jnp.where(lanes == tile, jnp.sum(total, axis=1, keepdims=True), sums[at])

    def exact_block(block, tile, place, starts, beside):
        corner = [
            jnp.broadcast_to(panel_ref[block // 4, block % 4, c : c + 1, :], (8, BLK)) for c in range(9)
        ]
        ax, ay, az, bx, by, bz, cx, cy, cz = corner
        ux, uy, uz = bx - ax, by - ay, bz - az
        vx, vy, vz = cx - ax, cy - ay, cz - az
        wx, wy, wz = cx - bx, cy - by, cz - bz
        ux2, uy2, uz2 = ux + ux, uy + uy, uz + uz
        nx = uy2 * vz - uz2 * vy
        ny = uz2 * vx - ux2 * vz
        nz = ux2 * vy - uy2 * vx
        side_ab = ux * ux + uy * uy + uz * uz
        side_bc = wx * wx + wy * wy + wz * wz
        side_ca = vx * vx + vy * vy + vz * vz
        for part in range(TILE // 8):
            at = pl.ds(part * 8, 8)
            beside(part)
            qx, qy, qz = spread[place][0, at], spread[place][1, at], spread[place][2, at]

            def from_point(x, y, z):
                x, y, z = x - qx, y - qy, z - qz
                square = x * x + y * y + z * z
                return x, y, z, square * lax.rsqrt(square)

            px, py, pz, la = from_point(ax, ay, az)
            lb = from_point(bx, by, bz)[3]
            lc = from_point(cx, cy, cz)[3]
            y = px * nx + py * ny + pz * nz
            x = (la + lb) * (lb + lc) * (lc + la) - (side_ab * lc + side_bc * la + side_ca * lb)
            if starts:
                real[place][at], imag[place][at] = x, y
                turns[place][at] = jnp.zeros((8, BLK), jnp.float32)
            else:
                u, v = real[place][at], imag[place][at]
                below = y < 0.0
                r, i = u * x - v * y, u * y + v * x
                same = jnp.logical_not(jnp.logical_xor(v < 0.0, below))
                wrapped = jnp.logical_and(same, jnp.logical_xor(i < 0.0, below))
                turns[place][at] += jnp.where(wrapped, jnp.where(below, -1.0, 1.0), 0.0)
                real[place][at], imag[place][at] = r, i
        row = pl.ds(block, 1)
        field = dipole_field([centres[c, row, :] for c in range(6)], points_ref[tile, 0:3, :])
        minus[pl.ds(tile, 1), :] -= field

    first = widen(tiles[1])
    for part in range(TILE // 8):
        spread_part(1, part, first)

    def one_tile(index, place):
        tile = tiles[index]
        last, following = tiles[index - 1], tiles[index + 1]
        member, half = tile // 2, tile % 2
        across = widen(following)

        def beside(part):
            angle_part(1 - place, part, last)
            spread_part(1 - place, part, across)

        exact_block(live_ref[member, half, 0], tile, place, True, beside)

        def more(slot, carry):
            @pl.when(slot % 4 == 0)
            def _():
                u, v = real[place][...], imag[place][...]
                factor = 1.0 / (jnp.abs(u) + jnp.abs(v))
                real[place][...], imag[place][...] = u * factor, v * factor

            exact_block(live_ref[member, half, slot], tile, place, False, lambda part: None)
            return carry

        lax.fori_loop(1, live_ref[member, half, PANELS], more, 0)

    def two_tiles(step, carry):
        one_tile(2 * step + 1, 1)

        @pl.when(2 * step + 2 <= found)
        def _():
            one_tile(2 * step + 2, 0)

        return carry

    lax.fori_loop(0, (found + 1) // 2, two_tiles, 0)
    for place in range(2):

        @pl.when(found % 2 == place)
        def _():
            for part in range(TILE // 8):
                angle_part(place, part, tiles[found])

    rows = sums[...].T
    rows = rows[0 : 2 * MEMBERS, :] + minus[...]
    for member in range(MEMBERS):
        out_ref[member] = rows[2 * member : 2 * member + 2, :]


def near_call(live, panel, points, flipped):
    hbm = pl.BlockSpec(memory_space=pl.ANY)
    vmem = pl.BlockSpec(memory_space=pltpu.VMEM)
    f32 = jnp.float32
    return pl.pallas_call(
        near_kernel,
        out_shape=jax.ShapeDtypeStruct((MEMBERS, 2, TILE), f32),
        in_specs=[hbm, vmem, vmem, vmem],
        out_specs=vmem,
        scratch_shapes=[
            pltpu.SMEM((MEMBERS, 2, 32), jnp.int32),
            pltpu.VMEM((2 * MEMBERS, 8, TILE), f32),
            pltpu.VMEM((2, 32, 3 * BLK), jnp.bfloat16),
            pltpu.VMEM((6, HELD, TILE), f32),
            pltpu.VMEM((3, TILE, BLK), f32),
            pltpu.VMEM((3, TILE, BLK), f32),
        ]
        + [pltpu.VMEM((TILE, BLK), f32)] * 6
        + [
            pltpu.SMEM((2 * MEMBERS + 2,), jnp.int32),
            pltpu.VMEM((TILE, BLK), f32),
            pltpu.VMEM((2 * MEMBERS, TILE), f32),
            pltpu.SemaphoreType.DMA,
        ],
        compiler_params=pltpu.CompilerParams(vmem_limit_bytes=VMEM_LIMIT),
        name="near",
    )(live, panel, points, flipped)


def reduce_kernel(
    partial, panel, points, out_ref, far, centres, arrived, send_sem, recv_sem,
):
    me = lax.axis_index("owner")
    lane = lax.axis_index("qgrp")
    core = remainder(me, 2)
    group = me - core
    member = core * PAN_TURN + lane
    partners = [(to_core, to_lane) for to_lane in far_lanes(lane) for to_core in range(2)]
    partners.append((1 - core, lane))
    barrier = pltpu.get_barrier_semaphore()
    for to_core, to_lane in partners:
        pl.semaphore_signal(barrier, inc=1, device_id=(group + to_core, to_lane), device_id_type=MESH)
    spread_poles(panel, centres)

    def far_field(step, carry):
        for index in range(MEMBERS_STEP):
            one = step * MEMBERS_STEP + index
            for half in range(2):
                field = dipole_field([centres[c] for c in range(6)], points[one, 3 * half : 3 * half + 3, :])
                far[one, half : half + 1, :] = partial[one, half : half + 1, :] + jnp.sum(
                    field, axis=0, keepdims=True
                )
        return carry

    lax.fori_loop(0, MEMBERS // MEMBERS_STEP, far_field, 0)
    pl.semaphore_wait(barrier, MEMBERS - 1)

    for to_core, to_lane in partners:
        pltpu.make_async_remote_copy(
            src_ref=far.at[to_core * PAN_TURN + to_lane], dst_ref=arrived.at[member],
            send_sem=send_sem, recv_sem=recv_sem, device_id=(group + to_core, to_lane), device_id_type=MESH,
        ).start()
    arrived[member] = far[member]
    part = arrived.at[pl.ds(0, MEMBERS - 1)]
    pltpu.make_async_copy(part, part, recv_sem).wait()
    out_ref[...] = jnp.sum(arrived[...], axis=0)
    pltpu.make_async_copy(part, part, send_sem).wait()


def on_device(queries, winding_in, triangles, dipoles, plan, near_blocks, near_count):
    vmem = pl.BlockSpec(memory_space=pltpu.VMEM)
    hbm = pl.BlockSpec(memory_space=pl.ANY)
    f32 = jnp.float32
    panel, points, live, flipped = pl.pallas_call(
        gather_kernel,
        out_shape=(
            jax.ShapeDtypeStruct((PARTS, TURNS, ROWS, BLK), f32),
            jax.ShapeDtypeStruct((MEMBERS, 8, TILE), f32),
            jax.ShapeDtypeStruct((MEMBERS, 2, 32), jnp.int32),
            jax.ShapeDtypeStruct((MEMBERS, TILE, 32), jnp.bfloat16),
        ),
        in_specs=[hbm] * 6,
        out_specs=(hbm, hbm, hbm, vmem),
        scratch_shapes=[
            pltpu.VMEM((3, 2 * TILE), f32),
            pltpu.VMEM((9, BLOCKS * BLK), f32),
            pltpu.VMEM((6, BLOCKS), f32),
            pltpu.VMEM((2, NEAR, PANELS), jnp.int32),
            pltpu.VMEM((2, PANELS), jnp.int32),
            pltpu.SMEM((TURNS,), jnp.int32),
            pltpu.VMEM((8, 4, ROWS, BLK), f32),
            pltpu.VMEM((8, 4, ROWS, BLK), f32),
            pltpu.VMEM((4, TURNS, ROWS, BLK), f32),
            pltpu.VMEM((8, TURNS, ROWS, BLK), f32),
            pltpu.VMEM((TURNS, ROWS, BLK), f32),
            pltpu.VMEM((8, TILE), f32),
            pltpu.VMEM((MEMBERS, 8, TILE), f32),
            pltpu.VMEM((MEMBERS, 2, 32), jnp.int32),
            pltpu.SemaphoreType.DMA((6,)),
            pltpu.SemaphoreType.DMA((3,)),
        ]
        + [pltpu.SemaphoreType.DMA] * 9,
        compiler_params=pltpu.CompilerParams(collective_id=0, has_side_effects=True, vmem_limit_bytes=VMEM_LIMIT),
        name="gather",
    )(
        *[
            pltpu.with_memory_space_constraint(array, pltpu.HBM)
            for array in (plan, queries, triangles, dipoles, near_blocks.transpose(0, 2, 1), near_count)
        ],
    )
    partial = near_call(live, panel, points, flipped)
    total = pl.pallas_call(
        reduce_kernel,
        out_shape=jax.ShapeDtypeStruct((2, TILE), f32),
        in_specs=[vmem] * 3,
        out_specs=vmem,
        scratch_shapes=[
            pltpu.VMEM((MEMBERS, 2, TILE), f32),
            pltpu.VMEM((6, HELD, TILE), f32),
            pltpu.VMEM((MEMBERS, 2, TILE), f32),
            pltpu.SemaphoreType.DMA,
            pltpu.SemaphoreType.DMA,
        ],
        compiler_params=pltpu.CompilerParams(collective_id=1, has_side_effects=True, vmem_limit_bytes=VMEM_LIMIT),
        name="reduce",
    )(partial, panel, points)
    return winding_in + total.reshape(-1)


def solution(mesh):
    return jax.shard_map(
        on_device,
        mesh=mesh,
        in_specs=(
            P(None, ("owner", "qgrp")),
            P(("owner", "qgrp")),
            P(None, ("owner", "qgrp")),
            P(None, ("owner", "qgrp")),
            P(),
            P(("owner", "qgrp"), None, None),
            P(("owner", "qgrp"), None),
        ),
        out_specs=P(("owner", "qgrp")),
        check_vma=False,
    )
```
